128 devices in a mesh: ctx: 8 (over y, z_hi), fsdp: 16 (over x, z_lo, core).
Axes of the slice: x: 4, y: 4, z: 4 (z_hi: 2, z_lo: 2; z = z_hi * 2 + z_lo), core: 2. Of those that a mesh axis runs over, the one named last changes fastest.
Arguments:
- tokens: bfloat16 [16384, 1280], P(('ctx', 'fsdp')), may hold values from -6 to 6
- norm_gain: bfloat16 [1280], P(('ctx', 'fsdp')), may hold values from 0.099609375 to 1.8984375
- w_query: bfloat16 [1280, 1280], P(('ctx', 'fsdp')), may hold values from -0.25 to 0.25
- w_key: bfloat16 [1280, 320], P(('ctx', 'fsdp')), may hold values from -0.15625 to 0.15625
- w_value: bfloat16 [1280, 320], P(('ctx', 'fsdp')), may hold values from -0.15625 to 0.15625
- w_out: bfloat16 [1280, 1280], P(('ctx', 'fsdp')), may hold values from -0.625 to 0.625
- mlp_gain: bfloat16 [1280], P(('ctx', 'fsdp')), may hold values from 0.099609375 to 1.8984375
- w_gate: bfloat16 [1280, 3584], P(('ctx', 'fsdp')), may hold values from -0.15625 to 0.15625
- w_up: bfloat16 [1280, 3584], P(('ctx', 'fsdp')), may hold values from -0.15625 to 0.15625
- w_down: bfloat16 [3584, 1280], P(('ctx', 'fsdp')), may hold values from -0.09375 to 0.09375
- block_pair: int32 [16, 8], P('fsdp'), may hold values from 0 to 7, each once within a row
- seq_len: int32 [16], P('fsdp'), may hold values from 640 to 1024, as said below
- seq_start: int32 [16], P('fsdp'), may hold values from 0 to 63, as said below
- out_grad: bfloat16 [16384, 1280], P(('ctx', 'fsdp')), may hold values from -6 to 6
Outputs:
- activations: bfloat16 [16384, 1280], P(('ctx', 'fsdp'))
- input_grad: bfloat16 [16384, 1280], P(('ctx', 'fsdp'))
- grad_norm_gain: float32 [1280], P(('ctx', 'fsdp'))
- grad_query: float32 [1280, 1280], P(('ctx', 'fsdp'))
- grad_key: float32 [1280, 320], P(('ctx', 'fsdp'))
- grad_value: float32 [1280, 320], P(('ctx', 'fsdp'))
- grad_out: float32 [1280, 1280], P(('ctx', 'fsdp'))
- grad_mlp_gain: float32 [1280], P(('ctx', 'fsdp'))
- grad_gate: float32 [1280, 3584], P(('ctx', 'fsdp'))
- grad_up: float32 [1280, 3584], P(('ctx', 'fsdp'))
- grad_down: float32 [3584, 1280], P(('ctx', 'fsdp'))
- seq_rms: float32 [16, 3], P('fsdp')
The draws below stay inside these ranges and needn't reach their ends.
Inputs may be any that keep to these rules, and one draw needn't show every extreme that they name: The one sequence of group g fills slots seq_start[g] to seq_start[g] + seq_len[g] - 1 of the group's 1024 slots; some group fills all of them. seq_start[g] + seq_len[g] <= 1024.
All inputs are finite; a program needn't handle non-finite values.
Results may differ from the reference program's by a relative error of at most 0.022.
Values may be sent and summed in bfloat16 or wider, within the bound.
No kernel may reach another device: no remote copies, remote signals or barrier semaphores. Data moves between devices by JAX's collectives and lax.ppermute only.
A program may use at most 128 MiB of HBM per device.

```python
import math
import jax
import jax.numpy as jnp
from jax import lax

D = 1280
QUERY_HEADS = 20
KEY_VALUE_HEADS = 5
HEAD_WIDTH = 64
FF = 3584
BLK = 64
TOK_GROUP = 1024
TOKENS = 16384
QW = 1280
KW = 320
LEN_LO = 640
START_HI = 63
N_CTX = 8
N_FSDP = 16


def sequence_spans(key):
    key_lengths, key_starts, key_order = jax.random.split(key, 3)
    lengths = jax.random.randint(key_lengths, (N_FSDP,), LEN_LO, TOK_GROUP + 1)
    headroom = jnp.minimum(TOK_GROUP - lengths, BLK - 1)
    starts = jax.random.randint(key_starts, (N_FSDP,), 0, headroom + 1)
    shuffled = jax.random.permutation(key_order, N_FSDP)
    longest = shuffled[0]
    shortest = shuffled[1]
    lengths = lengths.at[longest].set(TOK_GROUP).at[shortest].set(LEN_LO)
    starts = starts.at[longest].set(0).at[shortest].set(START_HI)
    return (lengths.astype(jnp.int32), starts.astype(jnp.int32))


def draw_seq_len(key, part):
    return sequence_spans(key)[0]


def draw_seq_start(key, part):
    return sequence_spans(key)[1]


def block_scale(own_key, dims, cuts, least, top_value):
    def one(position, parts):
        draws = jax.random.uniform(jax.random.fold_in(jax.random.fold_in(own_key, 6), position), (parts,), jnp.float32, least / len(cuts), top_value / len(cuts))
        return jnp.repeat(jnp.exp(draws), dims[position] // parts).reshape((-1,) + (1,) * (len(dims) - position - 1))

    loudness = one(*cuts[0])
    for cut in cuts[1:]:
        loudness = loudness * one(*cut)
    return loudness


def normal_values(own_key, shape, width, most, cuts=(), held_as=jnp.bfloat16):
    array = width * jax.random.normal(own_key, shape, jnp.float32)
    if cuts:
        array = array * block_scale(own_key, shape, cuts, -0.22, 0.18)
    return jnp.clip(array, -most, most).astype(held_as)


def setup_inputs(seed: int = 0) -> dict:
    splits = jax.random.split(jax.random.key(seed), 15)
    tokens = normal_values(splits[0], (TOKENS, D), 1.0, 6.0, ((0, 128),))
    norm_gain = jnp.clip(1.0 + 0.18 * jax.random.normal(splits[1], (D,), jnp.float32), 0.099609375, 1.8984375).astype(jnp.bfloat16)
    w_query = normal_values(splits[2], (D, QW), (D // 2) ** -0.5, 0.25, ((0, 128),))
    w_key = normal_values(splits[3], (D, KW), D ** -0.5, 0.15625, ((0, 128),))
    w_value = normal_values(splits[4], (D, KW), D ** -0.5, 0.15625, ((0, 128),))
    w_out = normal_values(splits[5], (QW, D), (QW // 16) ** -0.5, 0.625, ((0, 128),))
    mlp_gain = jnp.clip(1.0 + 0.18 * jax.random.normal(splits[6], (D,), jnp.float32), 0.099609375, 1.8984375).astype(jnp.bfloat16)
    w_gate = normal_values(splits[7], (D, FF), D ** -0.5, 0.15625, ((0, 128),))
    w_up = normal_values(splits[8], (D, FF), D ** -0.5, 0.15625, ((0, 128),))
    w_down = normal_values(splits[9], (FF, D), FF ** -0.5, 0.09375, ((0, 128),))
    block_pair = jax.vmap(lambda own: jax.random.permutation(own, N_CTX))(jax.random.split(splits[10], N_FSDP)).reshape((N_FSDP, N_CTX)).astype(jnp.int32)
    seq_len = draw_seq_len(jax.random.fold_in(splits[14], 71), 0)
    seq_start = draw_seq_start(jax.random.fold_in(splits[14], 71), 0)
    out_grad = normal_values(splits[13], (TOKENS, D), 1.0, 6.0, ((0, 128),))
    return dict(tokens=tokens, norm_gain=norm_gain, w_query=w_query, w_key=w_key, w_value=w_value, w_out=w_out, mlp_gain=mlp_gain, w_gate=w_gate, w_up=w_up, w_down=w_down, block_pair=block_pair, seq_len=seq_len, seq_start=seq_start, out_grad=out_grad)


EPSILON = 1e-05
ROPE_BASE = 10000.0
MASKED_SCORE = -1e+30

@jax.custom_vjp
def reduced_precision(v):
    return lax.optimization_barrier(v.astype(jnp.bfloat16)).astype(jnp.float32)

@jax.custom_vjp
def reduced_precision_backward(v):
    return v

def low_keep(v):
    return (reduced_precision(v), None)

def low_pass(kept, grad):
    return (grad,)

def back_keep(v):
    return (v, None)

def back_low(kept, grad):
    return (reduced_precision(grad),)
reduced_precision.defvjp(low_keep, low_pass)
reduced_precision_backward.defvjp(back_keep, back_low)

def precise_product(left, right):
    return jnp.dot(left, right, precision=lax.Precision.HIGHEST, preferred_element_type=jnp.float32)

def norm_apply(values, gain_values):
    factor = lax.rsqrt(lax.optimization_barrier(jnp.mean(values * values, axis=-1, keepdims=True)) + EPSILON)
    return values * factor * gain_values

def rope_tables(angles_at, head_size):
    half_size = head_size // 2
    powers = jnp.arange(half_size, dtype=jnp.float32) * (2.0 / head_size)
    speeds = jnp.power(ROPE_BASE, -powers)
    angles = angles_at[:, None] * speeds[None, :]
    return (jnp.cos(angles)[:, None, :], jnp.sin(angles)[:, None, :])

def apply_rotary(values, cosine_values, sine_values):
    half_size = values.shape[-1] // 2
    leading = values[..., :half_size]
    trailing = values[..., half_size:]
    return jnp.concatenate([leading * cosine_values - trailing * sine_values, trailing * cosine_values + leading * sine_values], axis=-1)

def group_places(pair_row, devices_ctx, block_size):
    slots = jnp.arange(devices_ctx * 2 * block_size, dtype=jnp.int32)
    owners = slots // (2 * block_size)
    inside = slots % (2 * block_size)
    columns = jnp.arange(devices_ctx, dtype=jnp.int32)
    paired = lax.optimization_barrier(jnp.sum(jnp.where(owners[:, None] == columns[None, :], pair_row[None, :], 0), axis=1)).astype(jnp.int32)
    blocks = jnp.where(inside < block_size, paired, 2 * devices_ctx - 1 - paired)
    return (blocks * block_size + inside % block_size).astype(jnp.int32)

def attend(query_rotated, key_rotated, value_reduced, allowed):
    row_total = query_rotated.shape[0]
    rows_per_block = math.gcd(row_total, 512)
    query_block_list = query_rotated.reshape(row_total // rows_per_block, rows_per_block, KEY_VALUE_HEADS, QUERY_HEADS // KEY_VALUE_HEADS, HEAD_WIDTH)
    mask_blocks = allowed.reshape(row_total // rows_per_block, rows_per_block, row_total)

    def block_attend(pieces):
        query_block, mask_block = pieces
        scores = reduced_precision_backward(HEAD_WIDTH ** (-0.5) * jnp.einsum('qhgd,khd->hgqk', query_block, key_rotated, precision=lax.Precision.HIGHEST))
        scores = jnp.where(mask_block[None, None], scores, MASKED_SCORE)
        row_top = lax.optimization_barrier(jnp.max(scores, axis=-1, keepdims=True))
        expons = jnp.exp(scores - row_top)
        chances = reduced_precision(expons / lax.optimization_barrier(jnp.sum(expons, axis=-1, keepdims=True)))
        return jnp.einsum('hgqk,khd->qhgd', chances, value_reduced, precision=lax.Precision.HIGHEST)
    outcome = lax.map(jax.checkpoint(block_attend), (query_block_list, mask_blocks))
    return outcome.reshape(row_total, QUERY_HEADS * HEAD_WIDTH)

def layer_apply(inputs, gain_one, query_w, key_w, value_weight, out_w, gain_two, gate_w, up_w, down_w, cosine_values, sine_values, allowed):
    row_total = inputs.shape[0]
    normalized_rows = reduced_precision(norm_apply(inputs, gain_one))
    query_pre = reduced_precision_backward(precise_product(normalized_rows, query_w))
    key_unrotated = reduced_precision_backward(precise_product(normalized_rows, key_w))
    value_reduced = reduced_precision(reduced_precision_backward(precise_product(normalized_rows, value_weight))).reshape(row_total, KEY_VALUE_HEADS, HEAD_WIDTH)
    query_rotated = reduced_precision(apply_rotary(query_pre.reshape(row_total, QUERY_HEADS, HEAD_WIDTH), cosine_values, sine_values))
    key_rotated = reduced_precision(apply_rotary(key_unrotated.reshape(row_total, KEY_VALUE_HEADS, HEAD_WIDTH), cosine_values, sine_values))
    attended = reduced_precision(reduced_precision_backward(attend(query_rotated, key_rotated, value_reduced, allowed)))
    branch = reduced_precision_backward(precise_product(attended, out_w))
    middle = inputs + branch
    normed_two = reduced_precision(norm_apply(middle, gain_two))
    gate_value = reduced_precision_backward(precise_product(normed_two, gate_w))
    up_value = reduced_precision_backward(precise_product(normed_two, up_w))
    hidden = reduced_precision(jax.nn.silu(gate_value) * up_value)
    feed_out = reduced_precision_backward(precise_product(hidden, down_w))
    return (middle + feed_out, (branch, feed_out))

def reference(tokens, norm_gain, w_query, w_key, w_value, w_out, mlp_gain, w_gate, w_up, w_down, block_pair, seq_len, seq_start, out_grad):
    dev_rows = 2 * BLK
    group_rows = dev_rows * N_CTX

    def group_order(values):
        return values.astype(jnp.float32).reshape(N_CTX, N_FSDP, dev_rows, D).transpose(1, 0, 2, 3).reshape(N_FSDP, group_rows, D)

    def device_order(values):
        return values.reshape(N_FSDP, N_CTX, dev_rows, D).transpose(1, 0, 2, 3).reshape(N_CTX * N_FSDP * dev_rows, D)
    params = tuple((item.astype(jnp.float32) for item in (norm_gain, w_query, w_key, w_value, w_out, mlp_gain, w_gate, w_up, w_down)))

    def group_step(carry, pieces):
        inputs, cot_rows, pair_row, seq_length, first_slot = pieces
        places = group_places(pair_row, N_CTX, BLK)
        valid_rows = (places >= first_slot) & (places < first_slot + seq_length)
        allowed = valid_rows[:, None] & valid_rows[None, :] & (places[None, :] <= places[:, None]) | (places[None, :] == places[:, None])
        cosine_values, sine_values = rope_tables((places - first_slot).astype(jnp.float32), HEAD_WIDTH)

        def forward(inputs_in, *weights_in):
            return layer_apply(inputs_in, *weights_in, cosine_values, sine_values, allowed)
        final_out, back_fn, extras = jax.vjp(forward, inputs, *params, has_aux=True)
        branch, feed_out = extras
        row_weight = valid_rows.astype(jnp.float32)[:, None]
        grads = back_fn(cot_rows * row_weight)
        sums = jnp.stack([jnp.sum(row_weight * branch * branch), jnp.sum(row_weight * feed_out * feed_out), jnp.sum(row_weight * final_out * final_out)])
        stats = jnp.sqrt(sums / (seq_length.astype(jnp.float32) * D))
        carry = tuple((total + grad_term for total, grad_term in zip(carry, grads[1:])))
        return (carry, (final_out, grads[0], stats))
    init = tuple((jnp.zeros(item.shape, jnp.float32) for item in params))
    totals, outputs = lax.scan(group_step, init, (group_order(tokens), group_order(out_grad), block_pair, seq_len, seq_start))
    finals, input_grads, stats = outputs
    return (device_order(finals).astype(jnp.bfloat16), device_order(input_grads).astype(jnp.bfloat16), totals[0], totals[1], totals[2], totals[3], totals[4], totals[5], totals[6], totals[7], totals[8], stats)
```

```python
import jax
import jax.numpy as jnp
from jax import lax
from jax.sharding import Mesh, PartitionSpec as P

QUERY_HEADS = 20
KEY_VALUE_HEADS = 5
HEAD_WIDTH = 64
QUERY_WIDTH = QUERY_HEADS * HEAD_WIDTH
KEY_WIDTH = KEY_VALUE_HEADS * HEAD_WIDTH
GAIN_COLS = 128
PAD_UNITS = 32

EPSILON = 1e-05
ROPE_BASE = 10000.0
MASKED_SCORE = -1e30

AXES = ("y", "zh", "x", "zl", "core")
SIZES = (4, 2, 4, 2, 2)
ROW_AXES = ("y", "core")
SLICE_AXES = ("x", "zh", "zl")
F32 = jnp.float32
BF16 = jnp.bfloat16


def device_number(x, y, z, core):
    return (((y * 2 + z // 2) * 4 + x) * 2 + z % 2) * 2 + core


def pairs_of(move):
    pairs = []
    for y in range(4):
        for z in range(4):
            for x in range(4):
                for core in range(2):
                    tx, ty, tz, tc = move(x, y, z, core)
                    pairs.append(
                        (device_number(x, y, z, core), device_number(tx % 4, ty % 4, tz % 4, tc))
                    )
    return pairs


def send(values, move):
    return lax.ppermute(values, AXES, pairs_of(move))


def swap_cores(values):
    return send(values, lambda x, y, z, core: (x, y, z, 1 - core))


def swap_half_core(values):
    return send(values, lambda x, y, z, core: (x, y, core * 2 + z % 2, z // 2))


def stage_move(stage, distance):
    def move(x, y, z, core):
        spot = [x, y, z]
        spot[(stage + core) % 3] += distance
        return (spot[0], spot[1], spot[2], core)

    return move


def gather_stage(values, stage):
    arrived = [send(values, stage_move(stage, -distance)) for distance in (1, 2, 3)]
    return jnp.concatenate([values] + arrived, axis=0)


def reduce_stage(values, stage):
    rows = values.shape[0] // 4
    parts = [values[step * rows : (step + 1) * rows] for step in range(4)]
    total = parts[0].astype(F32)
    for distance in (1, 2, 3):
        total = total + send(parts[distance], stage_move(stage, distance)).astype(F32)
    return total


def reduce_rows(term):
    low = term.astype(BF16)
    half = low.shape[0] // 2
    total = low[:half].astype(F32) + swap_cores(low[half:]).astype(F32)
    for stage in (2, 1, 0):
        total = reduce_stage(total.astype(BF16), stage)
    return total


def row_order(place, core):
    x, y, z = place
    third, second, first, inner = jnp.meshgrid(
        jnp.arange(4), jnp.arange(4), jnp.arange(4), jnp.arange(10), indexing="ij"
    )
    if core == 0:
        sx, sy, sz = x + first, y + second, z + third
    else:
        sy, sz, sx = y + first, z + second, x + third
    numbers = device_number(sx % 4, sy % 4, sz % 4, core) * 10 + inner
    return numbers.reshape(-1).astype(jnp.int32)


def slice_order():
    x, zh, zl, y, core, inner = jnp.meshgrid(
        *(jnp.arange(n) for n in (4, 2, 2, 4, 2, 10)), indexing="ij"
    )
    return (device_number(x, y, zh * 2 + zl, core) * 10 + inner).reshape(-1).astype(jnp.int32)


def one_hot(order):
    return (jnp.arange(order.shape[0], dtype=jnp.int32)[:, None] == order[None, :]).astype(BF16)


def exact_move(values, hot):
    high = values.astype(BF16)
    low = (values - high.astype(F32)).astype(BF16)
    return mm(high, hot) + mm(low, hot)


def mm(left, right):
    return jnp.dot(left, right, preferred_element_type=F32)


def mm_nt(left, right):
    return lax.dot_general(left, right, (((1,), (1,)), ((), ())), preferred_element_type=F32)


def mm_tn(left, right):
    return lax.dot_general(left, right, (((0,), (0,)), ((), ())), preferred_element_type=F32)


def norm_factor(values):
    return lax.rsqrt(jnp.mean(values * values, axis=-1, keepdims=True) + EPSILON)


def norm_back(values, factor, gain, grad):
    weighted = gain * grad
    inner = jnp.mean(weighted * values, axis=-1, keepdims=True)
    return factor * weighted - values * (factor * factor * factor) * inner


def rope_tables(angles_at, head_size):
    half_size = head_size // 2
    powers = jnp.arange(half_size, dtype=F32) * (2.0 / head_size)
    speeds = jnp.power(ROPE_BASE, -powers)
    angles = angles_at[:, None] * speeds[None, :]
    return (jnp.cos(angles)[:, None, :], jnp.sin(angles)[:, None, :])


def apply_rotary(values, cosine_values, sine_values):
    half_size = values.shape[-1] // 2
    leading = values[..., :half_size]
    trailing = values[..., half_size:]
    return jnp.concatenate(
        [
            leading * cosine_values - trailing * sine_values,
            trailing * cosine_values + leading * sine_values,
        ],
        axis=-1,
    )


def group_places(pair_row, devices_ctx, block_size):
    slots = jnp.arange(devices_ctx * 2 * block_size, dtype=jnp.int32)
    owners = slots // (2 * block_size)
    inside = slots % (2 * block_size)
    columns = jnp.arange(devices_ctx, dtype=jnp.int32)
    paired = jnp.sum(jnp.where(owners[:, None] == columns[None, :], pair_row[None, :], 0), axis=1)
    blocks = jnp.where(inside < block_size, paired, 2 * devices_ctx - 1 - paired)
    return blocks * block_size + inside % block_size


def head_scores(query_head, key_head, allowed, scale_factor):
    scores = (
        jnp.einsum("grd,kd->grk", query_head, key_head, preferred_element_type=F32) * scale_factor
    )
    return jnp.where(allowed[None], scores, MASKED_SCORE)


def head_forward(query_head, key_head, value_head, allowed, scale_factor):
    scores = head_scores(query_head, key_head, allowed, scale_factor)
    row_top = jnp.max(scores, axis=-1, keepdims=True)
    expons = jnp.exp(scores - row_top)
    totals = jnp.sum(expons, axis=-1, keepdims=True)
    chances = (expons / totals).astype(BF16)
    outcome = jnp.einsum("grk,kd->grd", chances, value_head, preferred_element_type=F32)
    return (outcome, row_top[..., 0] + jnp.log(totals[..., 0]))


def head_backward(query_head, key_head, value_head, grad_head, log_totals, allowed, scale_factor):
    scores = head_scores(query_head, key_head, allowed, scale_factor)
    chances = jnp.exp(scores - log_totals[..., None])
    chances_low = chances.astype(BF16)
    chance_grad = jnp.einsum("grd,kd->grk", grad_head, value_head, preferred_element_type=F32)
    weighted = jnp.sum(chances * chance_grad, axis=-1, keepdims=True)
    score_grad = (chances * (chance_grad - weighted)).astype(BF16)
    query_grad = (
        jnp.einsum("grk,kd->grd", score_grad, key_head, preferred_element_type=F32) * scale_factor
    )
    key_grad = (
        jnp.einsum("grk,grd->kd", score_grad, query_head, preferred_element_type=F32)
        * scale_factor
    )
    value_grad = jnp.einsum("grk,grd->kd", chances_low, grad_head, preferred_element_type=F32)
    return (query_grad, key_grad, value_grad)


def pack_units(weight):
    rows = weight.shape[0]
    runs = weight.reshape(rows, 8, 4, 2, 2, 28).transpose(1, 0, 2, 4, 3, 5)
    runs = jnp.pad(runs, ((0, 0),) * 5 + ((0, PAD_UNITS - 28),))
    return runs.reshape(8, rows, 16 * PAD_UNITS)


def unpack_units(packed):
    rows = packed.shape[1]
    runs = packed.reshape(8, rows, 4, 2, 2, PAD_UNITS)[..., :28]
    return runs.transpose(1, 0, 2, 4, 3, 5).reshape(rows, 8 * 16 * 28)


def local(
    tokens,
    norm_gain,
    w_query,
    w_key,
    w_value,
    w_out,
    mlp_gain,
    w_gate,
    w_up,
    w_down,
    block_pair,
    seq_len,
    seq_start,
    out_grad,
):
    shard_rows, model_width = tokens.shape
    block_size = shard_rows // 2
    devices_ctx = 8
    at_y, at_zh, at_x, at_zl, at_core = (lax.axis_index(name) for name in AXES)
    place = (at_x, at_y, at_zh * 2 + at_zl)
    position = at_y * 2 + at_zh
    query_per_key = QUERY_HEADS // KEY_VALUE_HEADS
    scale_factor = HEAD_WIDTH ** (-0.5)

    gains = jnp.stack([norm_gain, mlp_gain], axis=1)
    gains = jnp.pad(gains, ((0, 0), (0, GAIN_COLS - 2)))
    packed = jnp.concatenate([w_key, w_value, gains, w_query, w_out], axis=1)
    packed = gather_stage(packed, 0)
    packed = gather_stage(packed, 1)
    split = 2 * KEY_WIDTH + GAIN_COLS
    key_part = gather_stage(packed[:, :split], 2)
    key_other = swap_cores(key_part)
    query_part = gather_stage(packed[:, split : split + QUERY_WIDTH], 2)
    query_other = swap_cores(query_part)
    out_part = gather_stage(packed[:, split + QUERY_WIDTH :], 2)
    out_other = swap_cores(out_part)

    units = jnp.concatenate([pack_units(w_gate), pack_units(w_up)], axis=2)
    units = lax.all_to_all(units, ROW_AXES, 0, 0, tiled=True)
    units_full = lax.all_gather(
        units.reshape(-1, units.shape[2]), SLICE_AXES, axis=0, tiled=True
    )
    down_rows = swap_half_core(jnp.pad(w_down, ((0, PAD_UNITS - w_down.shape[0]), (0, 0))))
    down_full = lax.all_gather(down_rows, SLICE_AXES, axis=0, tiled=True)

    places_all = group_places(block_pair[0], devices_ctx, block_size)
    places_here = lax.dynamic_slice_in_dim(places_all, position * shard_rows, shard_rows)
    first_slot = seq_start[0]
    seq_length = seq_len[0]
    valid_all = (places_all >= first_slot) & (places_all < first_slot + seq_length)
    valid_here = (places_here >= first_slot) & (places_here < first_slot + seq_length)
    allowed = valid_here[:, None] & valid_all[None, :] & (
        places_all[None, :] <= places_here[:, None]
    ) | (places_all[None, :] == places_here[:, None])
    cosine, sine = rope_tables((places_here - first_slot).astype(F32), HEAD_WIDTH)
    row_weight = valid_here.astype(F32)[:, None]

    orders = [row_order(place, core) for core in (0, 1)]
    mine = jnp.where(at_core == 0, orders[0], orders[1])
    other = jnp.where(at_core == 0, orders[1], orders[0])
    hot = one_hot(jnp.concatenate([mine, other]))
    half = model_width // 2
    slice_hot = one_hot(slice_order())

    cotangent = out_grad.astype(F32) * row_weight
    feed_grad = cotangent.astype(BF16)
    grad_rows = lax.all_gather(feed_grad, ROW_AXES, axis=0, tiled=True)

    inputs = tokens.astype(F32)
    factor_one = norm_factor(inputs)
    tokens_moved = mm(tokens, hot)
    gain_cols = jnp.concatenate([key_part[:, 2 * KEY_WIDTH :], key_other[:, 2 * KEY_WIDTH :]])
    gain_rows = gain_cols.T[:8]
    gain_one = gain_rows[0:1].astype(F32)
    gain_two = mm_nt(gain_rows, hot)[1:2]
    normed = (tokens_moved * factor_one * gain_one).astype(BF16)

    def project(rows, part, other_part):
        return mm(rows[:, :half], part) + mm(rows[:, half:], other_part)

    key_value = project(normed, key_part[:, : 2 * KEY_WIDTH], key_other[:, : 2 * KEY_WIDTH])
    keys = apply_rotary(
        key_value[:, :KEY_WIDTH].reshape(shard_rows, KEY_VALUE_HEADS, HEAD_WIDTH), cosine, sine
    ).reshape(shard_rows, KEY_WIDTH)
    low_pairs = jnp.concatenate([keys, key_value[:, KEY_WIDTH:]], axis=1).astype(BF16)
    gathered = lax.all_to_all(
        jnp.broadcast_to(low_pairs[None], (devices_ctx,) + low_pairs.shape),
        ("y", "zh"),
        0,
        0,
        tiled=True,
    ).reshape(devices_ctx * shard_rows, 2 * KEY_WIDTH)

    query_pre = project(normed, query_part, query_other)
    queries = apply_rotary(
        query_pre.reshape(shard_rows, QUERY_HEADS, HEAD_WIDTH), cosine, sine
    ).astype(BF16)
    query_heads = queries.reshape(
        shard_rows, KEY_VALUE_HEADS, query_per_key, HEAD_WIDTH
    ).transpose(1, 2, 0, 3)
    key_heads = (
        gathered[:, :KEY_WIDTH].reshape(-1, KEY_VALUE_HEADS, HEAD_WIDTH).transpose(1, 0, 2)
    )
    value_heads = (
        gathered[:, KEY_WIDTH:].reshape(-1, KEY_VALUE_HEADS, HEAD_WIDTH).transpose(1, 0, 2)
    )

    def forward_head(pieces):
        return head_forward(pieces[0], pieces[1], pieces[2], allowed, scale_factor)

    head_outs, log_totals = lax.map(forward_head, (query_heads, key_heads, value_heads))
    attended = (
        head_outs.transpose(2, 0, 1, 3).reshape(shard_rows, QUERY_WIDTH).astype(BF16)
    )
    attended_moved = mm(attended, hot).astype(BF16)
    branch = project(attended_moved, out_part, out_other)
    middle = inputs + branch
    factor_two = norm_factor(middle)
    normed_two = (middle * factor_two * gain_two).astype(BF16)
    normed_two = mm(normed_two, slice_hot).astype(BF16)

    normed_rows = lax.all_gather(normed_two, ROW_AXES, axis=0, tiled=True)
    gate_up = mm(normed_rows, units_full)
    units_here = gate_up.shape[1] // 2
    gate_value = gate_up[:, :units_here]
    up_value = gate_up[:, units_here:]
    gate_sigmoid = 1.0 / (1.0 + jnp.exp(-gate_value))
    gate_silu = gate_value * gate_sigmoid
    hidden = (gate_silu * up_value).astype(BF16)
    hidden_grad = mm_nt(grad_rows, down_full)
    gate_low = hidden_grad * up_value * gate_sigmoid * (1.0 + gate_value * (1.0 - gate_sigmoid))
    up_low = hidden_grad * gate_silu
    unit_grads = jnp.concatenate([gate_low.astype(BF16), up_low.astype(BF16)], axis=1)
    normed_two_grad = lax.psum_scatter(
        mm_nt(unit_grads, units_full).astype(BF16), ROW_AXES, scatter_dimension=0, tiled=True
    ).astype(F32)
    feed_out = lax.psum_scatter(
        mm(hidden, down_full).astype(BF16), ROW_AXES, scatter_dimension=0, tiled=True
    ).astype(F32)
    unit_term = lax.psum_scatter(
        mm_tn(normed_rows, unit_grads).astype(BF16), SLICE_AXES, scatter_dimension=0, tiled=True
    )
    down_term = lax.psum_scatter(
        mm_tn(hidden, grad_rows).astype(BF16), SLICE_AXES, scatter_dimension=0, tiled=True
    )
    final_out = middle + feed_out
    sums = jnp.stack(
        [
            jnp.sum(row_weight * branch * branch),
            jnp.sum(row_weight * feed_out * feed_out),
            jnp.sum(row_weight * final_out * final_out),
        ]
    )
    sums = jnp.broadcast_to(jnp.pad(sums, (0, 125))[None], (8, 128))
    sums = sums + send(sums, lambda x, y, z, core: (x, y, z + 2, core))
    sums = sums + send(sums, lambda x, y, z, core: (x, y ^ 1, z, core))
    sums = sums + send(sums, lambda x, y, z, core: (x, y ^ 2, z, core))
    seq_rms = jnp.sqrt(sums[:1, :3] / (seq_length.astype(F32) * model_width))

    normed_two_grad = exact_move(normed_two_grad, slice_hot.T)
    mid_grad = cotangent + norm_back(middle, factor_two, gain_two, normed_two_grad)
    gain_two_rows = mm((normed_two_grad * middle * factor_two).astype(BF16), hot).astype(BF16)
    branch_grad = mid_grad.astype(BF16)
    attended_grad = jnp.concatenate(
        [mm_nt(branch_grad, out_part), mm_nt(branch_grad, out_other)], axis=1
    ).astype(BF16)
    attended_grad = mm_nt(attended_grad, hot).astype(BF16)
    out_sum = reduce_rows(mm_tn(attended_moved, branch_grad))
    grad_heads = attended_grad.reshape(
        shard_rows, KEY_VALUE_HEADS, query_per_key, HEAD_WIDTH
    ).transpose(1, 2, 0, 3)

    def backward_head(pieces):
        return head_backward(
            pieces[0], pieces[1], pieces[2], pieces[3], pieces[4], allowed, scale_factor
        )

    query_parts, key_pieces, value_pieces = lax.map(
        backward_head, (query_heads, key_heads, value_heads, grad_heads, log_totals)
    )
    query_grad = query_parts.transpose(2, 0, 1, 3).reshape(shard_rows, QUERY_HEADS, HEAD_WIDTH)
    pair_grads = jnp.concatenate(
        [
            key_pieces.transpose(1, 0, 2).reshape(-1, KEY_WIDTH),
            value_pieces.transpose(1, 0, 2).reshape(-1, KEY_WIDTH),
        ],
        axis=1,
    ).astype(BF16)
    pair_grads = lax.all_to_all(
        pair_grads.reshape(devices_ctx, shard_rows, 2 * KEY_WIDTH), ("y", "zh"), 0, 0, tiled=True
    )
    pair_grads = jnp.sum(pair_grads.astype(F32), axis=0)
    query_low = (
        apply_rotary(query_grad, cosine, -sine).reshape(shard_rows, QUERY_WIDTH).astype(BF16)
    )
    key_grad = apply_rotary(
        pair_grads[:, :KEY_WIDTH].reshape(shard_rows, KEY_VALUE_HEADS, HEAD_WIDTH), cosine, -sine
    ).reshape(shard_rows, KEY_WIDTH)
    pair_low = jnp.concatenate([key_grad, pair_grads[:, KEY_WIDTH:]], axis=1).astype(BF16)
    query_sum = reduce_rows(mm_tn(normed, query_low))

    def project_back(grads, part, other_part):
        return jnp.concatenate([mm_nt(grads, part), mm_nt(grads, other_part)], axis=1)

    normed_grad = project_back(query_low, query_part, query_other) + project_back(
        pair_low, key_part[:, : 2 * KEY_WIDTH], key_other[:, : 2 * KEY_WIDTH]
    )
    input_part = norm_back(tokens_moved, factor_one, gain_one, normed_grad)
    input_grad = (mid_grad + exact_move(input_part, hot.T)).astype(BF16)
    gain_one_rows = (normed_grad * tokens_moved * factor_one).astype(BF16)
    picks = jnp.arange(GAIN_COLS) < GAIN_COLS // 2
    picks = jnp.broadcast_to(picks[None], (shard_rows, GAIN_COLS))
    gain_terms = mm_tn(gain_one_rows, picks.astype(BF16)) + mm_tn(
        gain_two_rows, (~picks).astype(BF16)
    )
    pair_sum = reduce_rows(
        jnp.concatenate([mm_tn(normed, pair_low), gain_terms], axis=1)
    )

    unit_term = lax.all_to_all(
        unit_term.reshape(8, -1, unit_term.shape[1]), ROW_AXES, 0, 0, tiled=True
    ).astype(F32)
    down_sum = swap_half_core(down_term)[: w_down.shape[0]].astype(F32)
    return (
        final_out.astype(BF16),
        input_grad,
        pair_sum[:, 2 * KEY_WIDTH],
        query_sum,
        pair_sum[:, :KEY_WIDTH],
        pair_sum[:, KEY_WIDTH : 2 * KEY_WIDTH],
        out_sum,
        pair_sum[:, 2 * KEY_WIDTH + GAIN_COLS - 1],
        unpack_units(unit_term[:, :, :units_here]),
        unpack_units(unit_term[:, :, units_here:]),
        down_sum,
        seq_rms,
    )


def solution(mesh):
    fine = Mesh(mesh.devices.reshape(SIZES), AXES)
    rows = P(AXES, None)
    flat = P(AXES)
    group = ("x", "zl", "core")
    in_specs = (
        (rows, flat, rows, rows, rows, rows, flat, rows, rows, rows)
        + (P(group, None), P(group), P(group))
        + (rows,)
    )
    out_specs = (rows, rows, flat, rows, rows, rows, rows, flat, rows, rows, rows, P(group, None))
    return jax.shard_map(
        local, mesh=fine, in_specs=in_specs, out_specs=out_specs, check_vma=False
    )
```

```python
import jax
import jax.numpy as jnp
from jax import lax
from jax.experimental import pallas as pl
from jax.experimental.pallas import tpu as pltpu
from jax.sharding import Mesh, PartitionSpec as P

QUERY_HEADS = 20
KEY_VALUE_HEADS = 5
HEAD_WIDTH = 64
QUERY_WIDTH = QUERY_HEADS * HEAD_WIDTH
KEY_WIDTH = KEY_VALUE_HEADS * HEAD_WIDTH
GAIN_COLS = 128
KERNEL_BYTES = 32 * 1024 * 1024
PAD_UNITS = 32

EPSILON = 1e-05
ROPE_BASE = 10000.0
MASKED_SCORE = -1e30

AXES = ("y", "zh", "x", "zl", "core")
SIZES = (4, 2, 4, 2, 2)
ROW_AXES = ("y", "core")
SLICE_AXES = ("x", "zh", "zl")
F32 = jnp.float32
BF16 = jnp.bfloat16


def device_number(x, y, z, core):
    return (((y * 2 + z // 2) * 4 + x) * 2 + z % 2) * 2 + core


def pairs_of(move):
    pairs = []
    for y in range(4):
        for z in range(4):
            for x in range(4):
                for core in range(2):
                    tx, ty, tz, tc = move(x, y, z, core)
                    pairs.append(
                        (device_number(x, y, z, core), device_number(tx % 4, ty % 4, tz % 4, tc))
                    )
    return pairs


def send(values, move):
    return lax.ppermute(values, AXES, pairs_of(move))


def swap_cores(values):
    return send(values, lambda x, y, z, core: (x, y, z, 1 - core))


def swap_half_core(values):
    return send(values, lambda x, y, z, core: (x, y, core * 2 + z % 2, z // 2))


def stage_move(stage, distance):
    def move(x, y, z, core):
        spot = [x, y, z]
        spot[(stage + core + 1) % 3] += distance
        return (spot[0], spot[1], spot[2], core)

    return move


def spread(values, stage):
    arrived = [send(values, stage_move(stage, -distance)) for distance in (1, 2, 3)]
    return [values] + arrived


def join(blocks):
    return lax.optimization_barrier(jnp.concatenate(blocks, axis=0))


def scatter(total, stage):
    low = total.astype(BF16)
    rows = low.shape[0] // 4
    parts = [low[step * rows : (step + 1) * rows] for step in range(4)]
    arrived = [send(parts[step], stage_move(stage, step)) for step in (1, 2, 3)]
    return [parts[0]] + arrived


def add_up(blocks):
    total = blocks[0].astype(F32)
    for block in blocks[1:]:
        total = total + block.astype(F32)
    return total


def phase(*values):
    return lax.optimization_barrier(values)


def along_y(values, distance):
    return send(values, lambda x, y, z, core: (x, y + distance, z, core))


def gather_rows(own):
    blocks = [own] + [along_y(own, -distance) for distance in (1, 2, 3)]
    return blocks + [swap_cores(block) for block in blocks]


def add_cores(own, other):
    return [(a.astype(F32) + swap_cores(b).astype(F32)) for a, b in zip(own, other)]


def reduce_blocks(sums):
    total = sums[0]
    for distance in (1, 2, 3):
        total = total + along_y(sums[distance].astype(BF16), distance).astype(F32)
    return total


def after(values, *earlier):
    return lax.optimization_barrier((values,) + earlier)[0]


def row_order(place, core):
    third, second, first, inner = jnp.meshgrid(
        jnp.arange(4), jnp.arange(4), jnp.arange(4), jnp.arange(10), indexing="ij"
    )
    spot = list(place)
    for stage, step in enumerate((first, second, third)):
        axis = (stage + core + 1) % 3
        spot[axis] = spot[axis] + step
    sx, sy, sz = spot
    numbers = device_number(sx % 4, sy % 4, sz % 4, core) * 10 + inner
    return numbers.reshape(-1).astype(jnp.int32)


def slice_order():
    x, zh, zl, y, core, inner = jnp.meshgrid(
        *(jnp.arange(n) for n in (4, 2, 2, 4, 2, 10)), indexing="ij"
    )
    return (device_number(x, y, zh * 2 + zl, core) * 10 + inner).reshape(-1).astype(jnp.int32)


def one_hot(order):
    return (jnp.arange(order.shape[0], dtype=jnp.int32)[:, None] == order[None, :]).astype(BF16)


def exact_move(values, hot):
    high = values.astype(BF16)
    low = (values - high.astype(F32)).astype(BF16)
    return mm(high, hot) + mm(low, hot)


def mm(left, right):
    return jnp.dot(left, right, preferred_element_type=F32)


def mm_nt(left, right):
    return lax.dot_general(left, right, (((1,), (1,)), ((), ())), preferred_element_type=F32)


def mm_tn(left, right):
    return lax.dot_general(left, right, (((0,), (0,)), ((), ())), preferred_element_type=F32)


def norm_factor(values):
    return lax.rsqrt(jnp.mean(values * values, axis=-1, keepdims=True) + EPSILON)


def norm_back(values, factor, gain, grad):
    weighted = gain * grad
    inner = jnp.mean(weighted * values, axis=-1, keepdims=True)
    return factor * weighted - values * (factor * factor * factor) * inner


def rope_tables(angles_at):
    half_size = HEAD_WIDTH // 2
    powers = jnp.arange(half_size, dtype=F32) * (2.0 / HEAD_WIDTH)
    speeds = jnp.power(ROPE_BASE, -powers)
    angles = angles_at[:, None] * speeds[None, :]
    cosine, sine = jnp.cos(angles), jnp.sin(angles)
    return (jnp.concatenate([cosine] * 4, axis=1), jnp.concatenate([-sine, sine] * 2, axis=1))


def rotate_pairs(values, cosine, sine):
    width = values.shape[1]
    half_size = HEAD_WIDTH // 2
    lanes = lax.broadcasted_iota(jnp.int32, values.shape, 1) % HEAD_WIDTH
    ahead = pltpu.roll(values, width - half_size, 1)
    behind = pltpu.roll(values, half_size, 1)
    return values * cosine + jnp.where(lanes < half_size, ahead, behind) * sine


def rotate_plain(values, cosine, sine):
    half_size = HEAD_WIDTH // 2
    leads = (jnp.arange(values.shape[1]) % HEAD_WIDTH < half_size)[None]
    partner = jnp.where(
        leads, jnp.roll(values, -half_size, axis=1), jnp.roll(values, half_size, axis=1)
    )
    return values * cosine + partner * sine


def wide_table(table, width):
    return jnp.concatenate([table] * (width // table.shape[1]), axis=1)


def low_high(rows):
    low = [rows[at : at + 64] for at in range(0, rows.shape[0], 128)]
    high = [rows[at + 64 : at + 128] for at in range(0, rows.shape[0], 128)]
    return jnp.concatenate(low, axis=0), jnp.concatenate(high, axis=0)


def stack_heads(rows, head):
    pieces = [
        rows[at : at + 64, (4 * head + step) * HEAD_WIDTH : (4 * head + step + 1) * HEAD_WIDTH]
        for at in (0, 64)
        for step in range(4)
    ]
    return jnp.concatenate(pieces, axis=0)


def unstack_heads(stack):
    halves = [
        jnp.concatenate([stack[at + 64 * step : at + 64 * step + 64] for step in range(4)], axis=1)
        for at in (0, 256)
    ]
    return jnp.concatenate(halves, axis=0)


def mask_bias(keys_ref, rows_ref):
    keys_low, keys_high = keys_ref[:512], keys_ref[512:]

    def bias(keys, lanes):
        seen = (keys[:, 0:1] <= rows_ref[0:1, lanes]) | (keys[:, 1:2] == rows_ref[1:2, lanes])
        return jnp.where(seen, 0.0, MASKED_SCORE).astype(F32)

    return bias(keys_low, slice(0, 512)), bias(keys_high, slice(256, 512))


def attend_kernel(q_ref, kv_ref, cos_ref, sin_ref, keys_ref, rows_ref, out_ref, turned_ref, log_ref):
    cosine = wide_table(cos_ref[...], QUERY_WIDTH)
    sine = wide_table(sin_ref[...], QUERY_WIDTH)
    queries = (rotate_pairs(q_ref[...], cosine, sine) * HEAD_WIDTH**-0.5).astype(BF16)
    turned_ref[...] = queries
    kv_low, kv_high = low_high(kv_ref[...])
    bias_low, bias_high = mask_bias(keys_ref, rows_ref)
    for head in range(KEY_VALUE_HEADS):
        at = slice(head * HEAD_WIDTH, (head + 1) * HEAD_WIDTH)
        vat = slice(KEY_WIDTH + head * HEAD_WIDTH, KEY_WIDTH + (head + 1) * HEAD_WIDTH)
        stack = stack_heads(queries, head)
        score_low = mm_nt(kv_low[:, at], stack) + bias_low
        score_high = mm_nt(kv_high[:, at], stack[256:]) + bias_high
        top_low = jnp.max(score_low, axis=0, keepdims=True)
        top_high = jnp.max(score_high, axis=0, keepdims=True)
        top = jnp.concatenate(
            [top_low[:, :256], jnp.maximum(top_low[:, 256:], top_high)], axis=1
        )
        exp_low = jnp.exp(score_low - top)
        exp_high = jnp.exp(score_high - top[:, 256:])
        total = jnp.sum(exp_low, axis=0, keepdims=True)
        total_high = jnp.sum(exp_high, axis=0, keepdims=True)
        total = jnp.concatenate([total[:, :256], total[:, 256:] + total_high], axis=1)
        result = mm_tn(kv_low[:, vat], exp_low.astype(BF16))
        result_high = mm_tn(kv_high[:, vat], exp_high.astype(BF16))
        result = jnp.concatenate([result[:, :256], result[:, 256:] + result_high], axis=1)
        result = (result / total).T
        out_ref[:, head * 256 : (head + 1) * 256] = unstack_heads(result).astype(BF16)
        log_ref[head : head + 1, :] = top + jnp.log(total)


def attend_back_kernel(
    q_ref, kv_ref, out_ref, grad_ref, log_ref, cos_ref, sin_ref, keys_ref, rows_ref, dq_ref, dkv_ref
):
    kv_low, kv_high = low_high(kv_ref[...])
    bias_low, bias_high = mask_bias(keys_ref, rows_ref)
    queries = q_ref[...]
    outs = out_ref[...]
    grads = grad_ref[...]
    ones = jnp.ones((8, HEAD_WIDTH), F32)
    dq_parts, dk_low, dk_high, dv_low, dv_high = [], [], [], [], []
    for head in range(KEY_VALUE_HEADS):
        at = slice(head * HEAD_WIDTH, (head + 1) * HEAD_WIDTH)
        vat = slice(KEY_WIDTH + head * HEAD_WIDTH, KEY_WIDTH + (head + 1) * HEAD_WIDTH)
        stack = stack_heads(queries, head)
        grad = stack_heads(grads, head)
        product = grad.astype(F32) * stack_heads(outs, head).astype(F32)
        delta = lax.dot_general(
            ones,
            product,
            (((1,), (1,)), ((), ())),
            preferred_element_type=F32,
            precision=lax.Precision.HIGHEST,
        )[0:1]
        logs = log_ref[head : head + 1, :]
        key_low, key_high = kv_low[:, at], kv_high[:, at]
        probs_low = jnp.exp(mm_nt(key_low, stack) + bias_low - logs)
        probs_high = jnp.exp(mm_nt(key_high, stack[256:]) + bias_high - logs[:, 256:])
        back_low = mm_nt(kv_low[:, vat], grad)
        back_high = mm_nt(kv_high[:, vat], grad[256:])
        score_low = (probs_low * (back_low - delta)).astype(BF16)
        score_high = (probs_high * (back_high - delta[:, 256:])).astype(BF16)
        dv_low.append(mm(probs_low.astype(BF16), grad))
        dv_high.append(mm(probs_high.astype(BF16), grad[256:]))
        dk_low.append(mm(score_low, stack))
        dk_high.append(mm(score_high, stack[256:]))
        dq = mm_tn(key_low, score_low)
        dq_high = mm_tn(key_high, score_high)
        dq = jnp.concatenate([dq[:, :256], dq[:, 256:] + dq_high], axis=1)
        dq_parts.append(unstack_heads((dq * HEAD_WIDTH**-0.5).T))
    cosine = wide_table(cos_ref[...], QUERY_WIDTH)
    sine = wide_table(sin_ref[...], QUERY_WIDTH)
    dq_ref[...] = rotate_pairs(jnp.concatenate(dq_parts, axis=1), cosine, -sine).astype(BF16)
    low = jnp.concatenate(dk_low + dv_low, axis=1).astype(BF16)
    high = jnp.concatenate(dk_high + dv_high, axis=1).astype(BF16)
    for at in range(8):
        dkv_ref[128 * at : 128 * at + 64] = low[64 * at : 64 * at + 64]
        dkv_ref[128 * at + 64 : 128 * at + 128] = high[64 * at : 64 * at + 64]


def run_kernel(kernel, shapes, operands, flops):
    return pl.pallas_call(
        kernel,
        out_shape=[jax.ShapeDtypeStruct(shape, kind) for shape, kind in shapes],
        in_specs=[pl.BlockSpec(memory_space=pltpu.VMEM)] * len(operands),
        out_specs=[pl.BlockSpec(memory_space=pltpu.VMEM)] * len(shapes),
        compiler_params=pltpu.CompilerParams(vmem_limit_bytes=KERNEL_BYTES),
        cost_estimate=pl.CostEstimate(
            flops=flops,
            bytes_accessed=sum(v.size * v.dtype.itemsize for v in operands),
            transcendentals=0,
        ),
    )(*operands)


def unpack_kernel(slices_ref, units_ref, down_ref):
    for block in range(16):
        rows = slices_ref[block * 128 : block * 128 + 128]
        units_ref[block * 80 : block * 80 + 80] = rows[:80]
        down_ref[block * 32 : block * 32 + 32, :1024] = rows[80:112]
        down_ref[block * 32 : block * 32 + 16, 1024:] = rows[112:, :256]
        down_ref[block * 32 + 16 : block * 32 + 32, 1024:] = rows[112:, 256:512]


def feed_kernel(
    xa_ref,
    xb_ref,
    ga_ref,
    gb_ref,
    units_ref,
    down_ref,
    hidden_ref,
    unit_ref,
    back_a_ref,
    back_b_ref,
    out_a_ref,
    out_b_ref,
    rows_ref,
    grads_ref,
    sems,
):
    half = xa_ref.shape[0]
    copies = [
        pltpu.make_async_copy(xa_ref, rows_ref.at[0:half], sems.at[0]),
        pltpu.make_async_copy(xb_ref, rows_ref.at[half : 2 * half], sems.at[1]),
        pltpu.make_async_copy(ga_ref, grads_ref.at[0:half], sems.at[2]),
        pltpu.make_async_copy(gb_ref, grads_ref.at[half : 2 * half], sems.at[3]),
    ]
    for copy in copies:
        copy.start()
    copies[0].wait()
    copies[1].wait()
    units = units_ref.shape[1] // 2
    both = mm(rows_ref[...], units_ref[...])
    gate, up = both[:, :units], both[:, units:]
    sigmoid = 1.0 / (1.0 + jnp.exp(-gate))
    silu = gate * sigmoid
    hidden = (silu * up).astype(BF16)
    hidden_ref[...] = hidden
    copies[2].wait()
    copies[3].wait()
    hidden_grad = mm_nt(grads_ref[...], down_ref[...])
    gate_low = (hidden_grad * up * sigmoid * (1.0 + gate * (1.0 - sigmoid))).astype(BF16)
    up_low = (hidden_grad * silu).astype(BF16)
    unit = jnp.concatenate([gate_low, up_low], axis=1)
    unit_ref[...] = unit
    back = mm_nt(unit, units_ref[...]).astype(BF16)
    back_a_ref[...] = back[:half]
    back_b_ref[...] = back[half:]
    outs = mm(hidden, down_ref[...]).astype(BF16)
    out_a_ref[...] = outs[:half]
    out_b_ref[...] = outs[half:]


def feed_chunk(rows_a, rows_b, grads_a, grads_b, units, down):
    count, width = rows_a.shape[0] * 2, rows_a.shape[1]
    vmem = pl.BlockSpec(memory_space=pltpu.VMEM)
    anywhere = pl.BlockSpec(memory_space=pl.ANY)
    shapes = [(count, down.shape[0]), (count, units.shape[1])] + [rows_a.shape] * 4
    return pl.pallas_call(
        feed_kernel,
        out_shape=[jax.ShapeDtypeStruct(shape, BF16) for shape in shapes],
        in_specs=[anywhere] * 4 + [vmem] * 2,
        out_specs=[vmem] * 6,
        scratch_shapes=[
            pltpu.VMEM((count, width), BF16),
            pltpu.VMEM((count, width), BF16),
            pltpu.SemaphoreType.DMA((4,)),
        ],
        compiler_params=pltpu.CompilerParams(vmem_limit_bytes=KERNEL_BYTES),
        cost_estimate=pl.CostEstimate(
            flops=2 * count * width * 3 * units.shape[1],
            bytes_accessed=2 * (units.size + down.size + 4 * rows_a.size),
            transcendentals=0,
        ),
    )(rows_a, rows_b, grads_a, grads_b, units, down)


def weight_kernel(*refs):
    sources, term_out = refs[:24], refs[24]
    rows, unit, grads, hidden = refs[25:29]
    sems = refs[29]
    copies = []
    for step in range(4):
        base = step * 256
        copies += [
            pltpu.make_async_copy(
                sources[step], rows.at[base : base + 128], sems.at[6 * step]
            ),
            pltpu.make_async_copy(
                sources[step + 4], rows.at[base + 128 : base + 256], sems.at[6 * step + 1]
            ),
            pltpu.make_async_copy(
                sources[step + 20], unit.at[base : base + 256], sems.at[6 * step + 2]
            ),
            pltpu.make_async_copy(
                sources[step + 8], grads.at[base : base + 128], sems.at[6 * step + 3]
            ),
            pltpu.make_async_copy(
                sources[step + 12], grads.at[base + 128 : base + 256], sems.at[6 * step + 4]
            ),
            pltpu.make_async_copy(
                sources[step + 16], hidden.at[base : base + 256], sems.at[6 * step + 5]
            ),
        ]
    for copy in copies:
        copy.start()
    for copy in copies:
        copy.wait()
    for at in range(0, 16, 4):
        total = mm_tn(rows[:, at * 80 : at * 80 + 320], unit[...]).astype(BF16)
        for block in range(4):
            term_out[(at + block) * 128 : (at + block) * 128 + 80] = total[
                block * 80 : block * 80 + 80
            ]
    for at in range(0, 16, 4):
        total = mm_tn(hidden[:, at * 32 : at * 32 + 128], grads[...]).astype(BF16)
        for block in range(4):
            rows_here = total[block * 32 : block * 32 + 32]
            base = (at + block) * 128
            term_out[base + 80 : base + 112] = rows_here[:, :1024]
            term_out[base + 112 : base + 128, 0:256] = rows_here[:16, 1024:]
            term_out[base + 112 : base + 128, 256:512] = rows_here[16:, 1024:]
            term_out[base + 112 : base + 128, 512:] = jnp.zeros((16, 512), BF16)


def weight_terms(rows, grads, hidden, unit):
    sources = list(rows) + list(grads) + list(hidden) + list(unit)
    count = 8 * rows[0].shape[0]
    return pl.pallas_call(
        weight_kernel,
        out_shape=jax.ShapeDtypeStruct((2048, 1024), BF16),
        in_specs=[pl.BlockSpec(memory_space=pl.ANY)] * 24,
        out_specs=pl.BlockSpec(memory_space=pltpu.VMEM),
        scratch_shapes=[
            pltpu.VMEM((count, rows[0].shape[1]), BF16),
            pltpu.VMEM((count, unit[0].shape[1]), BF16),
            pltpu.VMEM((count, grads[0].shape[1]), BF16),
            pltpu.VMEM((count, hidden[0].shape[1]), BF16),
            pltpu.SemaphoreType.DMA((24,)),
        ],
        compiler_params=pltpu.CompilerParams(vmem_limit_bytes=KERNEL_BYTES),
        cost_estimate=pl.CostEstimate(
            flops=2 * count * 1280 * 1536,
            bytes_accessed=sum(2 * v.size for v in sources) + 4 * 2**20,
            transcendentals=0,
        ),
    )(*sources)


def pack_slice(units, down):
    rest = jnp.concatenate([down[:16, 1024:], down[16:, 1024:]], axis=1)
    rest = jnp.pad(rest, ((0, 0), (0, 512)))
    return jnp.concatenate([units, down[:, :1024], rest], axis=0)


def unpack_slice(rows):
    rest = jnp.concatenate([rows[112:, :256], rows[112:, 256:512]], axis=0)
    return rows[:80], jnp.concatenate([rows[80:112], rest], axis=1)


def group_places(pair_row, devices_ctx, block_size):
    slots = jnp.arange(devices_ctx * 2 * block_size, dtype=jnp.int32)
    owners = slots // (2 * block_size)
    inside = slots % (2 * block_size)
    columns = jnp.arange(devices_ctx, dtype=jnp.int32)
    paired = jnp.sum(jnp.where(owners[:, None] == columns[None, :], pair_row[None, :], 0), axis=1)
    blocks = jnp.where(inside < block_size, paired, 2 * devices_ctx - 1 - paired)
    return blocks * block_size + inside % block_size


def pack_units(weight):
    rows = weight.shape[0]
    runs = weight.reshape(rows, 8, 4, 2, 2, 28).transpose(1, 0, 2, 4, 3, 5)
    runs = jnp.pad(runs, ((0, 0),) * 5 + ((0, PAD_UNITS - 28),))
    return runs.reshape(8, rows, 16 * PAD_UNITS)


def unpack_units(packed):
    rows = packed.shape[1]
    runs = packed.reshape(8, rows, 4, 2, 2, PAD_UNITS)[..., :28]
    return runs.transpose(1, 0, 2, 4, 3, 5).reshape(rows, 8 * 16 * 28)


def local(
    tokens,
    norm_gain,
    w_query,
    w_key,
    w_value,
    w_out,
    mlp_gain,
    w_gate,
    w_up,
    w_down,
    block_pair,
    seq_len,
    seq_start,
    out_grad,
):
    shard_rows, model_width = tokens.shape
    block_size = shard_rows // 2
    half = model_width // 2
    devices_ctx = 8
    at_y, at_zh, at_x, at_zl, at_core = (lax.axis_index(name) for name in AXES)
    place = (at_x, at_y, at_zh * 2 + at_zl)
    position = at_y * 2 + at_zh
    pair_cols = 2 * KEY_WIDTH
    split = pair_cols + GAIN_COLS

    gains = jnp.stack([norm_gain, mlp_gain], axis=1)
    gains = jnp.pad(gains, ((0, 0), (0, GAIN_COLS - 2)))
    front = spread(jnp.concatenate([w_key, w_value, gains, w_query, w_out], axis=1), 0)
    units = jnp.concatenate([pack_units(w_gate), pack_units(w_up)], axis=2)
    down_rows = jnp.pad(w_down, ((0, PAD_UNITS - w_down.shape[0]), (0, 0)))

    places_all = group_places(block_pair[0], devices_ctx, block_size)
    places_here = lax.dynamic_slice_in_dim(places_all, position * shard_rows, shard_rows)
    first_slot = seq_start[0]
    seq_length = seq_len[0]
    valid_all = (places_all >= first_slot) & (places_all < first_slot + seq_length)
    valid_here = (places_here >= first_slot) & (places_here < first_slot + seq_length)
    key_places = jnp.stack([jnp.where(valid_all, places_all, 1 << 20), places_all], axis=1)
    key_places = key_places.reshape(8, 2, 64, 2).transpose(1, 0, 2, 3).reshape(-1, 2)
    row_places = jnp.stack([jnp.where(valid_here, places_here, -1), places_here])
    row_places = jnp.concatenate([row_places[:, :64]] * 4 + [row_places[:, 64:]] * 4, axis=1)
    cosine, sine = rope_tables((places_here - first_slot).astype(F32))
    key_cosine = jnp.concatenate([cosine] * 3, axis=1)[:, :KEY_WIDTH]
    key_sine = jnp.concatenate([sine] * 3, axis=1)[:, :KEY_WIDTH]
    row_weight = valid_here.astype(F32)[:, None]

    cotangent = out_grad.astype(F32) * row_weight
    feed_grad = cotangent.astype(BF16)
    grad_rows = lax.all_gather(feed_grad, ROW_AXES, axis=0, tiled=True)

    (
        *arrived,
        units,
        down_rows,
        cosine,
        sine,
        key_cosine,
        key_sine,
        key_places,
        row_places,
        tokens,
    ) = phase(
        *front,
        units,
        down_rows,
        cosine,
        sine,
        key_cosine,
        key_sine,
        key_places,
        row_places,
        tokens,
    )

    front = spread(join(arrived), 1)
    units = lax.all_to_all(units, ROW_AXES, 0, 0, tiled=True)
    down_rows = swap_half_core(down_rows)
    orders = [row_order(place, core) for core in (0, 1)]
    mine = jnp.where(at_core == 0, orders[0], orders[1])
    other = jnp.where(at_core == 0, orders[1], orders[0])
    hot, slice_hot = one_hot(jnp.concatenate([mine, other])), one_hot(slice_order())
    inputs = tokens.astype(F32)
    factor_one = norm_factor(inputs)
    tokens_moved = mm(tokens, hot)
    *arrived, units, down_rows, hot, slice_hot, factor_one, tokens_moved = phase(
        *front, units, down_rows, hot, slice_hot, factor_one, tokens_moved
    )

    front = join(arrived)
    slices = pack_slice(units.reshape(-1, units.shape[2]), down_rows)
    slices = lax.all_gather(slices, SLICE_AXES, axis=0, tiled=True)
    *key_part, front = phase(*spread(front[:, :split], 2), front)

    key_part = join(key_part)
    key_part, key_other, front = phase(key_part, swap_cores(key_part), front)

    gain_cols = jnp.concatenate([key_part[:, pair_cols:], key_other[:, pair_cols:]])
    gain_rows = gain_cols.T[:8]
    gain_one = gain_rows[0:1].astype(F32)
    normed = (tokens_moved * factor_one * gain_one).astype(BF16)

    def project(rows, part, other_part):
        return mm(rows[:, :half], part) + mm(rows[:, half:], other_part)

    key_value = project(normed, key_part[:, :pair_cols], key_other[:, :pair_cols])
    keys = rotate_plain(key_value[:, :KEY_WIDTH], key_cosine, key_sine)
    low_pairs = jnp.concatenate([keys, key_value[:, KEY_WIDTH:]], axis=1).astype(BF16)
    gathered = lax.all_to_all(
        jnp.broadcast_to(low_pairs[None], (devices_ctx,) + low_pairs.shape),
        ("y", "zh"),
        0,
        0,
        tiled=True,
    ).reshape(devices_ctx * shard_rows, pair_cols)
    rest_part = spread(front[:, split:], 2)
    grad_blocks = [
        lax.dynamic_slice_in_dim(
            grad_rows, ((at_y + step) % 4 * 2 + (at_core + side) % 2) * shard_rows, shard_rows
        )
        for side in (0, 1)
        for step in range(4)
    ]
    gain_two = mm_nt(gain_rows, hot)[1:2]
    normed_swap = swap_cores(normed[:, half:])
    *arrived, gathered, gain_two, normed, normed_swap = phase(
        *rest_part, *grad_blocks, gathered, gain_two, normed, normed_swap
    )

    query_part = join([block[:, :QUERY_WIDTH] for block in arrived[:4]])
    out_part = join([block[:, QUERY_WIDTH:] for block in arrived[:4]])
    grad_blocks = arrived[4:]
    query_other = swap_cores(query_part)
    out_other = swap_cores(out_part)
    query_pre = project(normed, query_part, query_other)
    attended, queries, logs = run_kernel(
        attend_kernel,
        [((shard_rows, QUERY_WIDTH), BF16), ((shard_rows, QUERY_WIDTH), BF16), ((8, 512), F32)],
        (query_pre, gathered, cosine, sine, key_places, row_places),
        shard_rows * 1024 * QUERY_WIDTH * 4,
    )
    attended_moved = mm(attended, hot).astype(BF16)
    branch = project(attended_moved, out_part, out_other)
    middle = inputs + branch
    factor_two = norm_factor(middle)
    normed_two = (middle * factor_two * gain_two).astype(BF16)
    normed_two = mm(normed_two, slice_hot).astype(BF16)
    normed_two, middle, factor_two, branch = phase(normed_two, middle, factor_two, branch)

    row_blocks = [normed_two] + [along_y(normed_two, -distance) for distance in (1, 2, 3)]
    row_blocks = row_blocks + [swap_cores(normed_two), None, None, None]
    units_full, down_full = run_kernel(
        unpack_kernel, [((1280, 1024), BF16), ((512, 1280), BF16)], (slices,), 0
    )
    chunks = [None] * 4
    for step in (0, 1, 3, 2):
        if step:
            row_blocks[step] = after(row_blocks[step], chunks[0][0])
            row_blocks[step + 4] = swap_cores(row_blocks[step])
        chunks[step] = feed_chunk(
            row_blocks[step],
            row_blocks[step + 4],
            grad_blocks[step],
            grad_blocks[step + 4],
            units_full,
            down_full,
        )
    back_parts = [None] * 4
    for step in (0, 1, 3, 2):
        total = chunks[step][2].astype(F32) + swap_cores(chunks[step][3]).astype(F32)
        back_parts[step] = along_y(total.astype(BF16), step) if step else total
    terms = weight_terms(
        row_blocks[:1] + [after(block, chunks[2][0]) for block in row_blocks[1:]],
        grad_blocks,
        [c[0] for c in chunks],
        [c[1] for c in chunks],
    )
    feed_swap = swap_cores(jnp.concatenate([c[5] for c in chunks], axis=0))
    feed_sums = [
        chunks[step][4].astype(F32)
        + feed_swap[step * shard_rows : (step + 1) * shard_rows].astype(F32)
        for step in range(4)
    ]
    feed_sums = [feed_sums[0]] + [value.astype(BF16) for value in feed_sums[1:]]
    attended_swap = swap_cores(attended_moved[:, half:])
    *arrived, terms, attended_swap = phase(*back_parts, *feed_sums, terms, attended_swap)
    back_parts, feed_sums = arrived[:4], arrived[4:]

    terms = lax.psum_scatter(terms, SLICE_AXES, scatter_dimension=0, tiled=True)
    unit_term, down_term = unpack_slice(terms)
    units_here = down_full.shape[0]
    feed_parts = [feed_sums[0]] + [along_y(feed_sums[step], step) for step in (1, 2, 3)]
    normed_two_grad = mm_nt(add_up(back_parts).astype(BF16), slice_hot)
    mid_grad = cotangent + norm_back(middle, factor_two, gain_two, normed_two_grad)
    gain_two_rows = (normed_two_grad * middle * factor_two).astype(BF16)
    branch_grad = mid_grad.astype(BF16)
    branch_swap = swap_cores(branch_grad)
    attended_grad = jnp.concatenate(
        [mm_nt(branch_grad, out_part), mm_nt(branch_grad, out_other)], axis=1
    ).astype(BF16)
    attended_grad = mm_nt(attended_grad, hot).astype(BF16)
    query_low, pair_grads = run_kernel(
        attend_back_kernel,
        [((shard_rows, QUERY_WIDTH), BF16), ((1024, pair_cols), BF16)],
        (
            queries,
            gathered,
            attended,
            attended_grad,
            logs,
            cosine,
            sine,
            key_places,
            row_places,
        ),
        shard_rows * 1024 * QUERY_WIDTH * 10,
    )
    *feed_parts, query_low, pair_grads, mid_grad, branch_grad, branch_swap, gain_two_rows = phase(
        *feed_parts, query_low, pair_grads, mid_grad, branch_grad, branch_swap, gain_two_rows
    )

    pair_grads = lax.all_to_all(
        pair_grads.reshape(devices_ctx, shard_rows, pair_cols), ("y", "zh"), 0, 0, tiled=True
    )
    attended_both = jnp.concatenate([attended_moved[:, :half], attended_swap], axis=0)
    out_blocks = scatter(
        mm_tn(attended_both, jnp.concatenate([branch_grad, branch_swap], axis=0)), 2
    )
    query_swap = swap_cores(query_low)
    gain_two_rows = mm(gain_two_rows, hot).astype(BF16)
    feed_out = add_up(feed_parts)
    final_out = middle + feed_out
    sums = jnp.stack(
        [
            jnp.sum(row_weight * branch * branch),
            jnp.sum(row_weight * feed_out * feed_out),
            jnp.sum(row_weight * final_out * final_out),
        ]
    )
    sums = jnp.broadcast_to(jnp.pad(sums, (0, 125))[None], (8, 128))
    activations = final_out.astype(BF16)
    *out_blocks, pair_grads, query_swap, gain_two_rows, sums, activations = phase(
        *out_blocks, pair_grads, query_swap, gain_two_rows, sums, activations
    )

    normed_both = jnp.concatenate([normed[:, :half], normed_swap], axis=0)
    query_blocks = scatter(
        mm_tn(normed_both, jnp.concatenate([query_low, query_swap], axis=0)), 2
    )
    pair_grads = jnp.sum(pair_grads.astype(F32), axis=0)
    key_grad = rotate_plain(pair_grads[:, :KEY_WIDTH], key_cosine, -key_sine)
    pair_low = jnp.concatenate([key_grad, pair_grads[:, KEY_WIDTH:]], axis=1).astype(BF16)
    pair_swap = swap_cores(pair_low)

    def project_back(grads, part, other_part):
        return jnp.concatenate([mm_nt(grads, part), mm_nt(grads, other_part)], axis=1)

    normed_grad = project_back(query_low, query_part, query_other) + project_back(
        pair_low, key_part[:, :pair_cols], key_other[:, :pair_cols]
    )
    gain_one_rows = (normed_grad * tokens_moved * factor_one).astype(BF16)
    gain_swap = swap_cores(
        jnp.concatenate([gain_one_rows[:, half:], gain_two_rows[:, half:]], axis=0)
    )
    out_total = add_up(out_blocks)
    *query_blocks, pair_low, pair_swap, gain_swap, gain_one_rows, normed_grad, out_total = phase(
        *query_blocks, pair_low, pair_swap, gain_swap, gain_one_rows, normed_grad, out_total
    )

    picks = jnp.arange(GAIN_COLS) < GAIN_COLS // 2
    picks = jnp.broadcast_to(picks[None], (shard_rows, GAIN_COLS))
    picks = jnp.concatenate([picks, ~picks], axis=0).astype(BF16)
    gain_mine = jnp.concatenate([gain_one_rows[:, :half], gain_two_rows[:, :half]], axis=0)
    gain_terms = mm_tn(gain_mine, picks) + mm_tn(gain_swap, picks)
    pair_term = mm_tn(normed_both, jnp.concatenate([pair_low, pair_swap], axis=0))
    pair_blocks = scatter(jnp.concatenate([pair_term, gain_terms], axis=1), 2)
    query_total = add_up(query_blocks)
    sums_one = send(sums, lambda x, y, z, core: (x, y, z + 2, core))
    input_part = norm_back(tokens_moved, factor_one, gain_one, normed_grad)
    input_grad = (mid_grad + exact_move(input_part, hot.T)).astype(BF16)
    *pair_blocks, query_total, sums, sums_one, input_grad = phase(
        *pair_blocks, query_total, sums, sums_one, input_grad
    )

    total = jnp.concatenate([add_up(pair_blocks), query_total, out_total], axis=1)
    blocks = scatter(total, 1)
    sums = sums + sums_one
    sums_one = send(sums, lambda x, y, z, core: (x, y ^ 1, z, core))
    unit_term = lax.all_to_all(
        unit_term.reshape(8, -1, unit_term.shape[1]), ROW_AXES, 0, 0, tiled=True
    )
    down_sum = swap_half_core(down_term)
    *blocks, sums, sums_one, unit_term, down_sum = phase(
        *blocks, sums, sums_one, unit_term, down_sum
    )

    blocks = scatter(add_up(blocks), 0)
    sums = sums + sums_one
    sums = sums + send(sums, lambda x, y, z, core: (x, y ^ 2, z, core))
    seq_rms = jnp.sqrt(sums[:1, :3] / (seq_length.astype(F32) * model_width))
    unit_term = unit_term.astype(F32)
    total = add_up(blocks)
    return (
        activations,
        input_grad,
        total[:, pair_cols],
        total[:, split : split + QUERY_WIDTH],
        total[:, :KEY_WIDTH],
        total[:, KEY_WIDTH:pair_cols],
        total[:, split + QUERY_WIDTH :],
        total[:, pair_cols + GAIN_COLS - 1],
        unpack_units(unit_term[:, :, :units_here]),
        unpack_units(unit_term[:, :, units_here:]),
        down_sum[: w_down.shape[0]].astype(F32),
        seq_rms,
    )


def solution(mesh):
    fine = Mesh(mesh.devices.reshape(SIZES), AXES)
    rows = P(AXES, None)
    flat = P(AXES)
    group = ("x", "zl", "core")
    in_specs = (
        (rows, flat, rows, rows, rows, rows, flat, rows, rows, rows)
        + (P(group, None), P(group), P(group))
        + (rows,)
    )
    out_specs = (rows, rows, flat, rows, rows, rows, rows, flat, rows, rows, rows, P(group, None))
    return jax.shard_map(
        local, mesh=fine, in_specs=in_specs, out_specs=out_specs, check_vma=False
    )
```

```python
import functools

import jax
import jax.numpy as jnp
import numpy as np
from jax import lax
from jax.experimental import pallas as pl
from jax.experimental.pallas import tpu as pltpu
from jax.sharding import Mesh, PartitionSpec as P

QUERY_HEADS = 20
KEY_VALUE_HEADS = 5
HEAD_WIDTH = 64
QUERY_WIDTH = QUERY_HEADS * HEAD_WIDTH
KEY_WIDTH = KEY_VALUE_HEADS * HEAD_WIDTH
GAIN_COLS = 128
KERNEL_BYTES = 20 * 1024 * 1024
LARGE_BYTES = 58 * 1024 * 1024
FEED_BYTES = 24 * 1024 * 1024
PAD_UNITS = 32

EPSILON = 1e-05
ROPE_BASE = 10000.0
MASKED_SCORE = -1e30

AXES = ("y", "zh", "x", "zl", "core")
SIZES = (4, 2, 4, 2, 2)
ROW_AXES = ("y", "core")
SLICE_AXES = ("x", "zh", "zl")
F32 = jnp.float32
BF16 = jnp.bfloat16


def device_number(x, y, z, core):
    return (((y * 2 + z // 2) * 4 + x) * 2 + z % 2) * 2 + core


def pairs_of(move):
    pairs = []
    for y in range(4):
        for z in range(4):
            for x in range(4):
                for core in range(2):
                    tx, ty, tz, tc = move(x, y, z, core)
                    pairs.append(
                        (device_number(x, y, z, core), device_number(tx % 4, ty % 4, tz % 4, tc))
                    )
    return pairs


def send(values, move):
    return lax.ppermute(values, AXES, pairs_of(move))


def swap_cores(values):
    return send(values, lambda x, y, z, core: (x, y, z, 1 - core))


def swap_half_core(values):
    return send(values, lambda x, y, z, core: (x, y, core * 2 + z % 2, z // 2))


def stage_move(stage, distance):
    def move(x, y, z, core):
        spot = [x, y, z]
        spot[(stage + core + 1) % 3] += distance
        return (spot[0], spot[1], spot[2], core)

    return move


def spread(values, stage):
    arrived = [send(values, stage_move(stage, -distance)) for distance in (1, 2, 3)]
    return [values] + arrived


def join(blocks):
    return lax.optimization_barrier(jnp.concatenate(blocks, axis=0))


def cut(total):
    low = total.astype(BF16)
    rows = low.shape[0] // 4
    return [low[step * rows : (step + 1) * rows] for step in range(4)]


def scatter(total, stage):
    parts = total if isinstance(total, list) else cut(total)
    arrived = [send(parts[step], stage_move(stage, step)) for step in (1, 2, 3)]
    return [parts[0]] + arrived


def add_up(blocks):
    total = blocks[0].astype(F32)
    for block in blocks[1:]:
        total = total + block.astype(F32)
    return total


def phase(*values):
    return lax.optimization_barrier(values)


def along_y(values, distance):
    return send(values, lambda x, y, z, core: (x, y + distance, z, core))


def gather_rows(own):
    blocks = [own] + [along_y(own, -distance) for distance in (1, 2, 3)]
    return blocks + [swap_cores(block) for block in blocks]


def add_cores(own, other):
    return [(a.astype(F32) + swap_cores(b).astype(F32)) for a, b in zip(own, other)]


def reduce_blocks(sums):
    total = sums[0]
    for distance in (1, 2, 3):
        total = total + along_y(sums[distance].astype(BF16), distance).astype(F32)
    return total


def after(values, *earlier):
    return lax.optimization_barrier((values,) + earlier)[0]


def row_order(place, core):
    third, second, first, inner = jnp.meshgrid(
        jnp.arange(4), jnp.arange(4), jnp.arange(4), jnp.arange(10), indexing="ij"
    )
    spot = list(place)
    for stage, step in enumerate((first, second, third)):
        axis = (stage + core + 1) % 3
        spot[axis] = spot[axis] + step
    sx, sy, sz = spot
    numbers = device_number(sx % 4, sy % 4, sz % 4, core) * 10 + inner
    return numbers.reshape(-1).astype(jnp.int32)


def slice_order():
    x, zh, zl, y, core, inner = np.meshgrid(
        *(np.arange(n) for n in (4, 2, 2, 4, 2, 10)), indexing="ij"
    )
    return (device_number(x, y, zh * 2 + zl, core) * 10 + inner).reshape(-1).astype(np.int32)


def one_hot(order):
    return (jnp.arange(order.shape[0], dtype=jnp.int32)[:, None] == order[None, :]).astype(BF16)


def exact_move(values, hot):
    high = values.astype(BF16)
    low = (values - high.astype(F32)).astype(BF16)
    return mm(high, hot) + mm(low, hot)


def mm(left, right):
    return jnp.dot(left, right, preferred_element_type=F32)


def mm_nt(left, right):
    return lax.dot_general(left, right, (((1,), (1,)), ((), ())), preferred_element_type=F32)


def mm_tn(left, right):
    return lax.dot_general(left, right, (((0,), (0,)), ((), ())), preferred_element_type=F32)


def norm_factor(values):
    return lax.rsqrt(jnp.mean(values * values, axis=-1, keepdims=True) + EPSILON)


def norm_back(values, factor, gain, grad):
    weighted = gain * grad
    inner = jnp.mean(weighted * values, axis=-1, keepdims=True)
    return factor * weighted - values * (factor * factor * factor) * inner


def rope_tables(angles_at):
    half_size = HEAD_WIDTH // 2
    powers = jnp.arange(half_size, dtype=F32) * (2.0 / HEAD_WIDTH)
    speeds = jnp.power(ROPE_BASE, -powers)
    angles = angles_at[:, None] * speeds[None, :]
    cosine, sine = jnp.cos(angles), jnp.sin(angles)
    return (jnp.concatenate([cosine] * 4, axis=1), jnp.concatenate([-sine, sine] * 2, axis=1))


def rotate_pairs(values, cosine, sine):
    width = values.shape[1]
    half_size = HEAD_WIDTH // 2
    lanes = lax.broadcasted_iota(jnp.int32, values.shape, 1) % HEAD_WIDTH
    ahead = pltpu.roll(values, width - half_size, 1)
    behind = pltpu.roll(values, half_size, 1)
    return values * cosine + jnp.where(lanes < half_size, ahead, behind) * sine


def wide_table(table, width):
    return jnp.concatenate([table] * (width // table.shape[1]), axis=1)


def low_high(rows):
    low = [rows[at : at + 64] for at in range(0, rows.shape[0], 128)]
    high = [rows[at + 64 : at + 128] for at in range(0, rows.shape[0], 128)]
    return jnp.concatenate(low, axis=0), jnp.concatenate(high, axis=0)


def stack_heads(rows, head):
    pieces = [
        rows[at : at + 64, (4 * head + step) * HEAD_WIDTH : (4 * head + step + 1) * HEAD_WIDTH]
        for at in (0, 64)
        for step in range(4)
    ]
    return jnp.concatenate(pieces, axis=0)


def unstack_heads(stack):
    halves = [
        jnp.concatenate([stack[at + 64 * step : at + 64 * step + 64] for step in range(4)], axis=1)
        for at in (0, 256)
    ]
    return jnp.concatenate(halves, axis=0)


def mask_bias(keys_ref, rows_ref):
    columns = keys_ref[...].T
    keys_low, keys_high = columns[:512], columns[512:]

    def bias(keys, lanes):
        seen = (keys[:, 0:1] <= rows_ref[0:1, lanes]) | (keys[:, 1:2] == rows_ref[1:2, lanes])
        return jnp.where(seen, 0.0, MASKED_SCORE).astype(F32)

    return bias(keys_low, slice(0, 512)), bias(keys_high, slice(256, 512))


def attend_kernel(q_ref, part_ref, kv_ref, cos_ref, sin_ref, keys_ref, rows_ref, out_ref, turned_ref, log_ref):
    cosine = wide_table(cos_ref[...], QUERY_WIDTH)
    sine = wide_table(sin_ref[...], QUERY_WIDTH)
    queries = q_ref[...] + part_ref[...].astype(F32)
    queries = (rotate_pairs(queries, cosine, sine) * HEAD_WIDTH**-0.5).astype(BF16)
    turned_ref[...] = queries
    kv_low, kv_high = low_high(kv_ref[...])
    bias_low, bias_high = mask_bias(keys_ref, rows_ref)
    for head in range(KEY_VALUE_HEADS):
        at = slice(head * HEAD_WIDTH, (head + 1) * HEAD_WIDTH)
        vat = slice(KEY_WIDTH + head * HEAD_WIDTH, KEY_WIDTH + (head + 1) * HEAD_WIDTH)
        stack = stack_heads(queries, head)
        score_low = mm_nt(kv_low[:, at], stack) + bias_low
        score_high = mm_nt(kv_high[:, at], stack[256:]) + bias_high
        top_low = jnp.max(score_low, axis=0, keepdims=True)
        top_high = jnp.max(score_high, axis=0, keepdims=True)
        top = jnp.concatenate(
            [top_low[:, :256], jnp.maximum(top_low[:, 256:], top_high)], axis=1
        )
        exp_low = jnp.exp(score_low - top)
        exp_high = jnp.exp(score_high - top[:, 256:])
        total = jnp.sum(exp_low, axis=0, keepdims=True)
        total_high = jnp.sum(exp_high, axis=0, keepdims=True)
        total = jnp.concatenate([total[:, :256], total[:, 256:] + total_high], axis=1)
        result = mm_tn(kv_low[:, vat], exp_low.astype(BF16))
        result_high = mm_tn(kv_high[:, vat], exp_high.astype(BF16))
        result = jnp.concatenate([result[:, :256], result[:, 256:] + result_high], axis=1)
        result = (result / total).T
        out_ref[:, head * 256 : (head + 1) * 256] = unstack_heads(result).astype(BF16)
        log_ref[head : head + 1, :] = top + jnp.log(total)


def attend_back_kernel(
    q_ref, kv_ref, out_ref, grad_ref, log_ref, cos_ref, sin_ref, keys_ref, rows_ref, dq_ref, dkv_ref
):
    kv_low, kv_high = low_high(kv_ref[...])
    bias_low, bias_high = mask_bias(keys_ref, rows_ref)
    queries = q_ref[...]
    outs = out_ref[...]
    grads = grad_ref[...]
    ones = jnp.ones((8, HEAD_WIDTH), F32)
    dq_parts, dk_low, dk_high, dv_low, dv_high = [], [], [], [], []
    for head in range(KEY_VALUE_HEADS):
        at = slice(head * HEAD_WIDTH, (head + 1) * HEAD_WIDTH)
        vat = slice(KEY_WIDTH + head * HEAD_WIDTH, KEY_WIDTH + (head + 1) * HEAD_WIDTH)
        stack = stack_heads(queries, head)
        grad = stack_heads(grads, head)
        product = grad.astype(F32) * stack_heads(outs, head).astype(F32)
        delta = lax.dot_general(
            ones,
            product,
            (((1,), (1,)), ((), ())),
            preferred_element_type=F32,
            precision=lax.Precision.HIGHEST,
        )[0:1]
        logs = log_ref[head : head + 1, :]
        key_low, key_high = kv_low[:, at], kv_high[:, at]
        probs_low = jnp.exp(mm_nt(key_low, stack) + bias_low - logs)
        probs_high = jnp.exp(mm_nt(key_high, stack[256:]) + bias_high - logs[:, 256:])
        back_low = mm_nt(kv_low[:, vat], grad)
        back_high = mm_nt(kv_high[:, vat], grad[256:])
        score_low = (probs_low * (back_low - delta)).astype(BF16)
        score_high = (probs_high * (back_high - delta[:, 256:])).astype(BF16)
        dv_low.append(mm(probs_low.astype(BF16), grad))
        dv_high.append(mm(probs_high.astype(BF16), grad[256:]))
        dk_low.append(mm(score_low, stack))
        dk_high.append(mm(score_high, stack[256:]))
        dq = mm_tn(key_low, score_low)
        dq_high = mm_tn(key_high, score_high)
        dq = jnp.concatenate([dq[:, :256], dq[:, 256:] + dq_high], axis=1)
        dq_parts.append(unstack_heads((dq * HEAD_WIDTH**-0.5).T))
    cosine = wide_table(cos_ref[...], QUERY_WIDTH)
    sine = wide_table(sin_ref[...], QUERY_WIDTH)
    dq_ref[...] = rotate_pairs(jnp.concatenate(dq_parts, axis=1), cosine, -sine).astype(BF16)
    low = jnp.concatenate(dk_low + dv_low, axis=1).astype(BF16)
    high = jnp.concatenate(dk_high + dv_high, axis=1).astype(BF16)
    for at in range(8):
        dkv_ref[128 * at : 128 * at + 64] = low[64 * at : 64 * at + 64]
        dkv_ref[128 * at + 64 : 128 * at + 128] = high[64 * at : 64 * at + 64]


def run_kernel(kernel, shapes, operands, flops, limit=KERNEL_BYTES):
    return pl.pallas_call(
        kernel,
        out_shape=[jax.ShapeDtypeStruct(shape, kind) for shape, kind in shapes],
        in_specs=[pl.BlockSpec(memory_space=pltpu.VMEM)] * len(operands),
        out_specs=[pl.BlockSpec(memory_space=pltpu.VMEM)] * len(shapes),
        compiler_params=pltpu.CompilerParams(vmem_limit_bytes=limit),
        cost_estimate=pl.CostEstimate(
            flops=flops,
            bytes_accessed=sum(v.size * v.dtype.itemsize for v in operands),
            transcendentals=0,
        ),
    )(*operands)


def pair_kernel(
    moved_ref,
    factor_ref,
    part_ref,
    other_ref,
    cos_ref,
    sin_ref,
    pairs_ref,
    normed_ref,
    halves_ref,
    gains_ref,
):
    half = part_ref.shape[0]
    pair_cols = 2 * KEY_WIDTH
    gains = [ref[:, pair_cols:].astype(F32).T[:8] for ref in (part_ref, other_ref)]
    gains = jnp.concatenate(gains, axis=1)
    gains_ref[...] = gains
    scaled = moved_ref[...] * factor_ref[...]
    normed = (scaled * gains[0:1]).astype(BF16)
    normed_ref[...] = normed
    halves_ref[0:128] = normed[:, half:]
    halves_ref[128:256] = scaled[:, half:].astype(BF16)
    both = mm(normed[:, :half], part_ref[:, :pair_cols]) + mm(
        normed[:, half:], other_ref[:, :pair_cols]
    )
    wide = 3 * cos_ref.shape[1]
    turned = rotate_pairs(
        both[:, :wide], wide_table(cos_ref[...], wide), wide_table(sin_ref[...], wide)
    )
    pairs = jnp.concatenate([turned[:, :KEY_WIDTH], both[:, KEY_WIDTH:]], axis=1).astype(BF16)
    for at in range(8):
        pairs_ref[at] = pairs


def pair_back_kernel(parts_ref, cos_ref, sin_ref, low_ref):
    total = parts_ref[0].astype(F32)
    for at in range(1, 8):
        total = total + parts_ref[at].astype(F32)
    wide = 3 * cos_ref.shape[1]
    turned = rotate_pairs(
        total[:, :wide], wide_table(cos_ref[...], wide), -wide_table(sin_ref[...], wide)
    )
    low_ref[...] = jnp.concatenate(
        [turned[:, :KEY_WIDTH], total[:, KEY_WIDTH:]], axis=1
    ).astype(BF16)


def middle_kernel(
    back_a,
    back_b,
    back_c,
    back_d,
    cot_ref,
    middle_ref,
    factor_ref,
    gain_ref,
    hot_slice_ref,
    part_ref,
    other_ref,
    hot_ref,
    mid_ref,
    branch_ref,
    gains_ref,
    grad_ref,
    hot_slice,
    parts,
    hot,
    sems,
):
    half = part_ref.shape[0]
    copies = [
        pltpu.make_async_copy(hot_slice_ref, hot_slice, sems.at[0]),
        pltpu.make_async_copy(part_ref, parts.at[0:half], sems.at[1]),
        pltpu.make_async_copy(other_ref, parts.at[half : 2 * half], sems.at[2]),
        pltpu.make_async_copy(hot_ref, hot, sems.at[3]),
    ]
    for copy in copies:
        copy.start()
    total = back_a[...] + back_b[...].astype(F32) + back_c[...].astype(F32)
    total = (total + back_d[...].astype(F32)).astype(BF16)
    copies[0].wait()
    grad = mm_nt(total, hot_slice[...])
    middle, factor = middle_ref[...], factor_ref[...]
    mid = cot_ref[...] + norm_back(middle, factor, gain_ref[...], grad)
    mid_ref[...] = mid
    branch = mid.astype(BF16)
    branch_ref[...] = branch
    gains_ref[...] = (grad * middle * factor).astype(BF16)
    copies[1].wait()
    copies[2].wait()
    moved = mm_nt(branch, parts[...]).astype(BF16)
    copies[3].wait()
    grad_ref[...] = mm_nt(moved, hot[...]).astype(BF16)


def middle_call(small, large):
    vmem, hbm = pl.BlockSpec(memory_space=pltpu.VMEM), pl.BlockSpec(memory_space=pltpu.HBM)
    rows, width = small[0].shape
    square = pltpu.VMEM((width, width), BF16)
    return pl.pallas_call(
        middle_kernel,
        out_shape=[jax.ShapeDtypeStruct((rows, width), kind) for kind in (F32, BF16, BF16, BF16)],
        in_specs=[vmem] * len(small) + [hbm] * len(large),
        out_specs=[vmem] * 4,
        scratch_shapes=[square, square, square, pltpu.SemaphoreType.DMA((4,))],
        compiler_params=pltpu.CompilerParams(vmem_limit_bytes=LARGE_BYTES),
        cost_estimate=pl.CostEstimate(
            flops=6 * rows * width * width, bytes_accessed=16 * 2**20, transcendentals=0
        ),
    )(*small, *large)


def finish_kernel(
    feed_a, feed_b, feed_c, feed_d, middle_ref, branch_ref, weight_ref, out_ref, sums_ref
):
    feed = feed_a[...] + feed_b[...].astype(F32) + feed_c[...].astype(F32)
    feed = feed + feed_d[...].astype(F32)
    final = middle_ref[...] + feed
    out_ref[...] = final.astype(BF16)
    sums_ref[...] = jnp.zeros(sums_ref.shape, F32)
    for row, values in enumerate((branch_ref[...], feed, final)):
        part = jnp.sum(weight_ref[...] * values * values, axis=0, keepdims=True)
        part = jnp.sum(part, axis=1, keepdims=True)
        sums_ref[row : row + 1] = jnp.broadcast_to(part, (1, 128))


def query_kernel(
    normed_ref,
    halves_ref,
    a_ref,
    b_ref,
    c_ref,
    d_ref,
    own_ref,
    other_ref,
    both_ref,
    query_ref,
    out_ref,
    sems,
):
    width, count = query_ref.shape[1], a_ref.shape[0]
    copies = []
    for step, block in enumerate((a_ref, b_ref, c_ref, d_ref)):
        at = slice(step * count, (step + 1) * count)
        copies.append(
            pltpu.make_async_copy(block.at[:, 0:width], query_ref.at[at], sems.at[step])
        )
    for step, block in enumerate((a_ref, b_ref, c_ref, d_ref)):
        at = slice(step * count, (step + 1) * count)
        copies.append(
            pltpu.make_async_copy(
                block.at[:, width : 2 * width], out_ref.at[at], sems.at[4 + step]
            )
        )
    for copy in copies:
        copy.start()
    for copy in copies[:4]:
        copy.wait()
    half = own_ref.shape[0]
    both_ref[0:half] = normed_ref[:, : both_ref.shape[1]]
    both_ref[half : 2 * half] = halves_ref[0:half]
    both = mm(both_ref[...], query_ref[...])
    own_ref[...] = both[:half]
    other_ref[...] = both[half:].astype(BF16)
    for copy in copies[4:]:
        copy.wait()


def query_parts(normed, halves, blocks):
    vmem = pl.BlockSpec(memory_space=pltpu.VMEM)
    half, width = normed.shape[0], QUERY_WIDTH
    joined = jax.ShapeDtypeStruct((4 * blocks[0].shape[0], width), BF16)
    return pl.pallas_call(
        query_kernel,
        out_shape=[
            jax.ShapeDtypeStruct((half, width), F32),
            jax.ShapeDtypeStruct((half, width), BF16),
            jax.ShapeDtypeStruct(halves.shape, BF16),
            joined,
            joined,
        ],
        in_specs=[vmem] * 2 + [pl.BlockSpec(memory_space=pltpu.HBM)] * 4,
        out_specs=[vmem] * 5,
        scratch_shapes=[pltpu.SemaphoreType.DMA((8,))],
        compiler_params=pltpu.CompilerParams(vmem_limit_bytes=LARGE_BYTES),
        cost_estimate=pl.CostEstimate(
            flops=2 * halves.size * width, bytes_accessed=10 * 2**20, transcendentals=0
        ),
    )(normed, halves, *blocks)


def unpack_kernel(slices_ref, units_ref, down_ref, held, units, down, sems):
    copy = pltpu.make_async_copy(slices_ref, held, sems.at[0])
    copy.start()
    copy.wait()
    for block in range(16):
        base = block * 128
        units[block * 80 : block * 80 + 80] = held[base : base + 80]
    moves = [pltpu.make_async_copy(units, units_ref, sems.at[1])]
    moves[0].start()
    for block in range(16):
        base, at = block * 128, block * 32
        down[at : at + 32, :1024] = held[base + 80 : base + 112]
        down[at : at + 16, 1024:] = held[base + 112 : base + 128, :256]
        down[at + 16 : at + 32, 1024:] = held[base + 112 : base + 128, 256:512]
    moves.append(pltpu.make_async_copy(down, down_ref, sems.at[2]))
    moves[1].start()
    for move in moves:
        move.wait()


def unpack_slices(slices):
    hbm = pl.BlockSpec(memory_space=pltpu.HBM)
    shapes = [(1280, 1024), (512, 1280)]
    return pl.pallas_call(
        unpack_kernel,
        out_shape=[jax.ShapeDtypeStruct(shape, BF16) for shape in shapes],
        in_specs=[hbm],
        out_specs=[hbm] * 2,
        scratch_shapes=[pltpu.VMEM(shape, BF16) for shape in [slices.shape] + shapes]
        + [pltpu.SemaphoreType.DMA((3,))],
        compiler_params=pltpu.CompilerParams(vmem_limit_bytes=LARGE_BYTES),
        cost_estimate=pl.CostEstimate(
            flops=0, bytes_accessed=4 * slices.size, transcendentals=0
        ),
    )(slices)


def feed_kernel(
    xa_ref,
    xb_ref,
    all_grads_ref,
    places_ref,
    units_ref,
    down_ref,
    hidden_ref,
    unit_ref,
    back_a_ref,
    back_b_ref,
    out_a_ref,
    out_b_ref,
    rows_ref,
    grads_ref,
    sems,
    *,
    step,
):
    half = xa_ref.shape[0]
    low = slice(0, half)
    high = slice(half, 2 * half)
    spot_a = pl.ds(pl.multiple_of(places_ref[step], half), half)
    spot_b = pl.ds(pl.multiple_of(places_ref[step + 4], half), half)
    copies = [
        pltpu.make_async_copy(xa_ref, rows_ref.at[low], sems.at[0]),
        pltpu.make_async_copy(xb_ref, rows_ref.at[high], sems.at[1]),
    ]
    copies += [
        pltpu.make_async_copy(all_grads_ref.at[spot_a], grads_ref.at[low], sems.at[2]),
        pltpu.make_async_copy(all_grads_ref.at[spot_b], grads_ref.at[high], sems.at[3]),
    ]
    for copy in copies:
        copy.start()
    copies[0].wait()
    copies[1].wait()
    units = units_ref.shape[1] // 2
    both = mm(rows_ref[...], units_ref[...])
    gate, up = both[:, :units], both[:, units:]
    sigmoid = 1.0 / (1.0 + jnp.exp(-gate))
    silu = gate * sigmoid
    hidden = (silu * up).astype(BF16)
    hidden_ref[...] = hidden
    for copy in copies[2:]:
        copy.wait()
    hidden_grad = mm_nt(grads_ref[...], down_ref[...])
    gate_low = (hidden_grad * up * sigmoid * (1.0 + gate * (1.0 - sigmoid))).astype(BF16)
    up_low = (hidden_grad * silu).astype(BF16)
    unit = jnp.concatenate([gate_low, up_low], axis=1)
    unit_ref[...] = unit
    back = mm_nt(unit, units_ref[...]).astype(BF16)
    back_a_ref[...] = back[:half]
    back_b_ref[...] = back[half:]
    outs = mm(hidden, down_ref[...]).astype(BF16)
    out_a_ref[...] = outs[:half]
    out_b_ref[...] = outs[half:]


def feed_chunk(step, rows_a, rows_b, all_grads, places, units, down):
    count, width = rows_a.shape[0] * 2, rows_a.shape[1]
    vmem = pl.BlockSpec(memory_space=pltpu.VMEM)
    hbm = pl.BlockSpec(memory_space=pltpu.HBM)
    shapes = [(count, 512), (count, 1024)] + [rows_a.shape] * 4
    return pl.pallas_call(
        functools.partial(feed_kernel, step=step),
        out_shape=[jax.ShapeDtypeStruct(shape, BF16) for shape in shapes],
        in_specs=[hbm] * 3 + [pl.BlockSpec(memory_space=pltpu.SMEM)] + [vmem] * 2,
        out_specs=[vmem] * 6,
        scratch_shapes=[
            pltpu.VMEM((count, width), BF16),
            pltpu.VMEM((count, width), BF16),
            pltpu.SemaphoreType.DMA((4,)),
        ],
        compiler_params=pltpu.CompilerParams(vmem_limit_bytes=FEED_BYTES),
        cost_estimate=pl.CostEstimate(
            flops=2 * count * width * 3 * 1024,
            bytes_accessed=2 * (units.size + down.size + 4 * rows_a.size),
            transcendentals=0,
        ),
    )(rows_a, rows_b, all_grads, places, units, down)


def weight_kernel(*refs):
    sources, all_grads, places, term_out = refs[:16], refs[16], refs[17], refs[18]
    rows, unit, grads, hidden, terms = refs[19:24]
    in_sems, out_sems = refs[24:]
    copies, late = [], []
    for step in range(4):
        base = step * 256
        low, high, both = slice(base, base + 128), slice(base + 128, base + 256), slice(
            base, base + 256
        )
        spot_a = pl.ds(pl.multiple_of(places[step], 128), 128)
        spot_b = pl.ds(pl.multiple_of(places[step + 4], 128), 128)
        for pieces, source, target in (
            (copies, sources[step], rows.at[low]),
            (copies, sources[step + 4], rows.at[high]),
            (copies, sources[step + 12], unit.at[both]),
            (late, all_grads.at[spot_a], grads.at[low]),
            (late, all_grads.at[spot_b], grads.at[high]),
            (late, sources[step + 8], hidden.at[both]),
        ):
            sem = in_sems.at[len(copies) + len(late)]
            pieces.append(pltpu.make_async_copy(source, target, sem))
    for copy in copies + late:
        copy.start()
    for copy in copies:
        copy.wait()
    for at in range(0, 16, 4):
        total = mm_tn(rows[:, at * 80 : at * 80 + 320], unit[...]).astype(BF16)
        for step in range(4):
            base = (at + step) * 128
            terms[base : base + 80] = total[step * 80 : step * 80 + 80]
    for copy in late:
        copy.wait()
    moves = []
    for at in range(0, 16, 4):
        total = mm_tn(hidden[:, at * 32 : at * 32 + 128], grads[...]).astype(BF16)
        for step in range(4):
            rows_here = total[step * 32 : step * 32 + 32]
            base = (at + step) * 128
            terms[base + 80 : base + 112] = rows_here[:, :1024]
            terms[base + 112 : base + 128, 0:256] = rows_here[:16, 1024:]
            terms[base + 112 : base + 128, 256:512] = rows_here[16:, 1024:]
            terms[base + 112 : base + 128, 512:] = jnp.zeros((16, 512), BF16)
        piece = slice(at * 128, at * 128 + 512)
        moves.append(
            pltpu.make_async_copy(terms.at[piece], term_out.at[piece], out_sems.at[at // 4])
        )
        moves[-1].start()
    for move in moves:
        move.wait()


def weight_terms(rows, all_grads, places, chunks):
    sources = list(rows)
    for part in (0, 1):
        sources += [chunk[part] for chunk in chunks]
    hidden, unit = chunks[0][0], chunks[0][1]
    count, width = 8 * rows[0].shape[0], rows[0].shape[1]
    smem, hbm = pl.BlockSpec(memory_space=pltpu.SMEM), pl.BlockSpec(memory_space=pltpu.HBM)
    return pl.pallas_call(
        weight_kernel,
        out_shape=jax.ShapeDtypeStruct((2048, 1024), BF16),
        in_specs=[pl.BlockSpec(memory_space=pl.ANY)] * 16 + [hbm, smem],
        out_specs=hbm,
        scratch_shapes=[
            pltpu.VMEM((count, width), BF16),
            pltpu.VMEM((count, unit.shape[1]), BF16),
            pltpu.VMEM((count, width), BF16),
            pltpu.VMEM((count, hidden.shape[1]), BF16),
            pltpu.VMEM((2048, 1024), BF16),
            pltpu.SemaphoreType.DMA((24,)),
            pltpu.SemaphoreType.DMA((4,)),
        ],
        compiler_params=pltpu.CompilerParams(vmem_limit_bytes=24 * 1024 * 1024),
        cost_estimate=pl.CostEstimate(
            flops=2 * count * 1280 * 1536, bytes_accessed=2**20, transcendentals=0
        ),
    )(*sources, all_grads, places)


def term_kernel(normed_ref, q_ref, qs_ref, attended_ref, as_ref, b_ref, bs_ref, *outs):
    count = outs[0].shape[0]
    half = normed_ref.shape[1]
    queries = jnp.concatenate([q_ref[...], qs_ref[...]], axis=0)
    outs[4][...] = queries
    branch = jnp.concatenate([b_ref[...], bs_ref[...]], axis=0)
    attended = jnp.concatenate([attended_ref[:, :half], as_ref[...]], axis=0)
    query_term = mm_tn(normed_ref[...], queries).astype(BF16)
    out_term = mm_tn(attended, branch).astype(BF16)
    for step in range(4):
        at = slice(step * count, (step + 1) * count)
        outs[step][:, :QUERY_WIDTH] = query_term[at]
        outs[step][:, QUERY_WIDTH:] = out_term[at]


def pack_slice(units, down):
    rest = jnp.concatenate([down[:16, 1024:], down[16:, 1024:]], axis=1)
    rest = jnp.pad(rest, ((0, 0), (0, 512)))
    return jnp.concatenate([units, down[:, :1024], rest], axis=0)


def unpack_slice(rows):
    rest = jnp.concatenate([rows[112:, :256], rows[112:, 256:512]], axis=0)
    return rows[:80], jnp.concatenate([rows[80:112], rest], axis=1)


def group_places(pair_row, devices_ctx, block_size):
    slots = jnp.arange(devices_ctx * 2 * block_size, dtype=jnp.int32)
    owners = slots // (2 * block_size)
    inside = slots % (2 * block_size)
    columns = jnp.arange(devices_ctx, dtype=jnp.int32)
    paired = jnp.sum(jnp.where(owners[:, None] == columns[None, :], pair_row[None, :], 0), axis=1)
    blocks = jnp.where(inside < block_size, paired, 2 * devices_ctx - 1 - paired)
    return blocks * block_size + inside % block_size


def pack_units(weight):
    rows = weight.shape[0]
    runs = weight.reshape(rows, 8, 4, 2, 2, 28).transpose(1, 0, 2, 4, 3, 5)
    runs = jnp.pad(runs, ((0, 0),) * 5 + ((0, PAD_UNITS - 28),))
    return runs.reshape(8, rows, 16 * PAD_UNITS)


def unpack_units(packed):
    rows = packed.shape[1]
    runs = packed.reshape(8, rows, 4, 2, 2, PAD_UNITS)[..., :28]
    return runs.transpose(1, 0, 2, 4, 3, 5).reshape(rows, 8 * 16 * 28)


def local(
    tokens,
    norm_gain,
    w_query,
    w_key,
    w_value,
    w_out,
    mlp_gain,
    w_gate,
    w_up,
    w_down,
    block_pair,
    seq_len,
    seq_start,
    out_grad,
):
    shard_rows, model_width = tokens.shape
    block_size = shard_rows // 2
    half = model_width // 2
    devices_ctx = 8
    at_y, at_zh, at_x, at_zl, at_core = (lax.axis_index(name) for name in AXES)
    place = (at_x, at_y, at_zh * 2 + at_zl)
    position = at_y * 2 + at_zh
    pair_cols = 2 * KEY_WIDTH
    split = pair_cols + GAIN_COLS

    gains = jnp.stack([norm_gain, mlp_gain], axis=1)
    gains = jnp.pad(gains, ((0, 0), (0, GAIN_COLS - 2)))
    front = spread(jnp.concatenate([w_key, w_value, gains, w_query, w_out], axis=1), 0)
    units = jnp.concatenate([pack_units(w_gate), pack_units(w_up)], axis=2)
    down_rows = jnp.pad(w_down, ((0, PAD_UNITS - w_down.shape[0]), (0, 0)))

    places_all = group_places(block_pair[0], devices_ctx, block_size)
    places_here = lax.dynamic_slice_in_dim(places_all, position * shard_rows, shard_rows)
    first_slot = seq_start[0]
    seq_length = seq_len[0]
    valid_all = (places_all >= first_slot) & (places_all < first_slot + seq_length)
    valid_here = (places_here >= first_slot) & (places_here < first_slot + seq_length)
    key_places = jnp.stack([jnp.where(valid_all, places_all, 1 << 20), places_all])
    key_places = jnp.concatenate(
        [key_places[:, at : at + 64] for side in (0, 64) for at in range(side, 1024, 128)], axis=1
    )
    key_places = jnp.pad(key_places, ((0, 6), (0, 0)))
    row_places = jnp.stack([jnp.where(valid_here, places_here, -1), places_here])
    row_places = jnp.concatenate([row_places[:, :64]] * 4 + [row_places[:, 64:]] * 4, axis=1)
    cosine, sine = rope_tables((places_here - first_slot).astype(F32))
    row_weight = valid_here.astype(F32)[:, None]

    cotangent = out_grad.astype(F32) * row_weight
    feed_grad = cotangent.astype(BF16)
    grad_rows = lax.all_gather(feed_grad, ROW_AXES, axis=0, tiled=True)

    (
        *arrived,
        units,
        down_rows,
        cosine,
        sine,
        key_places,
        row_places,
        tokens,
    ) = phase(
        *front,
        units,
        down_rows,
        cosine,
        sine,
        key_places,
        row_places,
        tokens,
    )

    front = spread(join(arrived), 1)
    units = lax.all_to_all(units, ROW_AXES, 0, 0, tiled=True)
    down_rows = swap_half_core(down_rows)
    inputs = tokens.astype(F32)
    factor_one = norm_factor(inputs)
    *arrived, units, down_rows, factor_one, order_seed = phase(
        *front, units, down_rows, factor_one, at_core
    )

    slices = pack_slice(units.reshape(-1, units.shape[2]), down_rows)
    slices = lax.all_gather(after(slices, grad_rows), SLICE_AXES, axis=0, tiled=True)
    key_part = spread(join([block[:, :split] for block in arrived]), 2)
    rest = join([block[:, split:] for block in arrived])
    orders = [row_order(place, core) for core in (0, 1)]
    mine = jnp.where(order_seed == 0, orders[0], orders[1])
    other = jnp.where(order_seed == 0, orders[1], orders[0])
    hot = one_hot(jnp.concatenate([mine, other]))
    tokens_moved = mm(tokens, hot)
    *key_part, rest, hot, tokens_moved, order_seed = phase(
        *key_part, rest, hot, tokens_moved, order_seed
    )

    rest_part = spread(rest, 2)
    key_part = join(key_part)
    key_part, key_other = phase(key_part, swap_cores(key_part))

    pairs, normed, halves, gain_rows = run_kernel(
        pair_kernel,
        [
            ((devices_ctx, shard_rows, pair_cols), BF16),
            ((shard_rows, model_width), BF16),
            ((2 * shard_rows, half), BF16),
            ((8, model_width), F32),
        ],
        (tokens_moved, factor_one, key_part, key_other, cosine, sine),
        2 * shard_rows * model_width * pair_cols,
        LARGE_BYTES,
    )
    gain_one = gain_rows[0:1]

    def project(rows, part, other_part):
        return mm(rows[:, :half], part) + mm(rows[:, half:], other_part)

    gathered = lax.all_to_all(pairs, ("y", "zh"), 0, 0, tiled=True)
    gathered = gathered.reshape(devices_ctx * shard_rows, pair_cols)
    halves = swap_cores(halves)
    gain_two = mm_nt(gain_rows.astype(BF16), hot)[1:2]
    slice_hot = one_hot(after(jnp.asarray(slice_order()), order_seed))
    grad_places = jnp.stack(
        [
            ((at_y + step) % 4 * 2 + (at_core + side) % 2) * shard_rows
            for side in (0, 1)
            for step in range(4)
        ]
    ).astype(jnp.int32)
    *rest_part, gathered, gain_two, halves, slice_hot, grad_places, cotangent, row_weight = phase(
        *rest_part, gathered, gain_two, halves, slice_hot, grad_places, cotangent, row_weight
    )

    query_own, query_other, normed_both, query_part, out_part = query_parts(
        normed, halves, rest_part
    )
    query_other = swap_cores(query_other)
    out_other = swap_cores(out_part)
    attended, queries, logs = run_kernel(
        attend_kernel,
        [((shard_rows, QUERY_WIDTH), BF16), ((shard_rows, QUERY_WIDTH), BF16), ((8, 512), F32)],
        (query_own, query_other, gathered, cosine, sine, key_places, row_places),
        shard_rows * 1024 * QUERY_WIDTH * 4,
        LARGE_BYTES,
    )
    attended_moved = mm(attended, hot).astype(BF16)
    branch = project(attended_moved, out_part, out_other)
    middle = inputs + branch
    factor_two = norm_factor(middle)
    normed_two = (middle * factor_two * gain_two).astype(BF16)
    normed_two = mm(normed_two, slice_hot).astype(BF16)
    normed_two, middle, factor_two, branch = phase(normed_two, middle, factor_two, branch)

    row_blocks = [normed_two] + [along_y(normed_two, -distance) for distance in (1, 2, 3)]
    row_blocks = row_blocks + [swap_cores(normed_two), None, None, None]
    units_full, down_full = unpack_slices(slices)
    chunks = [None] * 4
    back_parts, ready = [None] * 4, [None] * 4
    for step in (0, 1, 3, 2):
        if step:
            row_blocks[step] = after(row_blocks[step], chunks[0][0])
            row_blocks[step + 4] = swap_cores(row_blocks[step])
        block = after(row_blocks[step], ready[1]) if step == 2 else row_blocks[step]
        chunks[step] = feed_chunk(
            step,
            block,
            row_blocks[step + 4],
            grad_rows,
            grad_places,
            units_full,
            down_full,
        )
        total = chunks[step][2].astype(F32) + swap_cores(chunks[step][3]).astype(F32)
        ready[step] = total.astype(BF16) if step else total
        back_parts[step] = along_y(ready[step], step) if step else total
    terms = weight_terms(
        row_blocks[:1] + [after(block, *ready) for block in row_blocks[1:]],
        grad_rows,
        grad_places,
        chunks,
    )
    feed_swap = jnp.concatenate([after(c[5], *ready) for c in chunks], axis=0)
    feed_swap = swap_cores(feed_swap)
    feed_sums = [
        chunks[step][4].astype(F32)
        + feed_swap[step * shard_rows : (step + 1) * shard_rows].astype(F32)
        for step in range(4)
    ]
    feed_sums = [feed_sums[0]] + [value.astype(BF16) for value in feed_sums[1:]]
    attended_swap = swap_cores(attended_moved[:, half:])
    *arrived, attended_swap, terms = phase(*back_parts, *feed_sums, attended_swap, terms)
    back_parts, feed_sums = arrived[:4], arrived[4:]
    terms = lax.psum_scatter(terms, "x", scatter_dimension=0, tiled=True)

    units_here = 16 * PAD_UNITS
    feed_parts = [feed_sums[0]] + [along_y(feed_sums[step], step) for step in (1, 2, 3)]
    mid_grad, branch_grad, gain_two_rows, attended_grad = middle_call(
        (*back_parts, cotangent, middle, factor_two, gain_two),
        (slice_hot, out_part, out_other, hot),
    )
    branch_swap = swap_cores(branch_grad)
    query_low, pair_grads = run_kernel(
        attend_back_kernel,
        [((shard_rows, QUERY_WIDTH), BF16), ((1024, pair_cols), BF16)],
        (
            queries,
            gathered,
            attended,
            attended_grad,
            logs,
            cosine,
            sine,
            key_places,
            row_places,
        ),
        shard_rows * 1024 * QUERY_WIDTH * 10,
        LARGE_BYTES,
    )
    *feed_parts, query_low, pair_grads, mid_grad, branch_grad, branch_swap, gain_two_rows = phase(
        *feed_parts, query_low, pair_grads, mid_grad, branch_grad, branch_swap, gain_two_rows
    )

    pair_grads = lax.all_to_all(
        pair_grads.reshape(devices_ctx, shard_rows, pair_cols), ("y", "zh"), 0, 0, tiled=True
    )
    query_swap = swap_cores(query_low)
    gain_two_rows = mm(gain_two_rows, hot).astype(BF16)
    gain_two_swap = swap_cores(gain_two_rows[:, half:])
    gain_two_both = jnp.concatenate([gain_two_rows[:, :half], gain_two_swap])
    *rest_term, query_both = run_kernel(
        term_kernel,
        [((160, 2 * QUERY_WIDTH), BF16)] * 4 + [((2 * shard_rows, QUERY_WIDTH), BF16)],
        (
            normed_both,
            query_low,
            query_swap,
            attended_moved,
            attended_swap,
            branch_grad,
            branch_swap,
        ),
        4 * half * 2 * shard_rows * QUERY_WIDTH,
        LARGE_BYTES,
    )
    rest_blocks = scatter(rest_term, 2)
    terms = lax.psum_scatter(
        after(terms, query_both), ("zh", "zl"), scatter_dimension=0, tiled=True
    )
    activations, sums = run_kernel(
        finish_kernel,
        [((shard_rows, model_width), BF16), ((8, 128), F32)],
        (*feed_parts, middle, branch, row_weight),
        0,
        LARGE_BYTES,
    )
    pair_grads, query_both, gain_two_both, sums = phase(
        pair_grads, query_both, gain_two_both, sums
    )

    (pair_low,) = run_kernel(
        pair_back_kernel,
        [((shard_rows, pair_cols), BF16)],
        (pair_grads, cosine, sine),
        0,
    )
    pair_both = jnp.concatenate([pair_low, swap_cores(pair_low)])
    sums_one = send(sums, lambda x, y, z, core: (x, y, z + 2, core))
    query_back = mm_nt(query_both, query_part)
    *rest_blocks, pair_both, sums, sums_one, tokens_moved, query_back = phase(
        *rest_blocks, pair_both, sums, sums_one, tokens_moved, query_back
    )

    scaled_both = jnp.concatenate(
        [(tokens_moved * factor_one)[:, :half], halves[shard_rows:].astype(F32)]
    )
    normed_grad = query_back + mm_nt(pair_both, key_part[:, :pair_cols])
    first_cols = np.arange(GAIN_COLS) < GAIN_COLS // 2
    first_cols = np.broadcast_to(first_cols, (2 * shard_rows, GAIN_COLS))
    gain_terms = mm_tn(gain_two_both, jnp.asarray(~first_cols, BF16)) + mm_tn(
        (normed_grad * scaled_both).astype(BF16), jnp.asarray(first_cols, BF16)
    )
    pair_term = mm_tn(normed_both, pair_both)
    pair_cuts = cut(jnp.concatenate([pair_term, gain_terms], axis=1))
    pair_blocks = scatter(pair_cuts, 2)
    normed_grad_swap = swap_cores(normed_grad[shard_rows:].astype(BF16))
    unit_term, down_term = unpack_slice(after(terms, pair_cuts[1]))
    unit_term = lax.all_to_all(
        unit_term.reshape(8, -1, unit_term.shape[1]), ROW_AXES, 0, 0, tiled=True
    )
    rest_total = add_up([after(rest_blocks[0], pair_cuts[1])] + rest_blocks[1:])
    sums = sums + sums_one
    sums_one = send(sums, lambda x, y, z, core: (x, y ^ 1, z, core))
    (
        *pair_blocks,
        rest_total,
        sums,
        sums_one,
        unit_term,
        down_term,
        normed_grad,
        normed_grad_swap,
    ) = phase(
        *pair_blocks,
        rest_total,
        sums,
        sums_one,
        unit_term,
        down_term,
        normed_grad[:shard_rows],
        normed_grad_swap,
    )

    cuts = cut(jnp.concatenate([add_up(pair_blocks), rest_total], axis=1))
    blocks = scatter(cuts, 1)
    unit_term = after(unit_term, cuts[1]).astype(F32)
    grad_gate = unpack_units(unit_term[:, :, :units_here])
    grad_up = unpack_units(unit_term[:, :, units_here:])
    down_sum = swap_half_core(down_term)
    sums = sums + sums_one
    sums_one = send(sums, lambda x, y, z, core: (x, y ^ 2, z, core))
    normed_grad, normed_grad_swap = after((normed_grad, normed_grad_swap), cuts[1])
    normed_grad = jnp.concatenate([normed_grad, normed_grad_swap.astype(F32)], axis=1)
    input_part = norm_back(tokens_moved, factor_one, gain_one, normed_grad)
    input_grad = (mid_grad + mm_nt(input_part.astype(BF16), hot)).astype(BF16)
    *blocks, sums, sums_one, grad_gate, grad_up, down_sum, input_grad = phase(
        *blocks, sums, sums_one, grad_gate, grad_up, down_sum, input_grad
    )

    blocks = scatter(add_up(blocks), 0)
    down_sum = down_sum[: w_down.shape[0]].astype(F32)
    sums = sums + sums_one
    sums = sums[:3, :1].reshape(1, 3)
    seq_rms = jnp.sqrt(sums / (seq_length.astype(F32) * model_width))
    total = add_up(blocks)
    return (
        activations,
        input_grad,
        total[:, pair_cols],
        total[:, split : split + QUERY_WIDTH],
        total[:, :KEY_WIDTH],
        total[:, KEY_WIDTH:pair_cols],
        total[:, split + QUERY_WIDTH :],
        total[:, pair_cols + GAIN_COLS - 1],
        grad_gate,
        grad_up,
        down_sum,
        seq_rms,
    )


def solution(mesh):
    fine = Mesh(mesh.devices.reshape(SIZES), AXES)
    rows = P(AXES, None)
    flat = P(AXES)
    group = ("x", "zl", "core")
    in_specs = (
        (rows, flat, rows, rows, rows, rows, flat, rows, rows, rows)
        + (P(group, None), P(group), P(group))
        + (rows,)
    )
    out_specs = (rows, rows, flat, rows, rows, rows, rows, flat, rows, rows, rows, P(group, None))
    return jax.shard_map(
        local, mesh=fine, in_specs=in_specs, out_specs=out_specs, check_vma=False
    )
```

```python
import functools

import jax
import jax.numpy as jnp
import numpy as np
from jax import lax
from jax.experimental import pallas as pl
from jax.experimental.pallas import tpu as pltpu
from jax.sharding import Mesh, PartitionSpec as P

QUERY_HEADS = 20
KEY_VALUE_HEADS = 5
HEAD_WIDTH = 64
QUERY_WIDTH = QUERY_HEADS * HEAD_WIDTH
KEY_WIDTH = KEY_VALUE_HEADS * HEAD_WIDTH
GAIN_COLS = 128
KERNEL_BYTES = 20 * 1024 * 1024
LARGE_BYTES = 58 * 1024 * 1024
FEED_BYTES = 24 * 1024 * 1024
PAD_UNITS = 32

EPSILON = 1e-05
ROPE_BASE = 10000.0
MASKED_SCORE = -1e30

AXES = ("y", "zh", "x", "zl", "core")
SIZES = (4, 2, 4, 2, 2)
ROW_AXES = ("y", "core")
SLICE_AXES = ("x", "zh", "zl")
F32 = jnp.float32
BF16 = jnp.bfloat16


def device_number(x, y, z, core):
    return (((y * 2 + z // 2) * 4 + x) * 2 + z % 2) * 2 + core


def pairs_of(move):
    pairs = []
    for y in range(4):
        for z in range(4):
            for x in range(4):
                for core in range(2):
                    tx, ty, tz, tc = move(x, y, z, core)
                    pairs.append(
                        (device_number(x, y, z, core), device_number(tx % 4, ty % 4, tz % 4, tc))
                    )
    return pairs


def send(values, move):
    return lax.ppermute(values, AXES, pairs_of(move))


def swap_cores(values):
    return send(values, lambda x, y, z, core: (x, y, z, 1 - core))


def swap_half_core(values):
    return send(values, lambda x, y, z, core: (x, y, core * 2 + z % 2, z // 2))


def stage_move(stage, distance):
    def move(x, y, z, core):
        spot = [x, y, z]
        spot[(stage + core + 1) % 3] += distance
        return (spot[0], spot[1], spot[2], core)

    return move


def spread(values, stage):
    arrived = [send(values, stage_move(stage, -distance)) for distance in (1, 2, 3)]
    return [values] + arrived


def join(blocks):
    return lax.optimization_barrier(jnp.concatenate(blocks, axis=0))


def cut(total):
    low = total.astype(BF16)
    rows = low.shape[0] // 4
    return [low[step * rows : (step + 1) * rows] for step in range(4)]


def scatter(total, stage):
    parts = total if isinstance(total, list) else cut(total)
    arrived = [send(parts[step], stage_move(stage, step)) for step in (1, 2, 3)]
    return [parts[0]] + arrived


def add_up(blocks):
    total = blocks[0].astype(F32)
    for block in blocks[1:]:
        total = total + block.astype(F32)
    return total


def phase(*values):
    return lax.optimization_barrier(values)


def along_y(values, distance):
    return send(values, lambda x, y, z, core: (x, y + distance, z, core))


def gather_rows(own):
    blocks = [own] + [along_y(own, -distance) for distance in (1, 2, 3)]
    return blocks + [swap_cores(block) for block in blocks]


def add_cores(own, other):
    return [(a.astype(F32) + swap_cores(b).astype(F32)) for a, b in zip(own, other)]


def reduce_blocks(sums):
    total = sums[0]
    for distance in (1, 2, 3):
        total = total + along_y(sums[distance].astype(BF16), distance).astype(F32)
    return total


def after(values, *earlier):
    return lax.optimization_barrier((values,) + earlier)[0]


def row_order(place, core):
    third, second, first, inner = jnp.meshgrid(
        jnp.arange(4), jnp.arange(4), jnp.arange(4), jnp.arange(10), indexing="ij"
    )
    spot = list(place)
    for stage, step in enumerate((first, second, third)):
        axis = (stage + core + 1) % 3
        spot[axis] = spot[axis] + step
    sx, sy, sz = spot
    numbers = device_number(sx % 4, sy % 4, sz % 4, core) * 10 + inner
    return numbers.reshape(-1).astype(jnp.int32)


def slice_order():
    x, zh, zl, y, core, inner = np.meshgrid(
        *(np.arange(n) for n in (4, 2, 2, 4, 2, 10)), indexing="ij"
    )
    return (device_number(x, y, zh * 2 + zl, core) * 10 + inner).reshape(-1).astype(np.int32)


def one_hot_back(order):
    return (order[:, None] == jnp.arange(order.shape[0], dtype=jnp.int32)[None, :]).astype(BF16)


def one_hot(order):
    return (jnp.arange(order.shape[0], dtype=jnp.int32)[:, None] == order[None, :]).astype(BF16)


def exact_move(values, hot):
    high = values.astype(BF16)
    low = (values - high.astype(F32)).astype(BF16)
    return mm(high, hot) + mm(low, hot)


def mm(left, right):
    return jnp.dot(left, right, preferred_element_type=F32)


def mm_nt(left, right):
    return lax.dot_general(left, right, (((1,), (1,)), ((), ())), preferred_element_type=F32)


def mm_tn(left, right):
    return lax.dot_general(left, right, (((0,), (0,)), ((), ())), preferred_element_type=F32)


def norm_factor(values):
    return lax.rsqrt(jnp.mean(values * values, axis=-1, keepdims=True) + EPSILON)


def norm_back(values, factor, gain, grad):
    weighted = gain * grad
    inner = jnp.mean(weighted * values, axis=-1, keepdims=True)
    return factor * weighted - values * (factor * factor * factor) * inner


def rope_tables(angles_at):
    half_size = HEAD_WIDTH // 2
    powers = jnp.arange(half_size, dtype=F32) * (2.0 / HEAD_WIDTH)
    speeds = jnp.power(ROPE_BASE, -powers)
    angles = angles_at[:, None] * speeds[None, :]
    cosine, sine = jnp.cos(angles), jnp.sin(angles)
    return (jnp.concatenate([cosine] * 4, axis=1), jnp.concatenate([-sine, sine] * 2, axis=1))


def rotate_pairs(values, cosine, sine):
    width = values.shape[1]
    half_size = HEAD_WIDTH // 2
    lanes = lax.broadcasted_iota(jnp.int32, values.shape, 1) % HEAD_WIDTH
    ahead = pltpu.roll(values, width - half_size, 1)
    behind = pltpu.roll(values, half_size, 1)
    return values * cosine + jnp.where(lanes < half_size, ahead, behind) * sine


def wide_table(table, width):
    return jnp.concatenate([table] * (width // table.shape[1]), axis=1)


def low_high(rows):
    low = [rows[at : at + 64] for at in range(0, rows.shape[0], 128)]
    high = [rows[at + 64 : at + 128] for at in range(0, rows.shape[0], 128)]
    return jnp.concatenate(low, axis=0), jnp.concatenate(high, axis=0)


def stack_heads(rows, head):
    pieces = [
        rows[at : at + 64, (4 * head + step) * HEAD_WIDTH : (4 * head + step + 1) * HEAD_WIDTH]
        for at in (0, 64)
        for step in range(4)
    ]
    return jnp.concatenate(pieces, axis=0)


def unstack_heads(stack):
    halves = [
        jnp.concatenate([stack[at + 64 * step : at + 64 * step + 64] for step in range(4)], axis=1)
        for at in (0, 256)
    ]
    return jnp.concatenate(halves, axis=0)


def mask_bias(keys_ref, rows_ref):
    columns = keys_ref[...].T
    keys_low, keys_high = columns[:512], columns[512:]

    def bias(keys, lanes):
        seen = (keys[:, 0:1] <= rows_ref[0:1, lanes]) | (keys[:, 1:2] == rows_ref[1:2, lanes])
        return jnp.where(seen, 0.0, MASKED_SCORE).astype(F32)

    return bias(keys_low, slice(0, 512)), bias(keys_high, slice(256, 512))


def attend_kernel(q_ref, part_ref, kv_ref, cos_ref, sin_ref, keys_ref, rows_ref, out_ref, turned_ref, log_ref):
    cosine = wide_table(cos_ref[...], QUERY_WIDTH)
    sine = wide_table(sin_ref[...], QUERY_WIDTH)
    queries = q_ref[...] + part_ref[...].astype(F32)
    queries = (rotate_pairs(queries, cosine, sine) * HEAD_WIDTH**-0.5).astype(BF16)
    turned_ref[...] = queries
    kv_low, kv_high = low_high(kv_ref[...])
    bias_low, bias_high = mask_bias(keys_ref, rows_ref)
    for head in range(KEY_VALUE_HEADS):
        at = slice(head * HEAD_WIDTH, (head + 1) * HEAD_WIDTH)
        vat = slice(KEY_WIDTH + head * HEAD_WIDTH, KEY_WIDTH + (head + 1) * HEAD_WIDTH)
        stack = stack_heads(queries, head)
        score_low = mm_nt(kv_low[:, at], stack) + bias_low
        score_high = mm_nt(kv_high[:, at], stack[256:]) + bias_high
        top_low = jnp.max(score_low, axis=0, keepdims=True)
        top_high = jnp.max(score_high, axis=0, keepdims=True)
        top = jnp.concatenate(
            [top_low[:, :256], jnp.maximum(top_low[:, 256:], top_high)], axis=1
        )
        exp_low = jnp.exp(score_low - top)
        exp_high = jnp.exp(score_high - top[:, 256:])
        total = jnp.sum(exp_low, axis=0, keepdims=True)
        total_high = jnp.sum(exp_high, axis=0, keepdims=True)
        total = jnp.concatenate([total[:, :256], total[:, 256:] + total_high], axis=1)
        result = mm_tn(kv_low[:, vat], exp_low.astype(BF16))
        result_high = mm_tn(kv_high[:, vat], exp_high.astype(BF16))
        result = jnp.concatenate([result[:, :256], result[:, 256:] + result_high], axis=1)
        result = (result / total).T
        out_ref[:, head * 256 : (head + 1) * 256] = unstack_heads(result).astype(BF16)
        log_ref[head : head + 1, :] = top + jnp.log(total)


def attend_back_kernel(
    q_ref, kv_ref, out_ref, grad_ref, log_ref, cos_ref, sin_ref, keys_ref, rows_ref, dq_ref, dkv_ref
):
    kv_low, kv_high = low_high(kv_ref[...])
    bias_low, bias_high = mask_bias(keys_ref, rows_ref)
    queries = q_ref[...]
    outs = out_ref[...]
    grads = grad_ref[...]
    ones = jnp.ones((8, HEAD_WIDTH), F32)
    dq_parts, dk_low, dk_high, dv_low, dv_high = [], [], [], [], []
    for head in range(KEY_VALUE_HEADS):
        at = slice(head * HEAD_WIDTH, (head + 1) * HEAD_WIDTH)
        vat = slice(KEY_WIDTH + head * HEAD_WIDTH, KEY_WIDTH + (head + 1) * HEAD_WIDTH)
        stack = stack_heads(queries, head)
        grad = stack_heads(grads, head)
        product = grad.astype(F32) * stack_heads(outs, head).astype(F32)
        delta = lax.dot_general(
            ones,
            product,
            (((1,), (1,)), ((), ())),
            preferred_element_type=F32,
            precision=lax.Precision.HIGHEST,
        )[0:1]
        logs = log_ref[head : head + 1, :]
        key_low, key_high = kv_low[:, at], kv_high[:, at]
        probs_low = jnp.exp(mm_nt(key_low, stack) + bias_low - logs)
        probs_high = jnp.exp(mm_nt(key_high, stack[256:]) + bias_high - logs[:, 256:])
        back_low = mm_nt(kv_low[:, vat], grad)
        back_high = mm_nt(kv_high[:, vat], grad[256:])
        score_low = (probs_low * (back_low - delta)).astype(BF16)
        score_high = (probs_high * (back_high - delta[:, 256:])).astype(BF16)
        dv_low.append(mm(probs_low.astype(BF16), grad))
        dv_high.append(mm(probs_high.astype(BF16), grad[256:]))
        dk_low.append(mm(score_low, stack))
        dk_high.append(mm(score_high, stack[256:]))
        dq = mm_tn(key_low, score_low)
        dq_high = mm_tn(key_high, score_high)
        dq = jnp.concatenate([dq[:, :256], dq[:, 256:] + dq_high], axis=1)
        dq_parts.append(unstack_heads((dq * HEAD_WIDTH**-0.5).T))
    cosine = wide_table(cos_ref[...], QUERY_WIDTH)
    sine = wide_table(sin_ref[...], QUERY_WIDTH)
    dq_ref[...] = rotate_pairs(jnp.concatenate(dq_parts, axis=1), cosine, -sine).astype(BF16)
    low = jnp.concatenate(dk_low + dv_low, axis=1).astype(BF16)
    high = jnp.concatenate(dk_high + dv_high, axis=1).astype(BF16)
    for at in range(8):
        dkv_ref[128 * at : 128 * at + 64] = low[64 * at : 64 * at + 64]
        dkv_ref[128 * at + 64 : 128 * at + 128] = high[64 * at : 64 * at + 64]


def run_kernel(kernel, shapes, operands, flops, limit=KERNEL_BYTES):
    return pl.pallas_call(
        kernel,
        out_shape=[jax.ShapeDtypeStruct(shape, kind) for shape, kind in shapes],
        in_specs=[pl.BlockSpec(memory_space=pltpu.VMEM)] * len(operands),
        out_specs=[pl.BlockSpec(memory_space=pltpu.VMEM)] * len(shapes),
        compiler_params=pltpu.CompilerParams(vmem_limit_bytes=limit),
        cost_estimate=pl.CostEstimate(
            flops=flops,
            bytes_accessed=sum(v.size * v.dtype.itemsize for v in operands),
            transcendentals=0,
        ),
    )(*operands)


def pair_kernel(
    moved_ref,
    factor_ref,
    part_ref,
    other_ref,
    cos_ref,
    sin_ref,
    pairs_ref,
    normed_ref,
    halves_ref,
    gains_ref,
):
    half = part_ref.shape[0]
    pair_cols = 2 * KEY_WIDTH
    gains = [ref[:, pair_cols:].astype(F32).T[:8] for ref in (part_ref, other_ref)]
    gains = jnp.concatenate(gains, axis=1)
    gains_ref[...] = gains
    scaled = moved_ref[...] * factor_ref[...]
    normed = (scaled * gains[0:1]).astype(BF16)
    normed_ref[...] = normed
    halves_ref[...] = normed[:, half:]
    both = mm(normed[:, :half], part_ref[:, :pair_cols]) + mm(
        normed[:, half:], other_ref[:, :pair_cols]
    )
    wide = 3 * cos_ref.shape[1]
    turned = rotate_pairs(
        both[:, :wide], wide_table(cos_ref[...], wide), wide_table(sin_ref[...], wide)
    )
    pairs = jnp.concatenate([turned[:, :KEY_WIDTH], both[:, KEY_WIDTH:]], axis=1).astype(BF16)
    for at in range(8):
        pairs_ref[at] = pairs


def pair_back_kernel(parts_ref, cos_ref, sin_ref, low_ref):
    total = parts_ref[0].astype(F32)
    for at in range(1, 8):
        total = total + parts_ref[at].astype(F32)
    wide = 3 * cos_ref.shape[1]
    turned = rotate_pairs(
        total[:, :wide], wide_table(cos_ref[...], wide), -wide_table(sin_ref[...], wide)
    )
    low_ref[...] = jnp.concatenate(
        [turned[:, :KEY_WIDTH], total[:, KEY_WIDTH:]], axis=1
    ).astype(BF16)


def middle_kernel(
    own_swap,
    back_a,
    back_b,
    back_c,
    back_d,
    cot_ref,
    middle_ref,
    factor_ref,
    gain_ref,
    hot_slice_ref,
    part_ref,
    other_ref,
    hot_ref,
    mid_ref,
    branch_ref,
    grad_ref,
    hot_slice,
    parts,
    hot,
    sems,
):
    half = part_ref.shape[0]
    copies = [
        pltpu.make_async_copy(hot_slice_ref, hot_slice, sems.at[0]),
        pltpu.make_async_copy(part_ref, parts.at[0:half], sems.at[1]),
        pltpu.make_async_copy(other_ref, parts.at[half : 2 * half], sems.at[2]),
        pltpu.make_async_copy(hot_ref, hot, sems.at[3]),
    ]
    for copy in copies:
        copy.start()
    total = own_swap[...].astype(F32) + back_a[...].astype(F32) + back_b[...].astype(F32)
    total = total + back_c[...].astype(F32)
    total = (total + back_d[...].astype(F32)).astype(BF16)
    copies[0].wait()
    grad = mm(total, hot_slice[...])
    middle, factor = middle_ref[...], factor_ref[...]
    mid = cot_ref[...] + norm_back(middle, factor, gain_ref[...], grad)
    mid_ref[...] = mid
    branch = mid.astype(BF16)
    branch_ref[...] = branch
    copies[1].wait()
    copies[2].wait()
    moved = mm_nt(branch, parts[...]).astype(BF16)
    copies[3].wait()
    grad_ref[...] = mm(moved, hot[...]).astype(BF16)


def middle_call(small, large):
    vmem, hbm = pl.BlockSpec(memory_space=pltpu.VMEM), pl.BlockSpec(memory_space=pltpu.HBM)
    rows, width = small[0].shape
    square = pltpu.VMEM((width, width), BF16)
    return pl.pallas_call(
        middle_kernel,
        out_shape=[jax.ShapeDtypeStruct((rows, width), kind) for kind in (F32, BF16, BF16)],
        in_specs=[vmem] * len(small) + [hbm] * len(large),
        out_specs=[vmem] * 3,
        scratch_shapes=[square, square, square, pltpu.SemaphoreType.DMA((4,))],
        compiler_params=pltpu.CompilerParams(vmem_limit_bytes=LARGE_BYTES),
        cost_estimate=pl.CostEstimate(
            flops=6 * rows * width * width, bytes_accessed=16 * 2**20, transcendentals=0
        ),
    )(*small, *large)


def finish_kernel(
    feed_a, feed_b, feed_c, feed_d, middle_ref, branch_ref, weight_ref, out_ref, sums_ref
):
    feed = feed_a[...] + feed_b[...].astype(F32) + feed_c[...].astype(F32)
    feed = feed + feed_d[...].astype(F32)
    final = middle_ref[...] + feed
    out_ref[...] = final.astype(BF16)
    sums_ref[...] = jnp.zeros(sums_ref.shape, F32)
    for row, values in enumerate((branch_ref[...], feed, final)):
        part = jnp.sum(weight_ref[...] * values * values, axis=0, keepdims=True)
        part = jnp.sum(part, axis=1, keepdims=True)
        sums_ref[row : row + 1] = jnp.broadcast_to(part, (1, 128))


def query_kernel(
    normed_ref,
    halves_ref,
    a_ref,
    b_ref,
    c_ref,
    d_ref,
    own_ref,
    other_ref,
    both_ref,
    query_ref,
    out_ref,
    sems,
):
    width, count = query_ref.shape[1], a_ref.shape[0]
    copies = []
    for step, block in enumerate((a_ref, b_ref, c_ref, d_ref)):
        at = slice(step * count, (step + 1) * count)
        copies.append(
            pltpu.make_async_copy(block.at[:, 0:width], query_ref.at[at], sems.at[step])
        )
    for step, block in enumerate((a_ref, b_ref, c_ref, d_ref)):
        at = slice(step * count, (step + 1) * count)
        copies.append(
            pltpu.make_async_copy(
                block.at[:, width : 2 * width], out_ref.at[at], sems.at[4 + step]
            )
        )
    for copy in copies:
        copy.start()
    for copy in copies[:4]:
        copy.wait()
    half = own_ref.shape[0]
    both_ref[0:half] = normed_ref[:, : both_ref.shape[1]]
    both_ref[half : 2 * half] = halves_ref[...]
    both = mm(both_ref[...], query_ref[...])
    own_ref[...] = both[:half]
    other_ref[...] = both[half:].astype(BF16)
    for copy in copies[4:]:
        copy.wait()


def query_parts(normed, halves, blocks):
    vmem = pl.BlockSpec(memory_space=pltpu.VMEM)
    half, width = normed.shape[0], QUERY_WIDTH
    joined = jax.ShapeDtypeStruct((4 * blocks[0].shape[0], width), BF16)
    return pl.pallas_call(
        query_kernel,
        out_shape=[
            jax.ShapeDtypeStruct((half, width), F32),
            jax.ShapeDtypeStruct((half, width), BF16),
            jax.ShapeDtypeStruct((2 * half, halves.shape[1]), BF16),
            joined,
            joined,
        ],
        in_specs=[vmem] * 2 + [pl.BlockSpec(memory_space=pltpu.HBM)] * 4,
        out_specs=[vmem] * 5,
        scratch_shapes=[pltpu.SemaphoreType.DMA((8,))],
        compiler_params=pltpu.CompilerParams(vmem_limit_bytes=LARGE_BYTES),
        cost_estimate=pl.CostEstimate(
            flops=4 * halves.size * width, bytes_accessed=10 * 2**20, transcendentals=0
        ),
    )(normed, halves, *blocks)


def unpack_kernel(slices_ref, units_ref, down_ref):
    for block in range(16):
        base, at = block * 128, block * 32
        units_ref[block * 80 : block * 80 + 80] = slices_ref[base : base + 80]
        down_ref[at : at + 32, :1024] = slices_ref[base + 80 : base + 112]
        down_ref[at : at + 16, 1024:] = slices_ref[base + 112 : base + 128, :256]
        down_ref[at + 16 : at + 32, 1024:] = slices_ref[base + 112 : base + 128, 256:512]


def unpack_slices(slices):
    return run_kernel(
        unpack_kernel, [((1280, 1024), BF16), ((512, 1280), BF16)], (slices,), 0, FEED_BYTES
    )


def feed_kernel(
    xa_ref,
    xb_ref,
    all_grads_ref,
    places_ref,
    units_ref,
    down_ref,
    hidden_ref,
    unit_ref,
    back_a_ref,
    back_b_ref,
    out_a_ref,
    out_b_ref,
    rows_ref,
    grads_ref,
    sems,
    *,
    step,
):
    half = xa_ref.shape[0]
    low = slice(0, half)
    high = slice(half, 2 * half)
    spot_a = pl.ds(pl.multiple_of(places_ref[step], half), half)
    spot_b = pl.ds(pl.multiple_of(places_ref[step + 4], half), half)
    copies = [
        pltpu.make_async_copy(xa_ref, rows_ref.at[low], sems.at[0]),
        pltpu.make_async_copy(xb_ref, rows_ref.at[high], sems.at[1]),
    ]
    copies += [
        pltpu.make_async_copy(all_grads_ref.at[spot_a], grads_ref.at[low], sems.at[2]),
        pltpu.make_async_copy(all_grads_ref.at[spot_b], grads_ref.at[high], sems.at[3]),
    ]
    for copy in copies:
        copy.start()
    copies[0].wait()
    copies[1].wait()
    units = units_ref.shape[1] // 2
    both = mm(rows_ref[...], units_ref[...])
    gate, up = both[:, :units], both[:, units:]
    sigmoid = 1.0 / (1.0 + jnp.exp(-gate))
    silu = gate * sigmoid
    hidden = (silu * up).astype(BF16)
    hidden_ref[...] = hidden
    for copy in copies[2:]:
        copy.wait()
    hidden_grad = mm_nt(grads_ref[...], down_ref[...])
    gate_low = (hidden_grad * up * sigmoid * (1.0 + gate * (1.0 - sigmoid))).astype(BF16)
    up_low = (hidden_grad * silu).astype(BF16)
    unit = jnp.concatenate([gate_low, up_low], axis=1)
    unit_ref[...] = unit
    back = mm_nt(unit, units_ref[...]).astype(BF16)
    back_a_ref[...] = back[:half]
    back_b_ref[...] = back[half:]
    outs = mm(hidden, down_ref[...]).astype(BF16)
    out_a_ref[...] = outs[:half]
    out_b_ref[...] = outs[half:]


def feed_chunk(step, rows_a, rows_b, all_grads, places, units, down):
    count, width = rows_a.shape[0] * 2, rows_a.shape[1]
    vmem = pl.BlockSpec(memory_space=pltpu.VMEM)
    hbm = pl.BlockSpec(memory_space=pltpu.HBM)
    shapes = [(count, 512), (count, 1024)] + [rows_a.shape] * 4
    return pl.pallas_call(
        functools.partial(feed_kernel, step=step),
        out_shape=[jax.ShapeDtypeStruct(shape, BF16) for shape in shapes],
        in_specs=[hbm] * 3 + [pl.BlockSpec(memory_space=pltpu.SMEM)] + [vmem] * 2,
        out_specs=[vmem] * 6,
        scratch_shapes=[
            pltpu.VMEM((count, width), BF16),
            pltpu.VMEM((count, width), BF16),
            pltpu.SemaphoreType.DMA((4,)),
        ],
        compiler_params=pltpu.CompilerParams(vmem_limit_bytes=FEED_BYTES),
        cost_estimate=pl.CostEstimate(
            flops=2 * count * width * 3 * 1024,
            bytes_accessed=2 * (units.size + down.size + 4 * rows_a.size),
            transcendentals=0,
        ),
    )(rows_a, rows_b, all_grads, places, units, down)


def weight_kernel(*refs):
    sources, all_grads, places, term_out = refs[:16], refs[16], refs[17], refs[18]
    rows, unit, grads, hidden, terms = refs[19:24]
    in_sems, out_sems = refs[24:]
    copies, late = [], []
    for step in range(4):
        base = step * 256
        low, high, both = slice(base, base + 128), slice(base + 128, base + 256), slice(
            base, base + 256
        )
        spot_a = pl.ds(pl.multiple_of(places[step], 128), 128)
        spot_b = pl.ds(pl.multiple_of(places[step + 4], 128), 128)
        for pieces, source, target in (
            (copies, sources[step], rows.at[low]),
            (copies, sources[step + 4], rows.at[high]),
            (copies, sources[step + 12], unit.at[both]),
            (late, all_grads.at[spot_a], grads.at[low]),
            (late, all_grads.at[spot_b], grads.at[high]),
            (late, sources[step + 8], hidden.at[both]),
        ):
            sem = in_sems.at[len(copies) + len(late)]
            pieces.append(pltpu.make_async_copy(source, target, sem))
    for copy in copies + late:
        copy.start()
    for copy in copies:
        copy.wait()
    for at in range(0, 16, 4):
        total = mm_tn(rows[:, at * 80 : at * 80 + 320], unit[...]).astype(BF16)
        for step in range(4):
            base = (at + step) * 128
            terms[base : base + 80] = total[step * 80 : step * 80 + 80]
    for copy in late:
        copy.wait()
    moves = []
    for at in range(0, 16, 4):
        total = mm_tn(hidden[:, at * 32 : at * 32 + 128], grads[...]).astype(BF16)
        for step in range(4):
            rows_here = total[step * 32 : step * 32 + 32]
            base = (at + step) * 128
            terms[base + 80 : base + 112] = rows_here[:, :1024]
            terms[base + 112 : base + 128, 0:256] = rows_here[:16, 1024:]
            terms[base + 112 : base + 128, 256:512] = rows_here[16:, 1024:]
            terms[base + 112 : base + 128, 512:] = jnp.zeros((16, 512), BF16)
        piece = slice(at * 128, at * 128 + 512)
        moves.append(
            pltpu.make_async_copy(terms.at[piece], term_out.at[piece], out_sems.at[at // 4])
        )
        moves[-1].start()
    for move in moves:
        move.wait()


def weight_terms(rows, all_grads, places, chunks):
    sources = list(rows)
    for part in (0, 1):
        sources += [chunk[part] for chunk in chunks]
    hidden, unit = chunks[0][0], chunks[0][1]
    count, width = 8 * rows[0].shape[0], rows[0].shape[1]
    smem, hbm = pl.BlockSpec(memory_space=pltpu.SMEM), pl.BlockSpec(memory_space=pltpu.HBM)
    return pl.pallas_call(
        weight_kernel,
        out_shape=jax.ShapeDtypeStruct((2048, 1024), BF16),
        in_specs=[pl.BlockSpec(memory_space=pl.ANY)] * 16 + [hbm, smem],
        out_specs=hbm,
        scratch_shapes=[
            pltpu.VMEM((count, width), BF16),
            pltpu.VMEM((count, unit.shape[1]), BF16),
            pltpu.VMEM((count, width), BF16),
            pltpu.VMEM((count, hidden.shape[1]), BF16),
            pltpu.VMEM((2048, 1024), BF16),
            pltpu.SemaphoreType.DMA((24,)),
            pltpu.SemaphoreType.DMA((4,)),
        ],
        compiler_params=pltpu.CompilerParams(vmem_limit_bytes=24 * 1024 * 1024),
        cost_estimate=pl.CostEstimate(
            flops=2 * count * 1280 * 1536, bytes_accessed=2**20, transcendentals=0
        ),
    )(*sources, all_grads, places)


def term_kernel(normed_ref, q_ref, qs_ref, attended_ref, as_ref, b_ref, bs_ref, *outs):
    count = outs[0].shape[0]
    half = normed_ref.shape[1]
    queries = jnp.concatenate([q_ref[...], qs_ref[...]], axis=0)
    outs[4][...] = queries
    branch = jnp.concatenate([b_ref[...], bs_ref[...]], axis=0)
    attended = jnp.concatenate([attended_ref[:, :half], as_ref[...]], axis=0)
    query_term = mm_tn(normed_ref[...], queries).astype(BF16)
    out_term = mm_tn(attended, branch).astype(BF16)
    for step in range(4):
        at = slice(step * count, (step + 1) * count)
        outs[step][:, :QUERY_WIDTH] = query_term[at]
        outs[step][:, QUERY_WIDTH:] = out_term[at]


def pack_slice(units, down):
    rest = jnp.concatenate([down[:16, 1024:], down[16:, 1024:]], axis=1)
    rest = jnp.pad(rest, ((0, 0), (0, 512)))
    return jnp.concatenate([units, down[:, :1024], rest], axis=0)


def unpack_slice(rows):
    rest = jnp.concatenate([rows[112:, :256], rows[112:, 256:512]], axis=0)
    return rows[:80], jnp.concatenate([rows[80:112], rest], axis=1)


def group_places(pair_row, devices_ctx, block_size):
    slots = jnp.arange(devices_ctx * 2 * block_size, dtype=jnp.int32)
    owners = slots // (2 * block_size)
    inside = slots % (2 * block_size)
    columns = jnp.arange(devices_ctx, dtype=jnp.int32)
    paired = jnp.sum(jnp.where(owners[:, None] == columns[None, :], pair_row[None, :], 0), axis=1)
    blocks = jnp.where(inside < block_size, paired, 2 * devices_ctx - 1 - paired)
    return blocks * block_size + inside % block_size


def pack_units(weight):
    rows = weight.shape[0]
    runs = weight.reshape(rows, 8, 4, 2, 2, 28).transpose(1, 0, 2, 4, 3, 5)
    runs = jnp.pad(runs, ((0, 0),) * 5 + ((0, PAD_UNITS - 28),))
    return runs.reshape(8, rows, 16 * PAD_UNITS)


def unpack_units(packed):
    rows = packed.shape[1]
    runs = packed.reshape(8, rows, 4, 2, 2, PAD_UNITS)[..., :28]
    return runs.transpose(1, 0, 2, 4, 3, 5).reshape(rows, 8 * 16 * 28)


def local(
    tokens,
    norm_gain,
    w_query,
    w_key,
    w_value,
    w_out,
    mlp_gain,
    w_gate,
    w_up,
    w_down,
    block_pair,
    seq_len,
    seq_start,
    out_grad,
):
    shard_rows, model_width = tokens.shape
    block_size = shard_rows // 2
    half = model_width // 2
    devices_ctx = 8
    at_y, at_zh, at_x, at_zl, at_core = (lax.axis_index(name) for name in AXES)
    place = (at_x, at_y, at_zh * 2 + at_zl)
    position = at_y * 2 + at_zh
    pair_cols = 2 * KEY_WIDTH
    split = pair_cols + GAIN_COLS

    first_slot = seq_start[0]
    seq_length = seq_len[0]
    own_pair = lax.dynamic_slice_in_dim(block_pair[0], position, 1)
    inside = jnp.arange(shard_rows, dtype=jnp.int32)
    blocks_here = jnp.where(inside < block_size, own_pair, 2 * devices_ctx - 1 - own_pair)
    places_here = blocks_here * block_size + inside % block_size
    valid_here = (places_here >= first_slot) & (places_here < first_slot + seq_length)
    row_weight = valid_here.astype(F32)[:, None]
    cotangent = out_grad.astype(F32) * row_weight
    feed_grad = cotangent.astype(BF16)
    grad_rows = lax.all_gather(feed_grad, ROW_AXES, axis=0, tiled=True)

    gains = jnp.stack([norm_gain, mlp_gain], axis=1)
    gains = jnp.pad(gains, ((0, 0), (0, GAIN_COLS - 2)))
    front = jnp.concatenate([w_key, w_value, gains, w_query, w_out], axis=1)
    front = spread(after(front, feed_grad), 0)
    units = jnp.concatenate([pack_units(w_gate), pack_units(w_up)], axis=2)
    *arrived, units, tokens, block_pair, places_here, valid_here = phase(
        *front, units, tokens, block_pair, places_here, valid_here
    )

    front = spread(join(arrived), 1)
    units = lax.all_to_all(units, ROW_AXES, 0, 0, tiled=True)
    down_rows = jnp.pad(w_down, ((0, PAD_UNITS - w_down.shape[0]), (0, 0)))
    down_rows = swap_half_core(after(down_rows, places_here))
    places_all = group_places(block_pair[0], devices_ctx, block_size)
    valid_all = (places_all >= first_slot) & (places_all < first_slot + seq_length)
    key_places = jnp.stack([jnp.where(valid_all, places_all, 1 << 20), places_all])
    key_places = jnp.concatenate(
        [key_places[:, at : at + 64] for side in (0, 64) for at in range(side, 1024, 128)], axis=1
    )
    key_places = jnp.pad(key_places, ((0, 6), (0, 0)))
    row_places = jnp.stack([jnp.where(valid_here, places_here, -1), places_here])
    row_places = jnp.concatenate([row_places[:, :64]] * 4 + [row_places[:, 64:]] * 4, axis=1)
    cosine, sine = rope_tables((places_here - first_slot).astype(F32))
    inputs = tokens.astype(F32)
    factor_one = norm_factor(inputs)
    *arrived, units, down_rows, factor_one, order_seed = phase(
        *front, units, down_rows, factor_one, at_core
    )

    slices = pack_slice(units.reshape(-1, units.shape[2]), down_rows)
    slices = lax.all_gather(after(slices, grad_rows), SLICE_AXES, axis=0, tiled=True)
    key_part = spread(join([block[:, :split] for block in arrived]), 2)
    rest = join([block[:, split:] for block in arrived])
    orders = [row_order(place, core) for core in (0, 1)]
    mine = jnp.where(order_seed == 0, orders[0], orders[1])
    other = jnp.where(order_seed == 0, orders[1], orders[0])
    order = jnp.concatenate([mine, other])
    hot = one_hot(order)
    tokens_moved = mm(tokens, hot)
    *key_part, rest, hot, tokens_moved, order = phase(
        *key_part, rest, hot, tokens_moved, order
    )

    rest_part = spread(rest, 2)
    key_part = join(key_part)
    key_part, key_other = phase(key_part, swap_cores(key_part))

    pairs, normed, halves, gain_rows = run_kernel(
        pair_kernel,
        [
            ((devices_ctx, shard_rows, pair_cols), BF16),
            ((shard_rows, model_width), BF16),
            ((shard_rows, half), BF16),
            ((8, model_width), F32),
        ],
        (tokens_moved, factor_one, key_part, key_other, cosine, sine),
        2 * shard_rows * model_width * pair_cols,
        LARGE_BYTES,
    )
    gain_one = gain_rows[0:1]

    def project(rows, part, other_part):
        return mm(rows[:, :half], part) + mm(rows[:, half:], other_part)

    gathered = lax.all_to_all(pairs, ("y", "zh"), 0, 0, tiled=True)
    gathered = gathered.reshape(devices_ctx * shard_rows, pair_cols)
    halves = swap_cores(halves)
    hot_back = one_hot_back(order)
    gain_two = mm(gain_rows.astype(BF16), hot_back)[1:2]
    slice_places = after(jnp.asarray(slice_order()), order)
    slice_hot, slice_back = one_hot(slice_places), one_hot_back(slice_places)
    grad_places = jnp.stack(
        [
            ((at_y + step) % 4 * 2 + (at_core + side) % 2) * shard_rows
            for side in (0, 1)
            for step in range(4)
        ]
    ).astype(jnp.int32)
    (
        *rest_part,
        gathered,
        gain_two,
        halves,
        slice_hot,
        slice_back,
        hot_back,
        grad_places,
        cotangent,
        row_weight,
    ) = phase(
        *rest_part,
        gathered,
        gain_two,
        halves,
        slice_hot,
        slice_back,
        hot_back,
        grad_places,
        cotangent,
        row_weight,
    )

    query_own, query_other, normed_both, query_part, out_part = query_parts(
        normed, halves, rest_part
    )
    query_other = swap_cores(query_other)
    out_other = swap_cores(after(out_part, query_other))
    attended, queries, logs = run_kernel(
        attend_kernel,
        [((shard_rows, QUERY_WIDTH), BF16), ((shard_rows, QUERY_WIDTH), BF16), ((8, 512), F32)],
        (query_own, query_other, gathered, cosine, sine, key_places, row_places),
        shard_rows * 1024 * QUERY_WIDTH * 4,
        LARGE_BYTES,
    )
    attended_moved = mm(attended, hot).astype(BF16)
    branch = project(attended_moved, out_part, out_other)
    middle = inputs + branch
    factor_two = norm_factor(middle)
    normed_two = (middle * factor_two * gain_two).astype(BF16)
    normed_two = mm(normed_two, slice_hot).astype(BF16)
    normed_two, middle, factor_two, branch = phase(normed_two, middle, factor_two, branch)

    ahead, behind = along_y(normed_two, -1), along_y(normed_two, 1)
    cut_at = shard_rows // 2
    row_blocks = [normed_two, ahead, None, behind, swap_cores(normed_two), None, None, None]
    units_full, down_full = unpack_slices(slices)
    chunks = [None] * 4
    back_parts, ready = [None] * 4, [None] * 4
    for step in (0, 1, 3, 2):
        if step == 1:
            ahead, behind = after((ahead, behind), chunks[0][0])
            across = [along_y(ahead[:cut_at], -1), along_y(behind[cut_at:], 1)]
            row_blocks[1], row_blocks[3] = ahead, behind
        if step == 2:
            row_blocks[2] = jnp.concatenate(after(tuple(across), chunks[1][0]), axis=0)
        if step:
            row_blocks[step + 4] = swap_cores(row_blocks[step])
        block = after(row_blocks[step], ready[1], ready[3]) if step == 2 else row_blocks[step]
        chunks[step] = feed_chunk(
            step,
            block,
            row_blocks[step + 4],
            grad_rows,
            grad_places,
            units_full,
            down_full,
        )
        swapped = swap_cores(chunks[step][3])
        total = chunks[step][2].astype(F32) + swapped.astype(F32)
        ready[step] = total.astype(BF16) if step else swapped
        back_parts[step] = along_y(ready[step], step) if step else None
    terms = weight_terms(
        row_blocks[:1] + [after(block, *ready) for block in row_blocks[1:]],
        grad_rows,
        grad_places,
        chunks,
    )
    back_parts[0] = chunks[0][2]
    feed_sums = [c[4].astype(F32) + swap_cores(c[5]).astype(F32) for c in chunks]
    feed_sums = [feed_sums[0]] + [value.astype(BF16) for value in feed_sums[1:]]
    attended_swap = swap_cores(attended_moved[:, half:])
    *arrived, attended_swap, terms, own_swap = phase(
        *back_parts, *feed_sums, attended_swap, terms, ready[0]
    )
    back_parts, feed_sums = arrived[:4], arrived[4:]
    terms = lax.psum_scatter(terms, "x", scatter_dimension=0, tiled=True)

    units_here = 16 * PAD_UNITS
    feed_parts = [feed_sums[0]] + [along_y(feed_sums[step], step) for step in (1, 2, 3)]
    mid_grad, branch_grad, attended_grad = middle_call(
        (own_swap, *back_parts, cotangent, middle, factor_two, gain_two),
        (slice_back, out_part, out_other, hot_back),
    )
    branch_swap = swap_cores(branch_grad)
    attended_grad = after(attended_grad, feed_parts[1], feed_parts[3])
    query_low, pair_grads = run_kernel(
        attend_back_kernel,
        [((shard_rows, QUERY_WIDTH), BF16), ((1024, pair_cols), BF16)],
        (
            queries,
            gathered,
            attended,
            attended_grad,
            logs,
            cosine,
            sine,
            key_places,
            row_places,
        ),
        shard_rows * 1024 * QUERY_WIDTH * 10,
        LARGE_BYTES,
    )
    *feed_parts, query_low, pair_grads, mid_grad, branch_grad, branch_swap = phase(
        *feed_parts, query_low, pair_grads, mid_grad, branch_grad, branch_swap
    )

    pair_grads = lax.all_to_all(
        pair_grads.reshape(devices_ctx, shard_rows, pair_cols), ("y", "zh"), 0, 0, tiled=True
    )
    query_swap = swap_cores(query_low)
    *rest_term, query_both = run_kernel(
        term_kernel,
        [((160, 2 * QUERY_WIDTH), BF16)] * 4 + [((2 * shard_rows, QUERY_WIDTH), BF16)],
        (
            normed_both,
            query_low,
            query_swap,
            attended_moved,
            attended_swap,
            branch_grad,
            branch_swap,
        ),
        4 * half * 2 * shard_rows * QUERY_WIDTH,
        LARGE_BYTES,
    )
    rest_blocks = scatter(rest_term, 2)
    activations, sums = run_kernel(
        finish_kernel,
        [((shard_rows, model_width), BF16), ((8, 128), F32)],
        (*feed_parts, middle, branch, row_weight),
        0,
        LARGE_BYTES,
    )
    pair_grads, query_both, sums, terms = phase(pair_grads, query_both, sums, terms)
    terms = lax.psum_scatter(terms, ("zh", "zl"), scatter_dimension=0, tiled=True)

    (pair_low,) = run_kernel(
        pair_back_kernel,
        [((shard_rows, pair_cols), BF16)],
        (pair_grads, cosine, sine),
        0,
    )
    pair_both = jnp.concatenate([pair_low, swap_cores(pair_low)])
    sums_one = send(sums, lambda x, y, z, core: (x, y, z + 2, core))
    query_back = mm_nt(query_both, query_part)
    pair_both, sums, sums_one, query_back = phase(pair_both, sums, sums_one, query_back)

    normed_grad = query_back + mm_nt(pair_both, key_part[:, :pair_cols])
    pair_term = mm_tn(normed_both, pair_both)
    pair_cuts = cut(pair_term)
    pair_blocks = scatter(pair_cuts, 2)
    normed_grad_swap = swap_cores(after(normed_grad, pair_cuts[1])[shard_rows:].astype(BF16))
    normed_grad = jnp.concatenate(
        [normed_grad[:shard_rows], after(normed_grad_swap, pair_cuts[1]).astype(F32)], axis=1
    )
    input_part = norm_back(tokens_moved, factor_one, gain_one, normed_grad)
    input_grad = (mid_grad + mm(input_part.astype(BF16), hot_back)).astype(BF16)
    unit_term, down_term = unpack_slice(after(terms, pair_cuts[1]))
    unit_term = lax.all_to_all(
        unit_term.reshape(8, -1, unit_term.shape[1]), ROW_AXES, 0, 0, tiled=True
    )
    rest_total = add_up([after(rest_blocks[0], pair_cuts[1])] + rest_blocks[1:])
    sums = sums + sums_one
    sums_one = send(sums, lambda x, y, z, core: (x, y ^ 1, z, core))
    (
        *pair_blocks,
        rest_total,
        sums,
        sums_one,
        input_grad,
    ) = phase(
        *pair_blocks,
        rest_total,
        sums,
        sums_one,
        input_grad,
    )

    cuts = cut(jnp.concatenate([add_up(pair_blocks), rest_total], axis=1))
    blocks = scatter(cuts, 1)
    down_sum = swap_half_core(down_term)
    sums = sums + sums_one
    sums_one = send(sums, lambda x, y, z, core: (x, y ^ 2, z, core))
    *blocks, sums, sums_one, unit_term, down_sum = phase(
        *blocks, sums, sums_one, unit_term, down_sum
    )

    cuts = cut(add_up(blocks))
    blocks = scatter(cuts, 0)
    unit_term = after(unit_term, cuts[1]).astype(F32)
    grad_gate = unpack_units(unit_term[:, :, :units_here])
    grad_up = unpack_units(unit_term[:, :, units_here:])
    mlp_term = jnp.sum(w_gate.astype(F32) * grad_gate, axis=1)
    mlp_term = mlp_term + jnp.sum(w_up.astype(F32) * grad_up, axis=1)
    grad_mlp_gain = mlp_term / mlp_gain.astype(F32)
    down_sum = down_sum[: w_down.shape[0]].astype(F32)
    sums = sums + sums_one
    sums = sums[:3, :1].reshape(1, 3)
    seq_rms = jnp.sqrt(sums / (seq_length.astype(F32) * model_width))
    total = add_up(blocks)
    weights = jnp.concatenate([w_key, w_value, w_query], axis=1).astype(F32)
    grad_norm_gain = jnp.sum(weights * total[:, : pair_cols + QUERY_WIDTH], axis=1)
    grad_norm_gain = grad_norm_gain / norm_gain.astype(F32)
    return (
        activations,
        input_grad,
        grad_norm_gain,
        total[:, pair_cols : pair_cols + QUERY_WIDTH],
        total[:, :KEY_WIDTH],
        total[:, KEY_WIDTH:pair_cols],
        total[:, pair_cols + QUERY_WIDTH :],
        grad_mlp_gain,
        grad_gate,
        grad_up,
        down_sum,
        seq_rms,
    )


def solution(mesh):
    fine = Mesh(mesh.devices.reshape(SIZES), AXES)
    rows = P(AXES, None)
    flat = P(AXES)
    group = ("x", "zl", "core")
    in_specs = (
        (rows, flat, rows, rows, rows, rows, flat, rows, rows, rows)
        + (P(group, None), P(group), P(group))
        + (rows,)
    )
    out_specs = (rows, rows, flat, rows, rows, rows, rows, flat, rows, rows, rows, P(group, None))
    return jax.shard_map(
        local, mesh=fine, in_specs=in_specs, out_specs=out_specs, check_vma=False
    )
```

```python
import functools

import jax
import jax.numpy as jnp
import numpy as np
from jax import lax
from jax.experimental import pallas as pl
from jax.experimental.pallas import tpu as pltpu
from jax.sharding import Mesh, PartitionSpec as P

QUERY_HEADS = 20
KEY_VALUE_HEADS = 5
HEAD_WIDTH = 64
QUERY_WIDTH = QUERY_HEADS * HEAD_WIDTH
KEY_WIDTH = KEY_VALUE_HEADS * HEAD_WIDTH
GAIN_COLS = 128
KERNEL_BYTES = 20 * 1024 * 1024
LARGE_BYTES = 58 * 1024 * 1024
FEED_BYTES = 24 * 1024 * 1024
PAD_UNITS = 32

EPSILON = 1e-05
ROPE_BASE = 10000.0
MASKED_SCORE = -1e30

AXES = ("y", "zh", "x", "zl", "core")
SIZES = (4, 2, 4, 2, 2)
ROW_AXES = ("y", "core")
SLICE_AXES = ("x", "zh", "zl")
F32 = jnp.float32
BF16 = jnp.bfloat16


def device_number(x, y, z, core):
    return (((y * 2 + z // 2) * 4 + x) * 2 + z % 2) * 2 + core


def pairs_of(move):
    pairs = []
    for y in range(4):
        for z in range(4):
            for x in range(4):
                for core in range(2):
                    tx, ty, tz, tc = move(x, y, z, core)
                    pairs.append(
                        (device_number(x, y, z, core), device_number(tx % 4, ty % 4, tz % 4, tc))
                    )
    return pairs


def send(values, move):
    return lax.ppermute(values, AXES, pairs_of(move))


def swap_cores(values):
    return send(values, lambda x, y, z, core: (x, y, z, 1 - core))


def swap_half_core(values):
    return send(values, lambda x, y, z, core: (x, y, core * 2 + z % 2, z // 2))


def stage_move(stage, distance):
    def move(x, y, z, core):
        spot = [x, y, z]
        spot[(stage + core + 1) % 3] += distance
        return (spot[0], spot[1], spot[2], core)

    return move


def spread(values, stage):
    arrived = [send(values, stage_move(stage, -distance)) for distance in (1, 2, 3)]
    return [values] + arrived


def join(blocks):
    return lax.optimization_barrier(jnp.concatenate(blocks, axis=0))


def cut(total):
    low = total.astype(BF16)
    rows = low.shape[0] // 4
    return [low[step * rows : (step + 1) * rows] for step in range(4)]


def scatter(total, stage):
    parts = total if isinstance(total, list) else cut(total)
    arrived = [send(parts[step], stage_move(stage, step)) for step in (1, 2, 3)]
    return [parts[0]] + arrived


def add_up(blocks):
    total = blocks[0].astype(F32)
    for block in blocks[1:]:
        total = total + block.astype(F32)
    return total


def phase(*values):
    return lax.optimization_barrier(values)


def along_y(values, distance):
    return send(values, lambda x, y, z, core: (x, y + distance, z, core))


def gather_rows(own):
    blocks = [own] + [along_y(own, -distance) for distance in (1, 2, 3)]
    return blocks + [swap_cores(block) for block in blocks]


def add_cores(own, other):
    return [(a.astype(F32) + swap_cores(b).astype(F32)) for a, b in zip(own, other)]


def reduce_blocks(sums):
    total = sums[0]
    for distance in (1, 2, 3):
        total = total + along_y(sums[distance].astype(BF16), distance).astype(F32)
    return total


def after(values, *earlier):
    return lax.optimization_barrier((values,) + earlier)[0]


def row_order(place, core):
    third, second, first, inner = jnp.meshgrid(
        jnp.arange(4), jnp.arange(4), jnp.arange(4), jnp.arange(10), indexing="ij"
    )
    spot = list(place)
    for stage, step in enumerate((first, second, third)):
        axis = (stage + core + 1) % 3
        spot[axis] = spot[axis] + step
    sx, sy, sz = spot
    numbers = device_number(sx % 4, sy % 4, sz % 4, core) * 10 + inner
    return numbers.reshape(-1).astype(jnp.int32)


def slice_order():
    x, zh, zl, y, core, inner = np.meshgrid(
        *(np.arange(n) for n in (4, 2, 2, 4, 2, 10)), indexing="ij"
    )
    return (device_number(x, y, zh * 2 + zl, core) * 10 + inner).reshape(-1).astype(np.int32)


def one_hot_back(order):
    return (order[:, None] == jnp.arange(order.shape[0], dtype=jnp.int32)[None, :]).astype(BF16)


def one_hot(order):
    return (jnp.arange(order.shape[0], dtype=jnp.int32)[:, None] == order[None, :]).astype(BF16)


def exact_move(values, hot):
    high = values.astype(BF16)
    low = (values - high.astype(F32)).astype(BF16)
    return mm(high, hot) + mm(low, hot)


def mm(left, right):
    return jnp.dot(left, right, preferred_element_type=F32)


def mm_nt(left, right):
    return lax.dot_general(left, right, (((1,), (1,)), ((), ())), preferred_element_type=F32)


def mm_tn(left, right):
    return lax.dot_general(left, right, (((0,), (0,)), ((), ())), preferred_element_type=F32)


def norm_factor(values):
    return lax.rsqrt(jnp.mean(values * values, axis=-1, keepdims=True) + EPSILON)


def norm_back(values, factor, gain, grad):
    weighted = gain * grad
    inner = jnp.mean(weighted * values, axis=-1, keepdims=True)
    return factor * weighted - values * (factor * factor * factor) * inner


def rope_tables(angles_at):
    half_size = HEAD_WIDTH // 2
    powers = jnp.arange(half_size, dtype=F32) * (2.0 / HEAD_WIDTH)
    speeds = jnp.power(ROPE_BASE, -powers)
    angles = angles_at[:, None] * speeds[None, :]
    cosine, sine = jnp.cos(angles), jnp.sin(angles)
    return (jnp.concatenate([cosine] * 4, axis=1), jnp.concatenate([-sine, sine] * 2, axis=1))


def rotate_pairs(values, cosine, sine):
    width = values.shape[1]
    half_size = HEAD_WIDTH // 2
    lanes = lax.broadcasted_iota(jnp.int32, values.shape, 1) % HEAD_WIDTH
    ahead = pltpu.roll(values, width - half_size, 1)
    behind = pltpu.roll(values, half_size, 1)
    return values * cosine + jnp.where(lanes < half_size, ahead, behind) * sine


def wide_table(table, width):
    return jnp.concatenate([table] * (width // table.shape[1]), axis=1)


def low_high(rows):
    low = [rows[at : at + 64] for at in range(0, rows.shape[0], 128)]
    high = [rows[at + 64 : at + 128] for at in range(0, rows.shape[0], 128)]
    return jnp.concatenate(low, axis=0), jnp.concatenate(high, axis=0)


def stack_heads(rows, head):
    pieces = [
        rows[at : at + 64, (4 * head + step) * HEAD_WIDTH : (4 * head + step + 1) * HEAD_WIDTH]
        for at in (0, 64)
        for step in range(4)
    ]
    return jnp.concatenate(pieces, axis=0)


def unstack_heads(stack):
    halves = [
        jnp.concatenate([stack[at + 64 * step : at + 64 * step + 64] for step in range(4)], axis=1)
        for at in (0, 256)
    ]
    return jnp.concatenate(halves, axis=0)


def mask_bias(keys_ref, rows_ref):
    columns = keys_ref[...].T
    keys_low, keys_high = columns[:512], columns[512:]

    def bias(keys, lanes):
        seen = (keys[:, 0:1] <= rows_ref[0:1, lanes]) | (keys[:, 1:2] == rows_ref[1:2, lanes])
        return jnp.where(seen, 0.0, MASKED_SCORE).astype(F32)

    return bias(keys_low, slice(0, 512)), bias(keys_high, slice(256, 512))


def attend_kernel(q_ref, part_ref, kv_ref, cos_ref, sin_ref, keys_ref, rows_ref, out_ref, turned_ref, log_ref):
    cosine = wide_table(cos_ref[...], QUERY_WIDTH)
    sine = wide_table(sin_ref[...], QUERY_WIDTH)
    queries = q_ref[...] + part_ref[...].astype(F32)
    queries = (rotate_pairs(queries, cosine, sine) * HEAD_WIDTH**-0.5).astype(BF16)
    turned_ref[...] = queries
    kv_low, kv_high = low_high(kv_ref[...])
    bias_low, bias_high = mask_bias(keys_ref, rows_ref)
    for head in range(KEY_VALUE_HEADS):
        at = slice(head * HEAD_WIDTH, (head + 1) * HEAD_WIDTH)
        vat = slice(KEY_WIDTH + head * HEAD_WIDTH, KEY_WIDTH + (head + 1) * HEAD_WIDTH)
        stack = stack_heads(queries, head)
        score_low = mm_nt(kv_low[:, at], stack) + bias_low
        score_high = mm_nt(kv_high[:, at], stack[256:]) + bias_high
        top_low = jnp.max(score_low, axis=0, keepdims=True)
        top_high = jnp.max(score_high, axis=0, keepdims=True)
        top = jnp.concatenate(
            [top_low[:, :256], jnp.maximum(top_low[:, 256:], top_high)], axis=1
        )
        exp_low = jnp.exp(score_low - top)
        exp_high = jnp.exp(score_high - top[:, 256:])
        total = jnp.sum(exp_low, axis=0, keepdims=True)
        total_high = jnp.sum(exp_high, axis=0, keepdims=True)
        total = jnp.concatenate([total[:, :256], total[:, 256:] + total_high], axis=1)
        result = mm_tn(kv_low[:, vat], exp_low.astype(BF16))
        result_high = mm_tn(kv_high[:, vat], exp_high.astype(BF16))
        result = jnp.concatenate([result[:, :256], result[:, 256:] + result_high], axis=1)
        result = (result / total).T
        out_ref[:, head * 256 : (head + 1) * 256] = unstack_heads(result).astype(BF16)
        log_ref[head : head + 1, :] = top + jnp.log(total)


def attend_back_kernel(
    q_ref, kv_ref, out_ref, grad_ref, log_ref, cos_ref, sin_ref, keys_ref, rows_ref, dq_ref, dkv_ref
):
    kv_low, kv_high = low_high(kv_ref[...])
    bias_low, bias_high = mask_bias(keys_ref, rows_ref)
    queries = q_ref[...]
    outs = out_ref[...]
    grads = grad_ref[...]
    ones = jnp.ones((8, HEAD_WIDTH), F32)
    dq_parts, dk_low, dk_high, dv_low, dv_high = [], [], [], [], []
    for head in range(KEY_VALUE_HEADS):
        at = slice(head * HEAD_WIDTH, (head + 1) * HEAD_WIDTH)
        vat = slice(KEY_WIDTH + head * HEAD_WIDTH, KEY_WIDTH + (head + 1) * HEAD_WIDTH)
        stack = stack_heads(queries, head)
        grad = stack_heads(grads, head)
        product = grad.astype(F32) * stack_heads(outs, head).astype(F32)
        delta = lax.dot_general(
            ones,
            product,
            (((1,), (1,)), ((), ())),
            preferred_element_type=F32,
            precision=lax.Precision.HIGHEST,
        )[0:1]
        logs = log_ref[head : head + 1, :]
        key_low, key_high = kv_low[:, at], kv_high[:, at]
        probs_low = jnp.exp(mm_nt(key_low, stack) + bias_low - logs)
        probs_high = jnp.exp(mm_nt(key_high, stack[256:]) + bias_high - logs[:, 256:])
        back_low = mm_nt(kv_low[:, vat], grad)
        back_high = mm_nt(kv_high[:, vat], grad[256:])
        score_low = (probs_low * (back_low - delta)).astype(BF16)
        score_high = (probs_high * (back_high - delta[:, 256:])).astype(BF16)
        dv_low.append(mm(probs_low.astype(BF16), grad))
        dv_high.append(mm(probs_high.astype(BF16), grad[256:]))
        dk_low.append(mm(score_low, stack))
        dk_high.append(mm(score_high, stack[256:]))
        dq = mm_tn(key_low, score_low)
        dq_high = mm_tn(key_high, score_high)
        dq = jnp.concatenate([dq[:, :256], dq[:, 256:] + dq_high], axis=1)
        dq_parts.append(unstack_heads((dq * HEAD_WIDTH**-0.5).T))
    cosine = wide_table(cos_ref[...], QUERY_WIDTH)
    sine = wide_table(sin_ref[...], QUERY_WIDTH)
    dq_ref[...] = rotate_pairs(jnp.concatenate(dq_parts, axis=1), cosine, -sine).astype(BF16)
    low = jnp.concatenate(dk_low + dv_low, axis=1).astype(BF16)
    high = jnp.concatenate(dk_high + dv_high, axis=1).astype(BF16)
    for at in range(8):
        dkv_ref[128 * at : 128 * at + 64] = low[64 * at : 64 * at + 64]
        dkv_ref[128 * at + 64 : 128 * at + 128] = high[64 * at : 64 * at + 64]


def run_kernel(kernel, shapes, operands, flops, limit=KERNEL_BYTES):
    return pl.pallas_call(
        kernel,
        out_shape=[jax.ShapeDtypeStruct(shape, kind) for shape, kind in shapes],
        in_specs=[pl.BlockSpec(memory_space=pltpu.VMEM)] * len(operands),
        out_specs=[pl.BlockSpec(memory_space=pltpu.VMEM)] * len(shapes),
        compiler_params=pltpu.CompilerParams(vmem_limit_bytes=limit),
        cost_estimate=pl.CostEstimate(
            flops=flops,
            bytes_accessed=sum(v.size * v.dtype.itemsize for v in operands),
            transcendentals=0,
        ),
    )(*operands)


def pair_kernel(
    moved_ref,
    factor_ref,
    part_ref,
    other_ref,
    cos_ref,
    sin_ref,
    pairs_ref,
    normed_ref,
    halves_ref,
    gains_ref,
):
    half = part_ref.shape[0]
    pair_cols = 2 * KEY_WIDTH
    gains = [ref[:, pair_cols:].astype(F32).T[:8] for ref in (part_ref, other_ref)]
    gains = jnp.concatenate(gains, axis=1)
    gains_ref[...] = gains
    scaled = moved_ref[...] * factor_ref[...]
    normed = (scaled * gains[0:1]).astype(BF16)
    normed_ref[...] = normed
    halves_ref[...] = normed[:, half:]
    both = mm(normed[:, :half], part_ref[:, :pair_cols]) + mm(
        normed[:, half:], other_ref[:, :pair_cols]
    )
    wide = 3 * cos_ref.shape[1]
    turned = rotate_pairs(
        both[:, :wide], wide_table(cos_ref[...], wide), wide_table(sin_ref[...], wide)
    )
    pairs = jnp.concatenate([turned[:, :KEY_WIDTH], both[:, KEY_WIDTH:]], axis=1).astype(BF16)
    for at in range(8):
        pairs_ref[at] = pairs


def pair_back_kernel(parts_ref, cos_ref, sin_ref, low_ref):
    total = parts_ref[0].astype(F32)
    for at in range(1, 8):
        total = total + parts_ref[at].astype(F32)
    wide = 3 * cos_ref.shape[1]
    turned = rotate_pairs(
        total[:, :wide], wide_table(cos_ref[...], wide), -wide_table(sin_ref[...], wide)
    )
    low_ref[...] = jnp.concatenate(
        [turned[:, :KEY_WIDTH], total[:, KEY_WIDTH:]], axis=1
    ).astype(BF16)


def middle_kernel(
    own_swap,
    back_a,
    back_b,
    back_c,
    back_d,
    cot_ref,
    weight_ref,
    middle_ref,
    factor_ref,
    gain_ref,
    hot_slice_ref,
    part_ref,
    other_ref,
    hot_ref,
    mid_ref,
    branch_ref,
    grad_ref,
    hot_slice,
    parts,
    hot,
    sems,
):
    half = part_ref.shape[0]
    copies = [
        pltpu.make_async_copy(hot_slice_ref, hot_slice, sems.at[0]),
        pltpu.make_async_copy(part_ref, parts.at[0:half], sems.at[1]),
        pltpu.make_async_copy(other_ref, parts.at[half : 2 * half], sems.at[2]),
        pltpu.make_async_copy(hot_ref, hot, sems.at[3]),
    ]
    for copy in copies:
        copy.start()
    total = own_swap[...].astype(F32) + back_a[...].astype(F32) + back_b[...].astype(F32)
    total = total + back_c[...].astype(F32)
    total = (total + back_d[...].astype(F32)).astype(BF16)
    copies[0].wait()
    grad = mm(total, hot_slice[...])
    middle, factor = middle_ref[...], factor_ref[...]
    mid = cot_ref[...].astype(F32) * weight_ref[...] + norm_back(middle, factor, gain_ref[...], grad)
    mid_ref[...] = mid
    branch = mid.astype(BF16)
    branch_ref[...] = branch
    copies[1].wait()
    copies[2].wait()
    moved = mm_nt(branch, parts[...]).astype(BF16)
    copies[3].wait()
    grad_ref[...] = mm(moved, hot[...]).astype(BF16)


def middle_call(small, large):
    vmem, hbm = pl.BlockSpec(memory_space=pltpu.VMEM), pl.BlockSpec(memory_space=pltpu.HBM)
    rows, width = small[0].shape
    square = pltpu.VMEM((width, width), BF16)
    return pl.pallas_call(
        middle_kernel,
        out_shape=[jax.ShapeDtypeStruct((rows, width), kind) for kind in (F32, BF16, BF16)],
        in_specs=[vmem] * len(small) + [hbm] * len(large),
        out_specs=[vmem] * 3,
        scratch_shapes=[square, square, square, pltpu.SemaphoreType.DMA((4,))],
        compiler_params=pltpu.CompilerParams(vmem_limit_bytes=LARGE_BYTES),
        cost_estimate=pl.CostEstimate(
            flops=6 * rows * width * width, bytes_accessed=16 * 2**20, transcendentals=0
        ),
    )(*small, *large)


def finish_kernel(
    feed_a, feed_b, feed_c, feed_d, middle_ref, branch_ref, weight_ref, out_ref, sums_ref
):
    feed = feed_a[...].astype(F32) + feed_b[...].astype(F32) + feed_c[...].astype(F32)
    feed = feed + feed_d[...].astype(F32)
    final = middle_ref[...] + feed
    out_ref[...] = final.astype(BF16)
    sums_ref[...] = jnp.zeros(sums_ref.shape, F32)
    for row, values in enumerate((branch_ref[...], feed, final)):
        part = jnp.sum(weight_ref[...] * values * values, axis=0, keepdims=True)
        part = jnp.sum(part, axis=1, keepdims=True)
        sums_ref[row : row + 1] = jnp.broadcast_to(part, (1, 128))


def query_kernel(
    normed_ref,
    halves_ref,
    a_ref,
    b_ref,
    c_ref,
    d_ref,
    own_ref,
    other_ref,
    both_ref,
    query_ref,
    out_ref,
    sems,
):
    width, count = query_ref.shape[1], a_ref.shape[0]
    copies = []
    for step, block in enumerate((a_ref, b_ref, c_ref, d_ref)):
        at = slice(step * count, (step + 1) * count)
        copies.append(
            pltpu.make_async_copy(block.at[:, 0:width], query_ref.at[at], sems.at[step])
        )
    for step, block in enumerate((a_ref, b_ref, c_ref, d_ref)):
        at = slice(step * count, (step + 1) * count)
        copies.append(
            pltpu.make_async_copy(
                block.at[:, width : 2 * width], out_ref.at[at], sems.at[4 + step]
            )
        )
    for copy in copies:
        copy.start()
    for copy in copies[:4]:
        copy.wait()
    half = own_ref.shape[0]
    both_ref[0:half] = normed_ref[:, : both_ref.shape[1]]
    both_ref[half : 2 * half] = halves_ref[...]
    both = mm(both_ref[...], query_ref[...])
    own_ref[...] = both[:half]
    other_ref[...] = both[half:].astype(BF16)
    for copy in copies[4:]:
        copy.wait()


def query_parts(normed, halves, blocks):
    vmem = pl.BlockSpec(memory_space=pltpu.VMEM)
    half, width = normed.shape[0], QUERY_WIDTH
    joined = jax.ShapeDtypeStruct((4 * blocks[0].shape[0], width), BF16)
    return pl.pallas_call(
        query_kernel,
        out_shape=[
            jax.ShapeDtypeStruct((half, width), F32),
            jax.ShapeDtypeStruct((half, width), BF16),
            jax.ShapeDtypeStruct((2 * half, halves.shape[1]), BF16),
            joined,
            joined,
        ],
        in_specs=[vmem] * 2 + [pl.BlockSpec(memory_space=pltpu.HBM)] * 4,
        out_specs=[vmem] * 5,
        scratch_shapes=[pltpu.SemaphoreType.DMA((8,))],
        compiler_params=pltpu.CompilerParams(vmem_limit_bytes=LARGE_BYTES),
        cost_estimate=pl.CostEstimate(
            flops=4 * halves.size * width, bytes_accessed=10 * 2**20, transcendentals=0
        ),
    )(normed, halves, *blocks)


def unpack_kernel(slices_ref, units_ref, down_ref):
    for block in range(16):
        base, at = block * 128, block * 32
        units_ref[block * 80 : block * 80 + 80] = slices_ref[base : base + 80]
        down_ref[at : at + 32, :1024] = slices_ref[base + 80 : base + 112]
        down_ref[at : at + 16, 1024:] = slices_ref[base + 112 : base + 128, :256]
        down_ref[at + 16 : at + 32, 1024:] = slices_ref[base + 112 : base + 128, 256:512]


def unpack_slices(slices):
    return run_kernel(
        unpack_kernel, [((1280, 1024), BF16), ((512, 1280), BF16)], (slices,), 0, FEED_BYTES
    )


def feed_kernel(
    xa_ref,
    xb_ref,
    all_grads_ref,
    places_ref,
    valid_ref,
    units_ref,
    down_ref,
    hidden_ref,
    unit_ref,
    back_a_ref,
    back_b_ref,
    out_a_ref,
    out_b_ref,
    rows_ref,
    grads_ref,
    sems,
    *,
    step,
):
    half = xa_ref.shape[0]
    low = slice(0, half)
    high = slice(half, 2 * half)
    spot_a = pl.ds(pl.multiple_of(places_ref[step], half), half)
    spot_b = pl.ds(pl.multiple_of(places_ref[step + 4], half), half)
    copies = [
        pltpu.make_async_copy(xa_ref, rows_ref.at[low], sems.at[0]),
        pltpu.make_async_copy(xb_ref, rows_ref.at[high], sems.at[1]),
    ]
    copies += [
        pltpu.make_async_copy(all_grads_ref.at[spot_a], grads_ref.at[low], sems.at[2]),
        pltpu.make_async_copy(all_grads_ref.at[spot_b], grads_ref.at[high], sems.at[3]),
    ]
    for copy in copies:
        copy.start()
    copies[0].wait()
    copies[1].wait()
    units = units_ref.shape[1] // 2
    both = mm(rows_ref[...], units_ref[...])
    gate, up = both[:, :units], both[:, units:]
    sigmoid = 1.0 / (1.0 + jnp.exp(-gate))
    silu = gate * sigmoid
    hidden = silu * up
    columns = valid_ref[...].T
    valid = jnp.concatenate(
        [columns[:, step : step + 1], columns[:, step + 4 : step + 5]], axis=0
    )
    hidden_ref[...] = (hidden * valid).astype(BF16)
    hidden = hidden.astype(BF16)
    for copy in copies[2:]:
        copy.wait()
    hidden_grad = mm_nt(grads_ref[...], down_ref[...]) * valid
    gate_low = (hidden_grad * up * sigmoid * (1.0 + gate * (1.0 - sigmoid))).astype(BF16)
    up_low = (hidden_grad * silu).astype(BF16)
    unit = jnp.concatenate([gate_low, up_low], axis=1)
    unit_ref[...] = unit
    back = mm_nt(unit, units_ref[...]).astype(BF16)
    back_a_ref[...] = back[:half]
    back_b_ref[...] = back[half:]
    outs = mm(hidden, down_ref[...]).astype(BF16)
    out_a_ref[...] = outs[:half]
    out_b_ref[...] = outs[half:]


def feed_chunk(step, rows_a, rows_b, all_grads, places, valid, units, down):
    count, width = rows_a.shape[0] * 2, rows_a.shape[1]
    vmem = pl.BlockSpec(memory_space=pltpu.VMEM)
    hbm = pl.BlockSpec(memory_space=pltpu.HBM)
    shapes = [(count, 512), (count, 1024)] + [rows_a.shape] * 4
    return pl.pallas_call(
        functools.partial(feed_kernel, step=step),
        out_shape=[jax.ShapeDtypeStruct(shape, BF16) for shape in shapes],
        in_specs=[hbm] * 3 + [pl.BlockSpec(memory_space=pltpu.SMEM)] + [vmem] * 3,
        out_specs=[vmem] * 6,
        scratch_shapes=[
            pltpu.VMEM((count, width), BF16),
            pltpu.VMEM((count, width), BF16),
            pltpu.SemaphoreType.DMA((4,)),
        ],
        compiler_params=pltpu.CompilerParams(vmem_limit_bytes=FEED_BYTES),
        cost_estimate=pl.CostEstimate(
            flops=2 * count * width * 3 * 1024,
            bytes_accessed=2 * (units.size + down.size + 4 * rows_a.size),
            transcendentals=0,
        ),
    )(rows_a, rows_b, all_grads, places, valid, units, down)


def weight_kernel(*refs):
    sources, all_grads, places, term_out = refs[:24], refs[24], refs[25], refs[26]
    feed_outs = refs[27:31]
    grads, terms, in_sems, out_sems = refs[31:]
    copies = []
    for step in range(4):
        base = step * 256
        for place, start in ((step, base), (step + 4, base + 128)):
            spot = pl.ds(pl.multiple_of(places[place], 128), 128)
            copies.append(
                pltpu.make_async_copy(
                    all_grads.at[spot], grads.at[start : start + 128], in_sems.at[len(copies)]
                )
            )
    for copy in copies:
        copy.start()
    for step in range(4):
        total = sources[step + 16][...].astype(F32) + sources[step + 20][...].astype(F32)
        feed_outs[step][...] = total.astype(BF16)
    for at in range(0, 16, 4):
        lanes = slice(at * 80, at * 80 + 320)
        total = None
        for step in range(4):
            pair = jnp.concatenate([sources[step][:, lanes], sources[step + 4][:, lanes]], axis=0)
            term = mm_tn(pair, sources[step + 12][...])
            total = term if total is None else total + term
        total = total.astype(BF16)
        for step in range(4):
            base = (at + step) * 128
            terms[base : base + 80] = total[step * 80 : step * 80 + 80]
    for copy in copies:
        copy.wait()
    hidden = jnp.concatenate([sources[step + 8][...] for step in range(4)], axis=0)
    moves = []
    for at in range(0, 16, 4):
        total = mm_tn(hidden[:, at * 32 : at * 32 + 128], grads[...]).astype(BF16)
        for step in range(4):
            rows_here = total[step * 32 : step * 32 + 32]
            base = (at + step) * 128
            terms[base + 80 : base + 112] = rows_here[:, :1024]
            terms[base + 112 : base + 128, 0:256] = rows_here[:16, 1024:]
            terms[base + 112 : base + 128, 256:512] = rows_here[16:, 1024:]
            terms[base + 112 : base + 128, 512:] = jnp.zeros((16, 512), BF16)
        piece = slice(at * 128, at * 128 + 512)
        moves.append(
            pltpu.make_async_copy(terms.at[piece], term_out.at[piece], out_sems.at[at // 4])
        )
        moves[-1].start()
    for move in moves:
        move.wait()


def weight_terms(rows, all_grads, places, chunks, feed_swaps):
    sources = list(rows)
    for part in (0, 1, 4):
        sources += [chunk[part] for chunk in chunks]
    sources += list(feed_swaps)
    count, width = 8 * rows[0].shape[0], rows[0].shape[1]
    smem, hbm = pl.BlockSpec(memory_space=pltpu.SMEM), pl.BlockSpec(memory_space=pltpu.HBM)
    return pl.pallas_call(
        weight_kernel,
        out_shape=[jax.ShapeDtypeStruct((2048, 1024), BF16)]
        + [jax.ShapeDtypeStruct(rows[0].shape, BF16)] * 4,
        in_specs=[pl.BlockSpec(memory_space=pltpu.VMEM)] * 24 + [hbm, smem],
        out_specs=[hbm] + [pl.BlockSpec(memory_space=pltpu.VMEM)] * 4,
        scratch_shapes=[
            pltpu.VMEM((count, width), BF16),
            pltpu.VMEM((2048, 1024), BF16),
            pltpu.SemaphoreType.DMA((8,)),
            pltpu.SemaphoreType.DMA((4,)),
        ],
        compiler_params=pltpu.CompilerParams(vmem_limit_bytes=24 * 1024 * 1024),
        cost_estimate=pl.CostEstimate(
            flops=2 * count * 1280 * 1536, bytes_accessed=2**20, transcendentals=0
        ),
    )(*sources, all_grads, places)


def term_kernel(normed_ref, q_ref, qs_ref, attended_ref, as_ref, b_ref, bs_ref, *outs):
    count = outs[0].shape[0]
    half = normed_ref.shape[1]
    queries = jnp.concatenate([q_ref[...], qs_ref[...]], axis=0)
    outs[4][...] = queries
    branch = jnp.concatenate([b_ref[...], bs_ref[...]], axis=0)
    attended = jnp.concatenate([attended_ref[:, :half], as_ref[...]], axis=0)
    query_term = mm_tn(normed_ref[...], queries).astype(BF16)
    out_term = mm_tn(attended, branch).astype(BF16)
    for step in range(4):
        at = slice(step * count, (step + 1) * count)
        outs[step][:, :QUERY_WIDTH] = query_term[at]
        outs[step][:, QUERY_WIDTH:] = out_term[at]


def pack_slice(units, down):
    rest = jnp.concatenate([down[:16, 1024:], down[16:, 1024:]], axis=1)
    rest = jnp.pad(rest, ((0, 0), (0, 512)))
    return jnp.concatenate([units, down[:, :1024], rest], axis=0)


def unpack_down(rows):
    rest = jnp.concatenate([rows[32:, :256], rows[32:, 256:512]], axis=0)
    return jnp.concatenate([rows[:32], rest], axis=1)


def group_places(pair_row, devices_ctx, block_size):
    slots = jnp.arange(devices_ctx * 2 * block_size, dtype=jnp.int32)
    owners = slots // (2 * block_size)
    inside = slots % (2 * block_size)
    columns = jnp.arange(devices_ctx, dtype=jnp.int32)
    paired = jnp.sum(jnp.where(owners[:, None] == columns[None, :], pair_row[None, :], 0), axis=1)
    blocks = jnp.where(inside < block_size, paired, 2 * devices_ctx - 1 - paired)
    return blocks * block_size + inside % block_size


def pack_units(weight):
    rows = weight.shape[0]
    runs = weight.reshape(rows, 8, 4, 2, 2, 28).transpose(1, 0, 2, 4, 3, 5)
    runs = jnp.pad(runs, ((0, 0),) * 5 + ((0, PAD_UNITS - 28),))
    return runs.reshape(8, rows, 16 * PAD_UNITS)


def unpack_units(packed):
    rows = packed.shape[1]
    runs = packed.reshape(8, rows, 4, 2, 2, PAD_UNITS)[..., :28]
    return runs.transpose(1, 0, 2, 4, 3, 5).reshape(rows, 8 * 16 * 28)


def local(
    tokens,
    norm_gain,
    w_query,
    w_key,
    w_value,
    w_out,
    mlp_gain,
    w_gate,
    w_up,
    w_down,
    block_pair,
    seq_len,
    seq_start,
    out_grad,
):
    shard_rows, model_width = tokens.shape
    block_size = shard_rows // 2
    half = model_width // 2
    devices_ctx = 8
    at_y, at_zh, at_x, at_zl, at_core = (lax.axis_index(name) for name in AXES)
    place = (at_x, at_y, at_zh * 2 + at_zl)
    position = at_y * 2 + at_zh
    pair_cols = 2 * KEY_WIDTH
    split = pair_cols + GAIN_COLS

    first_slot = seq_start[0]
    seq_length = seq_len[0]
    grad_rows = lax.all_gather(out_grad, ROW_AXES, axis=0, tiled=True)
    gains = jnp.stack([norm_gain, mlp_gain], axis=1)
    gains = jnp.pad(gains, ((0, 0), (0, GAIN_COLS - 2)))
    front = jnp.concatenate([w_key, w_value, gains, w_query, w_out], axis=1)
    front = spread(front, 0)
    units = jnp.concatenate([pack_units(w_gate), pack_units(w_up)], axis=2)
    *arrived, units, tokens, block_pair, out_grad = phase(
        *front, units, tokens, block_pair, out_grad
    )

    front = spread(join(arrived), 1)
    units = lax.all_to_all(units, ROW_AXES, 0, 0, tiled=True)
    down_rows = jnp.pad(w_down, ((0, PAD_UNITS - w_down.shape[0]), (0, 0)))
    down_rows = swap_half_core(after(down_rows, block_pair))
    places_all = group_places(block_pair[0], devices_ctx, block_size)
    places_here = lax.dynamic_slice_in_dim(places_all, position * shard_rows, shard_rows)
    valid_here = (places_here >= first_slot) & (places_here < first_slot + seq_length)
    row_weight = valid_here.astype(F32)[:, None]
    valid_all = (places_all >= first_slot) & (places_all < first_slot + seq_length)
    ring_valid = valid_all.astype(F32).reshape(4, 2, shard_rows)
    ring_valid = lax.dynamic_index_in_dim(ring_valid, at_zh, 1, keepdims=False)
    ring_valid = lax.dynamic_slice_in_dim(
        jnp.concatenate([ring_valid, ring_valid]), at_y, 4, axis=0
    )
    ring_valid = jnp.concatenate([ring_valid, swap_cores(ring_valid)])
    key_places = jnp.stack([jnp.where(valid_all, places_all, 1 << 20), places_all])
    key_places = jnp.concatenate(
        [key_places[:, at : at + 64] for side in (0, 64) for at in range(side, 1024, 128)], axis=1
    )
    key_places = jnp.pad(key_places, ((0, 6), (0, 0)))
    row_places = jnp.stack([jnp.where(valid_here, places_here, -1), places_here])
    row_places = jnp.concatenate([row_places[:, :64]] * 4 + [row_places[:, 64:]] * 4, axis=1)
    cosine, sine = rope_tables((places_here - first_slot).astype(F32))
    inputs = tokens.astype(F32)
    factor_one = norm_factor(inputs)
    *arrived, factor_one, order_seed = phase(*front, factor_one, at_core)

    key_part = join([block[:, :split] for block in arrived])
    units, down_rows = after((units, down_rows), key_part)
    slices = pack_slice(units.reshape(-1, units.shape[2]), down_rows)
    slices = lax.all_gather(after(slices, grad_rows), SLICE_AXES, axis=0, tiled=True)
    key_part = spread(key_part, 2)
    rest = join([block[:, split:] for block in arrived])
    orders = [row_order(place, core) for core in (0, 1)]
    mine = jnp.where(order_seed == 0, orders[0], orders[1])
    other = jnp.where(order_seed == 0, orders[1], orders[0])
    order = jnp.concatenate([mine, other])
    hot = one_hot(order)
    tokens_moved = mm(tokens, hot)
    *key_part, rest, hot, tokens_moved, order = phase(
        *key_part, rest, hot, tokens_moved, order
    )

    rest_part = spread(rest, 2)
    key_part = join(key_part)
    key_part, key_other = phase(key_part, swap_cores(key_part))

    pairs, normed, halves, gain_rows = run_kernel(
        pair_kernel,
        [
            ((devices_ctx, shard_rows, pair_cols), BF16),
            ((shard_rows, model_width), BF16),
            ((shard_rows, half), BF16),
            ((8, model_width), F32),
        ],
        (tokens_moved, factor_one, key_part, key_other, cosine, sine),
        2 * shard_rows * model_width * pair_cols,
        LARGE_BYTES,
    )
    gain_one = gain_rows[0:1]

    def project(rows, part, other_part):
        return mm(rows[:, :half], part) + mm(rows[:, half:], other_part)

    gathered = lax.all_to_all(pairs, ("y", "zh"), 0, 0, tiled=True)
    gathered = gathered.reshape(devices_ctx * shard_rows, pair_cols)
    halves = swap_cores(halves)
    hot_back = one_hot_back(order)
    gain_two = mm(gain_rows.astype(BF16), hot_back)[1:2]
    slice_places = after(jnp.asarray(slice_order()), order)
    slice_hot, slice_back = one_hot(slice_places), one_hot_back(slice_places)
    grad_places = jnp.stack(
        [
            ((at_y + step) % 4 * 2 + (at_core + side) % 2) * shard_rows
            for side in (0, 1)
            for step in range(4)
        ]
    ).astype(jnp.int32)
    (
        *rest_part,
        gathered,
        gain_two,
        halves,
        slice_hot,
        slice_back,
        hot_back,
        grad_places,
        ring_valid,
        row_weight,
    ) = phase(
        *rest_part,
        gathered,
        gain_two,
        halves,
        slice_hot,
        slice_back,
        hot_back,
        grad_places,
        ring_valid,
        row_weight,
    )

    query_own, query_other, normed_both, query_part, out_part = query_parts(
        normed, halves, rest_part
    )
    query_other = swap_cores(query_other)
    out_other = swap_cores(after(out_part, query_other))
    attended, queries, logs = run_kernel(
        attend_kernel,
        [((shard_rows, QUERY_WIDTH), BF16), ((shard_rows, QUERY_WIDTH), BF16), ((8, 512), F32)],
        (query_own, query_other, gathered, cosine, sine, key_places, row_places),
        shard_rows * 1024 * QUERY_WIDTH * 4,
        LARGE_BYTES,
    )
    attended_moved = mm(attended, hot).astype(BF16)
    branch = project(attended_moved, out_part, out_other)
    middle = inputs + branch
    factor_two = norm_factor(middle)
    normed_two = (middle * factor_two * gain_two).astype(BF16)
    normed_two = mm(normed_two, slice_hot).astype(BF16)
    normed_two, middle, factor_two, branch = phase(normed_two, middle, factor_two, branch)

    ahead, behind = along_y(normed_two, -1), along_y(normed_two, 1)
    cut_at = shard_rows // 2
    row_blocks = [normed_two, ahead, None, behind, swap_cores(normed_two), None, None, None]
    units_full, down_full = unpack_slices(slices)
    chunks = [None] * 4
    back_parts, ready, feed_swaps = [None] * 4, [None] * 4, [None] * 4
    for step in (0, 1, 3, 2):
        if step == 1:
            ahead, behind = after((ahead, behind), chunks[0][0])
            across = [along_y(ahead[:cut_at], -1), along_y(behind[cut_at:], 1)]
            row_blocks[1], row_blocks[3] = ahead, behind
        if step == 2:
            row_blocks[2] = jnp.concatenate(after(tuple(across), chunks[1][0]), axis=0)
        if step:
            row_blocks[step + 4] = swap_cores(row_blocks[step])
        block = after(row_blocks[step], ready[1], ready[3]) if step == 2 else row_blocks[step]
        chunks[step] = feed_chunk(
            step,
            block,
            row_blocks[step + 4],
            grad_rows,
            grad_places,
            ring_valid,
            units_full,
            down_full,
        )
        swapped = swap_cores(chunks[step][3])
        feed_swaps[step] = swap_cores(chunks[step][5])
        total = chunks[step][2].astype(F32) + swapped.astype(F32)
        ready[step] = total.astype(BF16) if step else swapped
        back_parts[step] = along_y(ready[step], step) if step else None
    terms, *feed_sums = weight_terms(
        row_blocks[:1] + [after(block, *ready) for block in row_blocks[1:]],
        grad_rows,
        grad_places,
        chunks,
        feed_swaps,
    )
    back_parts[0] = chunks[0][2]
    attended_swap = swap_cores(attended_moved[:, half:])
    *arrived, attended_swap, terms, own_swap = phase(
        *back_parts, *feed_sums, attended_swap, terms, ready[0]
    )
    back_parts, feed_sums = arrived[:4], arrived[4:]
    terms = lax.psum_scatter(terms, "x", scatter_dimension=0, tiled=True)

    units_here = 16 * PAD_UNITS
    feed_parts = [feed_sums[0]] + [along_y(feed_sums[step], step) for step in (1, 2, 3)]
    mid_grad, branch_grad, attended_grad = middle_call(
        (own_swap, *back_parts, out_grad, row_weight, middle, factor_two, gain_two),
        (slice_back, out_part, out_other, hot_back),
    )
    branch_swap = swap_cores(branch_grad)
    attended_grad = after(attended_grad, feed_parts[1])
    query_low, pair_grads = run_kernel(
        attend_back_kernel,
        [((shard_rows, QUERY_WIDTH), BF16), ((1024, pair_cols), BF16)],
        (
            queries,
            gathered,
            attended,
            attended_grad,
            logs,
            cosine,
            sine,
            key_places,
            row_places,
        ),
        shard_rows * 1024 * QUERY_WIDTH * 10,
        LARGE_BYTES,
    )
    *feed_parts, query_low, pair_grads, mid_grad, branch_grad, branch_swap = phase(
        *feed_parts, query_low, pair_grads, mid_grad, branch_grad, branch_swap
    )

    pair_grads = lax.all_to_all(
        pair_grads.reshape(devices_ctx, shard_rows, pair_cols), ("y", "zh"), 0, 0, tiled=True
    )
    query_swap = swap_cores(query_low)
    *rest_term, query_both = run_kernel(
        term_kernel,
        [((160, 2 * QUERY_WIDTH), BF16)] * 4 + [((2 * shard_rows, QUERY_WIDTH), BF16)],
        (
            normed_both,
            query_low,
            query_swap,
            attended_moved,
            attended_swap,
            branch_grad,
            branch_swap,
        ),
        4 * half * 2 * shard_rows * QUERY_WIDTH,
        LARGE_BYTES,
    )
    rest_blocks = scatter(rest_term, 2)
    activations, sums = run_kernel(
        finish_kernel,
        [((shard_rows, model_width), BF16), ((8, 128), F32)],
        (*feed_parts, middle, branch, row_weight),
        0,
        LARGE_BYTES,
    )
    sums_one = send(sums, lambda x, y, z, core: (x, y, z + 2, core))
    pair_grads, query_both, sums, sums_one, terms = phase(
        pair_grads, query_both, sums, sums_one, terms
    )
    terms = terms.reshape(4, 128, terms.shape[1])
    unit_parts = lax.all_to_all(
        terms[:, :80].reshape(32, 10, terms.shape[2]), ("zh", "zl", "y", "core"), 0, 0, tiled=True
    )
    down_term = lax.psum_scatter(
        terms[:, 80:].reshape(192, terms.shape[2]), ("zh", "zl"), scatter_dimension=0, tiled=True
    )

    (pair_low,) = run_kernel(
        pair_back_kernel,
        [((shard_rows, pair_cols), BF16)],
        (pair_grads, cosine, sine),
        0,
    )
    pair_both = jnp.concatenate([pair_low, swap_cores(pair_low)])
    query_back = mm_nt(query_both, query_part)
    sums = sums + sums_one
    sums_one = send(sums, lambda x, y, z, core: (x, y ^ 1, z, core))
    pair_both, sums, sums_one, query_back = phase(pair_both, sums, sums_one, query_back)

    normed_grad = query_back + mm_nt(pair_both, key_part[:, :pair_cols])
    pair_term = mm_tn(normed_both, pair_both)
    pair_cuts = cut(pair_term)
    pair_blocks = scatter(pair_cuts, 2)
    normed_grad_swap = swap_cores(after(normed_grad, pair_cuts[1])[shard_rows:].astype(BF16))
    normed_grad = jnp.concatenate(
        [normed_grad[:shard_rows], after(normed_grad_swap, pair_cuts[1]).astype(F32)], axis=1
    )
    input_part = norm_back(tokens_moved, factor_one, gain_one, normed_grad)
    input_grad = (mid_grad + mm(input_part.astype(BF16), hot_back)).astype(BF16)
    rest_total = add_up([after(rest_blocks[0], pair_cuts[1])] + rest_blocks[1:])
    sums = sums + sums_one
    sums_one = send(sums, lambda x, y, z, core: (x, y ^ 2, z, core))
    (
        *pair_blocks,
        rest_total,
        sums,
        sums_one,
        input_grad,
    ) = phase(
        *pair_blocks,
        rest_total,
        sums,
        sums_one,
        input_grad,
    )

    cuts = cut(jnp.concatenate([add_up(pair_blocks), rest_total], axis=1))
    blocks = scatter(cuts, 1)
    down_sum = swap_half_core(unpack_down(after(down_term, cuts[1])))
    unit_parts = after(unit_parts, cuts[1]).reshape(4, 8, 10, -1)
    unit_term = jnp.sum(unit_parts.astype(F32), axis=0)
    *blocks, unit_term, down_sum = phase(*blocks, unit_term, down_sum)

    cuts = cut(add_up(blocks))
    blocks = scatter(cuts, 0)
    unit_term = after(unit_term, cuts[1])
    grad_gate = unpack_units(unit_term[:, :, :units_here])
    grad_up = unpack_units(unit_term[:, :, units_here:])
    mlp_term = jnp.sum(w_gate.astype(F32) * grad_gate, axis=1)
    mlp_term = mlp_term + jnp.sum(w_up.astype(F32) * grad_up, axis=1)
    grad_mlp_gain = mlp_term / mlp_gain.astype(F32)
    down_sum = down_sum[: w_down.shape[0]].astype(F32)
    sums = sums + sums_one
    sums = sums[:3, :1].reshape(1, 3)
    seq_rms = jnp.sqrt(sums / (seq_length.astype(F32) * model_width))
    total = add_up(blocks)
    weights = jnp.concatenate([w_key, w_value, w_query], axis=1).astype(F32)
    grad_norm_gain = jnp.sum(weights * total[:, : pair_cols + QUERY_WIDTH], axis=1)
    grad_norm_gain = grad_norm_gain / norm_gain.astype(F32)
    return (
        activations,
        input_grad,
        grad_norm_gain,
        total[:, pair_cols : pair_cols + QUERY_WIDTH],
        total[:, :KEY_WIDTH],
        total[:, KEY_WIDTH:pair_cols],
        total[:, pair_cols + QUERY_WIDTH :],
        grad_mlp_gain,
        grad_gate,
        grad_up,
        down_sum,
        seq_rms,
    )


def solution(mesh):
    fine = Mesh(mesh.devices.reshape(SIZES), AXES)
    rows = P(AXES, None)
    flat = P(AXES)
    group = ("x", "zl", "core")
    in_specs = (
        (rows, flat, rows, rows, rows, rows, flat, rows, rows, rows)
        + (P(group, None), P(group), P(group))
        + (rows,)
    )
    out_specs = (rows, rows, flat, rows, rows, rows, rows, flat, rows, rows, rows, P(group, None))
    return jax.shard_map(
        local, mesh=fine, in_specs=in_specs, out_specs=out_specs, check_vma=False
    )
```

```python
import functools

import jax
import jax.numpy as jnp
import numpy as np
from jax import lax
from jax.experimental import pallas as pl
from jax.experimental.pallas import tpu as pltpu
from jax.sharding import Mesh, PartitionSpec as P

QUERY_HEADS = 20
KEY_VALUE_HEADS = 5
HEAD_WIDTH = 64
QUERY_WIDTH = QUERY_HEADS * HEAD_WIDTH
KEY_WIDTH = KEY_VALUE_HEADS * HEAD_WIDTH
GAIN_COLS = 128
SLICE_ROWS = 120
KERNEL_BYTES = 20 * 1024 * 1024
LARGE_BYTES = 58 * 1024 * 1024
FEED_BYTES = 24 * 1024 * 1024
PAD_UNITS = 32

EPSILON = 1e-05
ROPE_BASE = 10000.0
MASKED_SCORE = -1e30

AXES = ("y", "zh", "x", "zl", "core")
SIZES = (4, 2, 4, 2, 2)
ROW_AXES = ("y", "core")
SLICE_AXES = ("x", "zh", "zl")
F32 = jnp.float32
BF16 = jnp.bfloat16


def device_number(x, y, z, core):
    return (((y * 2 + z // 2) * 4 + x) * 2 + z % 2) * 2 + core


def pairs_of(move):
    pairs = []
    for y in range(4):
        for z in range(4):
            for x in range(4):
                for core in range(2):
                    tx, ty, tz, tc = move(x, y, z, core)
                    pairs.append(
                        (device_number(x, y, z, core), device_number(tx % 4, ty % 4, tz % 4, tc))
                    )
    return pairs


def send(values, move):
    return lax.ppermute(values, AXES, pairs_of(move))


def swap_cores(values):
    return send(values, lambda x, y, z, core: (x, y, z, 1 - core))


def swap_half_core(values):
    return send(values, lambda x, y, z, core: (x, y, core * 2 + z % 2, z // 2))


def stage_move(stage, distance):
    def move(x, y, z, core):
        spot = [x, y, z]
        spot[(stage + core + 1) % 3] += distance
        return (spot[0], spot[1], spot[2], core)

    return move


def spread(values, stage):
    arrived = [send(values, stage_move(stage, -distance)) for distance in (1, 2, 3)]
    return [values] + arrived


def join(blocks):
    return lax.optimization_barrier(jnp.concatenate(blocks, axis=0))


def cut(total):
    low = total.astype(BF16)
    rows = low.shape[0] // 4
    return [low[step * rows : (step + 1) * rows] for step in range(4)]


def scatter(total, stage):
    parts = total if isinstance(total, list) else cut(total)
    arrived = [send(parts[step], stage_move(stage, step)) for step in (1, 2, 3)]
    return [parts[0]] + arrived


def add_up(blocks):
    total = blocks[0].astype(F32)
    for block in blocks[1:]:
        total = total + block.astype(F32)
    return total


def phase(*values):
    return lax.optimization_barrier(values)


def along_y(values, distance):
    return send(values, lambda x, y, z, core: (x, y + distance, z, core))


def gather_rows(own):
    blocks = [own] + [along_y(own, -distance) for distance in (1, 2, 3)]
    return blocks + [swap_cores(block) for block in blocks]


def add_cores(own, other):
    return [(a.astype(F32) + swap_cores(b).astype(F32)) for a, b in zip(own, other)]


def reduce_blocks(sums):
    total = sums[0]
    for distance in (1, 2, 3):
        total = total + along_y(sums[distance].astype(BF16), distance).astype(F32)
    return total


def after(values, *earlier):
    return lax.optimization_barrier((values,) + earlier)[0]


def row_order(place, core):
    third, second, first, inner = jnp.meshgrid(
        jnp.arange(4), jnp.arange(4), jnp.arange(4), jnp.arange(10), indexing="ij"
    )
    spot = list(place)
    for stage, step in enumerate((first, second, third)):
        axis = (stage + core + 1) % 3
        spot[axis] = spot[axis] + step
    sx, sy, sz = spot
    numbers = device_number(sx % 4, sy % 4, sz % 4, core) * 10 + inner
    return numbers.reshape(-1).astype(jnp.int32)


def slice_order():
    x, zh, zl, y, core, inner = np.meshgrid(
        *(np.arange(n) for n in (4, 2, 2, 4, 2, 10)), indexing="ij"
    )
    return (device_number(x, y, zh * 2 + zl, core) * 10 + inner).reshape(-1).astype(np.int32)


def one_hot_back(order):
    return (order[:, None] == jnp.arange(order.shape[0], dtype=jnp.int32)[None, :]).astype(BF16)


def one_hot(order):
    return (jnp.arange(order.shape[0], dtype=jnp.int32)[:, None] == order[None, :]).astype(BF16)


def exact_move(values, hot):
    high = values.astype(BF16)
    low = (values - high.astype(F32)).astype(BF16)
    return mm(high, hot) + mm(low, hot)


def mm(left, right):
    return jnp.dot(left, right, preferred_element_type=F32)


def mm_nt(left, right):
    return lax.dot_general(left, right, (((1,), (1,)), ((), ())), preferred_element_type=F32)


def mm_tn(left, right):
    return lax.dot_general(left, right, (((0,), (0,)), ((), ())), preferred_element_type=F32)


def norm_factor(values):
    return lax.rsqrt(jnp.mean(values * values, axis=-1, keepdims=True) + EPSILON)


def norm_back(values, factor, gain, grad):
    weighted = gain * grad
    inner = jnp.mean(weighted * values, axis=-1, keepdims=True)
    return factor * weighted - values * (factor * factor * factor) * inner


def rope_tables(angles_at):
    half_size = HEAD_WIDTH // 2
    powers = jnp.arange(half_size, dtype=F32) * (2.0 / HEAD_WIDTH)
    speeds = jnp.power(ROPE_BASE, -powers)
    angles = angles_at[:, None] * speeds[None, :]
    cosine, sine = jnp.cos(angles), jnp.sin(angles)
    return (jnp.concatenate([cosine] * 4, axis=1), jnp.concatenate([-sine, sine] * 2, axis=1))


def rotate_pairs(values, cosine, sine):
    width = values.shape[1]
    half_size = HEAD_WIDTH // 2
    lanes = lax.broadcasted_iota(jnp.int32, values.shape, 1) % HEAD_WIDTH
    ahead = pltpu.roll(values, width - half_size, 1)
    behind = pltpu.roll(values, half_size, 1)
    return values * cosine + jnp.where(lanes < half_size, ahead, behind) * sine


def wide_table(table, width):
    return jnp.concatenate([table] * (width // table.shape[1]), axis=1)


def low_high(rows):
    low = [rows[at : at + 64] for at in range(0, rows.shape[0], 128)]
    high = [rows[at + 64 : at + 128] for at in range(0, rows.shape[0], 128)]
    return jnp.concatenate(low, axis=0), jnp.concatenate(high, axis=0)


def stack_heads(rows, head):
    pieces = [
        rows[at : at + 64, (4 * head + step) * HEAD_WIDTH : (4 * head + step + 1) * HEAD_WIDTH]
        for at in (0, 64)
        for step in range(4)
    ]
    return jnp.concatenate(pieces, axis=0)


def unstack_heads(stack):
    halves = [
        jnp.concatenate([stack[at + 64 * step : at + 64 * step + 64] for step in range(4)], axis=1)
        for at in (0, 256)
    ]
    return jnp.concatenate(halves, axis=0)


def mask_bias(keys_ref, rows_ref):
    columns = keys_ref[...].T
    keys_low, keys_high = columns[:512], columns[512:]

    def bias(keys, lanes):
        seen = (keys[:, 0:1] <= rows_ref[0:1, lanes]) | (keys[:, 1:2] == rows_ref[1:2, lanes])
        return jnp.where(seen, 0.0, MASKED_SCORE).astype(F32)

    return bias(keys_low, slice(0, 512)), bias(keys_high, slice(256, 512))


def attend_kernel(q_ref, part_ref, kv_ref, cos_ref, sin_ref, keys_ref, rows_ref, out_ref, turned_ref, log_ref):
    cosine = wide_table(cos_ref[...], QUERY_WIDTH)
    sine = wide_table(sin_ref[...], QUERY_WIDTH)
    queries = q_ref[...] + part_ref[...].astype(F32)
    queries = (rotate_pairs(queries, cosine, sine) * HEAD_WIDTH**-0.5).astype(BF16)
    turned_ref[...] = queries
    kv_low, kv_high = low_high(kv_ref[...])
    bias_low, bias_high = mask_bias(keys_ref, rows_ref)
    for head in range(KEY_VALUE_HEADS):
        at = slice(head * HEAD_WIDTH, (head + 1) * HEAD_WIDTH)
        vat = slice(KEY_WIDTH + head * HEAD_WIDTH, KEY_WIDTH + (head + 1) * HEAD_WIDTH)
        stack = stack_heads(queries, head)
        score_low = mm_nt(kv_low[:, at], stack) + bias_low
        score_high = mm_nt(kv_high[:, at], stack[256:]) + bias_high
        top_low = jnp.max(score_low, axis=0, keepdims=True)
        top_high = jnp.max(score_high, axis=0, keepdims=True)
        top = jnp.concatenate(
            [top_low[:, :256], jnp.maximum(top_low[:, 256:], top_high)], axis=1
        )
        exp_low = jnp.exp(score_low - top)
        exp_high = jnp.exp(score_high - top[:, 256:])
        total = jnp.sum(exp_low, axis=0, keepdims=True)
        total_high = jnp.sum(exp_high, axis=0, keepdims=True)
        total = jnp.concatenate([total[:, :256], total[:, 256:] + total_high], axis=1)
        result = mm_tn(kv_low[:, vat], exp_low.astype(BF16))
        result_high = mm_tn(kv_high[:, vat], exp_high.astype(BF16))
        result = jnp.concatenate([result[:, :256], result[:, 256:] + result_high], axis=1)
        result = (result / total).T
        out_ref[:, head * 256 : (head + 1) * 256] = unstack_heads(result).astype(BF16)
        log_ref[head : head + 1, :] = top + jnp.log(total)


def attend_back_kernel(
    q_ref, kv_ref, out_ref, grad_ref, log_ref, cos_ref, sin_ref, keys_ref, rows_ref, dq_ref, dkv_ref
):
    kv_low, kv_high = low_high(kv_ref[...])
    bias_low, bias_high = mask_bias(keys_ref, rows_ref)
    queries = q_ref[...]
    outs = out_ref[...]
    grads = grad_ref[...]
    ones = jnp.ones((8, HEAD_WIDTH), F32)
    dq_parts, dk_low, dk_high, dv_low, dv_high = [], [], [], [], []
    for head in range(KEY_VALUE_HEADS):
        at = slice(head * HEAD_WIDTH, (head + 1) * HEAD_WIDTH)
        vat = slice(KEY_WIDTH + head * HEAD_WIDTH, KEY_WIDTH + (head + 1) * HEAD_WIDTH)
        stack = stack_heads(queries, head)
        grad = stack_heads(grads, head)
        product = grad.astype(F32) * stack_heads(outs, head).astype(F32)
        delta = lax.dot_general(
            ones,
            product,
            (((1,), (1,)), ((), ())),
            preferred_element_type=F32,
            precision=lax.Precision.HIGHEST,
        )[0:1]
        logs = log_ref[head : head + 1, :]
        key_low, key_high = kv_low[:, at], kv_high[:, at]
        probs_low = jnp.exp(mm_nt(key_low, stack) + bias_low - logs)
        probs_high = jnp.exp(mm_nt(key_high, stack[256:]) + bias_high - logs[:, 256:])
        back_low = mm_nt(kv_low[:, vat], grad)
        back_high = mm_nt(kv_high[:, vat], grad[256:])
        score_low = (probs_low * (back_low - delta)).astype(BF16)
        score_high = (probs_high * (back_high - delta[:, 256:])).astype(BF16)
        dv_low.append(mm(probs_low.astype(BF16), grad))
        dv_high.append(mm(probs_high.astype(BF16), grad[256:]))
        dk_low.append(mm(score_low, stack))
        dk_high.append(mm(score_high, stack[256:]))
        dq = mm_tn(key_low, score_low)
        dq_high = mm_tn(key_high, score_high)
        dq = jnp.concatenate([dq[:, :256], dq[:, 256:] + dq_high], axis=1)
        dq_parts.append(unstack_heads((dq * HEAD_WIDTH**-0.5).T))
    cosine = wide_table(cos_ref[...], QUERY_WIDTH)
    sine = wide_table(sin_ref[...], QUERY_WIDTH)
    dq_ref[...] = rotate_pairs(jnp.concatenate(dq_parts, axis=1), cosine, -sine).astype(BF16)
    low = jnp.concatenate(dk_low + dv_low, axis=1).astype(BF16)
    high = jnp.concatenate(dk_high + dv_high, axis=1).astype(BF16)
    for at in range(8):
        dkv_ref[128 * at : 128 * at + 64] = low[64 * at : 64 * at + 64]
        dkv_ref[128 * at + 64 : 128 * at + 128] = high[64 * at : 64 * at + 64]


def run_kernel(kernel, shapes, operands, flops, limit=KERNEL_BYTES):
    return pl.pallas_call(
        kernel,
        out_shape=[jax.ShapeDtypeStruct(shape, kind) for shape, kind in shapes],
        in_specs=[pl.BlockSpec(memory_space=pltpu.VMEM)] * len(operands),
        out_specs=[pl.BlockSpec(memory_space=pltpu.VMEM)] * len(shapes),
        compiler_params=pltpu.CompilerParams(vmem_limit_bytes=limit),
        cost_estimate=pl.CostEstimate(
            flops=flops,
            bytes_accessed=sum(v.size * v.dtype.itemsize for v in operands),
            transcendentals=0,
        ),
    )(*operands)


def pair_kernel(
    moved_ref,
    factor_ref,
    part_ref,
    other_ref,
    cos_ref,
    sin_ref,
    pairs_ref,
    normed_ref,
    halves_ref,
    gains_ref,
):
    half = part_ref.shape[0]
    pair_cols = 2 * KEY_WIDTH
    gains = [ref[:, pair_cols:].astype(F32).T[:8] for ref in (part_ref, other_ref)]
    gains = jnp.concatenate(gains, axis=1)
    gains_ref[...] = gains
    scaled = moved_ref[...] * factor_ref[...]
    normed = (scaled * gains[0:1]).astype(BF16)
    normed_ref[...] = normed
    halves_ref[...] = normed[:, half:]
    both = mm(normed[:, :half], part_ref[:, :pair_cols]) + mm(
        normed[:, half:], other_ref[:, :pair_cols]
    )
    wide = 3 * cos_ref.shape[1]
    turned = rotate_pairs(
        both[:, :wide], wide_table(cos_ref[...], wide), wide_table(sin_ref[...], wide)
    )
    pairs = jnp.concatenate([turned[:, :KEY_WIDTH], both[:, KEY_WIDTH:]], axis=1).astype(BF16)
    for at in range(8):
        pairs_ref[at] = pairs


def pair_back_kernel(parts_ref, cos_ref, sin_ref, low_ref):
    total = parts_ref[0].astype(F32)
    for at in range(1, 8):
        total = total + parts_ref[at].astype(F32)
    wide = 3 * cos_ref.shape[1]
    turned = rotate_pairs(
        total[:, :wide], wide_table(cos_ref[...], wide), -wide_table(sin_ref[...], wide)
    )
    low_ref[...] = jnp.concatenate(
        [turned[:, :KEY_WIDTH], total[:, KEY_WIDTH:]], axis=1
    ).astype(BF16)


def middle_kernel(
    own_swap,
    back_a,
    back_b,
    back_c,
    back_d,
    cot_ref,
    weight_ref,
    middle_ref,
    factor_ref,
    gain_ref,
    hot_slice_ref,
    part_ref,
    other_ref,
    hot_ref,
    mid_ref,
    branch_ref,
    grad_ref,
    hot_slice,
    parts,
    hot,
    sems,
):
    half = part_ref.shape[0]
    copies = [
        pltpu.make_async_copy(hot_slice_ref, hot_slice, sems.at[0]),
        pltpu.make_async_copy(part_ref, parts.at[0:half], sems.at[1]),
        pltpu.make_async_copy(other_ref, parts.at[half : 2 * half], sems.at[2]),
        pltpu.make_async_copy(hot_ref, hot, sems.at[3]),
    ]
    for copy in copies:
        copy.start()
    total = own_swap[...].astype(F32) + back_a[...].astype(F32) + back_b[...].astype(F32)
    total = total + back_c[...].astype(F32)
    total = (total + back_d[...].astype(F32)).astype(BF16)
    copies[0].wait()
    grad = mm(total, hot_slice[...])
    middle, factor = middle_ref[...], factor_ref[...]
    mid = cot_ref[...].astype(F32) * weight_ref[...] + norm_back(middle, factor, gain_ref[...], grad)
    mid_ref[...] = mid
    branch = mid.astype(BF16)
    branch_ref[...] = branch
    copies[1].wait()
    copies[2].wait()
    moved = mm_nt(branch, parts[...]).astype(BF16)
    copies[3].wait()
    grad_ref[...] = mm(moved, hot[...]).astype(BF16)


def middle_call(small, large):
    vmem, hbm = pl.BlockSpec(memory_space=pltpu.VMEM), pl.BlockSpec(memory_space=pltpu.HBM)
    rows, width = small[0].shape
    square = pltpu.VMEM((width, width), BF16)
    return pl.pallas_call(
        middle_kernel,
        out_shape=[jax.ShapeDtypeStruct((rows, width), kind) for kind in (F32, BF16, BF16)],
        in_specs=[vmem] * len(small) + [hbm] * len(large),
        out_specs=[vmem] * 3,
        scratch_shapes=[square, square, square, pltpu.SemaphoreType.DMA((4,))],
        compiler_params=pltpu.CompilerParams(vmem_limit_bytes=LARGE_BYTES),
        cost_estimate=pl.CostEstimate(
            flops=6 * rows * width * width, bytes_accessed=16 * 2**20, transcendentals=0
        ),
    )(*small, *large)


def finish_kernel(
    feed_a, feed_b, feed_c, feed_d, middle_ref, branch_ref, weight_ref, out_ref, sums_ref
):
    feed = feed_a[...].astype(F32) + feed_b[...].astype(F32) + feed_c[...].astype(F32)
    feed = feed + feed_d[...].astype(F32)
    final = middle_ref[...] + feed
    out_ref[...] = final.astype(BF16)
    sums_ref[...] = jnp.zeros(sums_ref.shape, F32)
    for row, values in enumerate((branch_ref[...], feed, final)):
        part = jnp.sum(weight_ref[...] * values * values, axis=0, keepdims=True)
        part = jnp.sum(part, axis=1, keepdims=True)
        sums_ref[row : row + 1] = jnp.broadcast_to(part, (1, 128))


def query_kernel(
    normed_ref,
    halves_ref,
    a_ref,
    b_ref,
    c_ref,
    d_ref,
    own_ref,
    other_ref,
    both_ref,
    query_ref,
    out_ref,
    sems,
):
    width, count = query_ref.shape[1], a_ref.shape[0]
    copies = []
    for step, block in enumerate((a_ref, b_ref, c_ref, d_ref)):
        at = slice(step * count, (step + 1) * count)
        copies.append(
            pltpu.make_async_copy(block.at[:, 0:width], query_ref.at[at], sems.at[step])
        )
    for step, block in enumerate((a_ref, b_ref, c_ref, d_ref)):
        at = slice(step * count, (step + 1) * count)
        copies.append(
            pltpu.make_async_copy(
                block.at[:, width : 2 * width], out_ref.at[at], sems.at[4 + step]
            )
        )
    for copy in copies:
        copy.start()
    for copy in copies[:4]:
        copy.wait()
    half = own_ref.shape[0]
    both_ref[0:half] = normed_ref[:, : both_ref.shape[1]]
    both_ref[half : 2 * half] = halves_ref[...]
    both = mm(both_ref[...], query_ref[...])
    own_ref[...] = both[:half]
    other_ref[...] = both[half:].astype(BF16)
    for copy in copies[4:]:
        copy.wait()


def query_parts(normed, halves, blocks):
    vmem = pl.BlockSpec(memory_space=pltpu.VMEM)
    half, width = normed.shape[0], QUERY_WIDTH
    joined = jax.ShapeDtypeStruct((4 * blocks[0].shape[0], width), BF16)
    return pl.pallas_call(
        query_kernel,
        out_shape=[
            jax.ShapeDtypeStruct((half, width), F32),
            jax.ShapeDtypeStruct((half, width), BF16),
            jax.ShapeDtypeStruct((2 * half, halves.shape[1]), BF16),
            joined,
            joined,
        ],
        in_specs=[vmem] * 2 + [pl.BlockSpec(memory_space=pltpu.HBM)] * 4,
        out_specs=[vmem] * 5,
        scratch_shapes=[pltpu.SemaphoreType.DMA((8,))],
        compiler_params=pltpu.CompilerParams(vmem_limit_bytes=LARGE_BYTES),
        cost_estimate=pl.CostEstimate(
            flops=4 * halves.size * width, bytes_accessed=10 * 2**20, transcendentals=0
        ),
    )(normed, halves, *blocks)


def unpack_kernel(slices_ref, units_ref, down_ref):
    for block in range(16):
        base, at = block * SLICE_ROWS, block * 32
        units_ref[block * 80 : block * 80 + 80] = slices_ref[base : base + 80]
        down_ref[at : at + 32, :1024] = slices_ref[base + 80 : base + 112]
        rest = slices_ref[base + 112 : base + 120]
        down_ref[at : at + 32, 1024:] = jnp.concatenate(
            [rest[:, part * 256 : part * 256 + 256] for part in range(4)], axis=0
        )


def unpack_slices(slices):
    return run_kernel(
        unpack_kernel, [((1280, 1024), BF16), ((512, 1280), BF16)], (slices,), 0, FEED_BYTES
    )


def feed_kernel(
    xa_ref,
    xb_ref,
    all_grads_ref,
    places_ref,
    valid_ref,
    units_ref,
    down_ref,
    hidden_ref,
    unit_ref,
    back_a_ref,
    back_b_ref,
    out_a_ref,
    out_b_ref,
    rows_ref,
    grads_ref,
    sems,
    *,
    step,
):
    half = xa_ref.shape[0]
    low = slice(0, half)
    high = slice(half, 2 * half)
    spot_a = pl.ds(pl.multiple_of(places_ref[step], half), half)
    spot_b = pl.ds(pl.multiple_of(places_ref[step + 4], half), half)
    copies = [
        pltpu.make_async_copy(xa_ref, rows_ref.at[low], sems.at[0]),
        pltpu.make_async_copy(xb_ref, rows_ref.at[high], sems.at[1]),
    ]
    copies += [
        pltpu.make_async_copy(all_grads_ref.at[spot_a], grads_ref.at[low], sems.at[2]),
        pltpu.make_async_copy(all_grads_ref.at[spot_b], grads_ref.at[high], sems.at[3]),
    ]
    for copy in copies:
        copy.start()
    copies[0].wait()
    copies[1].wait()
    units = units_ref.shape[1] // 2
    both = mm(rows_ref[...], units_ref[...])
    gate, up = both[:, :units], both[:, units:]
    sigmoid = 1.0 / (1.0 + jnp.exp(-gate))
    silu = gate * sigmoid
    hidden = silu * up
    columns = valid_ref[...].T
    valid = jnp.concatenate(
        [columns[:, step : step + 1], columns[:, step + 4 : step + 5]], axis=0
    )
    hidden_ref[...] = (hidden * valid).astype(BF16)
    hidden = hidden.astype(BF16)
    for copy in copies[2:]:
        copy.wait()
    hidden_grad = mm_nt(grads_ref[...], down_ref[...]) * valid
    gate_low = (hidden_grad * up * sigmoid * (1.0 + gate * (1.0 - sigmoid))).astype(BF16)
    up_low = (hidden_grad * silu).astype(BF16)
    unit = jnp.concatenate([gate_low, up_low], axis=1)
    unit_ref[...] = unit
    back = mm_nt(unit, units_ref[...]).astype(BF16)
    back_a_ref[...] = back[:half]
    back_b_ref[...] = back[half:]
    outs = mm(hidden, down_ref[...]).astype(BF16)
    out_a_ref[...] = outs[:half]
    out_b_ref[...] = outs[half:]


def feed_chunk(step, rows_a, rows_b, all_grads, places, valid, units, down):
    count, width = rows_a.shape[0] * 2, rows_a.shape[1]
    vmem = pl.BlockSpec(memory_space=pltpu.VMEM)
    hbm = pl.BlockSpec(memory_space=pltpu.HBM)
    shapes = [(count, 512), (count, 1024)] + [rows_a.shape] * 4
    return pl.pallas_call(
        functools.partial(feed_kernel, step=step),
        out_shape=[jax.ShapeDtypeStruct(shape, BF16) for shape in shapes],
        in_specs=[hbm] * 3 + [pl.BlockSpec(memory_space=pltpu.SMEM)] + [vmem] * 3,
        out_specs=[vmem] * 6,
        scratch_shapes=[
            pltpu.VMEM((count, width), BF16),
            pltpu.VMEM((count, width), BF16),
            pltpu.SemaphoreType.DMA((4,)),
        ],
        compiler_params=pltpu.CompilerParams(vmem_limit_bytes=FEED_BYTES),
        cost_estimate=pl.CostEstimate(
            flops=2 * count * width * 3 * 1024,
            bytes_accessed=2 * (units.size + down.size + 4 * rows_a.size),
            transcendentals=0,
        ),
    )(rows_a, rows_b, all_grads, places, valid, units, down)


def weight_kernel(*refs):
    sources, all_grads, places, term_out = refs[:24], refs[24], refs[25], refs[26]
    feed_outs = refs[27:31]
    grads, terms, in_sems, out_sems = refs[31:]
    copies = []
    for step in range(4):
        base = step * 256
        for place, start in ((step, base), (step + 4, base + 128)):
            spot = pl.ds(pl.multiple_of(places[place], 128), 128)
            copies.append(
                pltpu.make_async_copy(
                    all_grads.at[spot], grads.at[start : start + 128], in_sems.at[len(copies)]
                )
            )
    for copy in copies:
        copy.start()
    for step in range(4):
        total = sources[step + 16][...].astype(F32) + sources[step + 20][...].astype(F32)
        feed_outs[step][...] = total.astype(BF16)
    for at in range(0, 16, 4):
        lanes = slice(at * 80, at * 80 + 320)
        total = None
        for step in range(4):
            pair = jnp.concatenate([sources[step][:, lanes], sources[step + 4][:, lanes]], axis=0)
            term = mm_tn(pair, sources[step + 12][...])
            total = term if total is None else total + term
        total = total.astype(BF16)
        for step in range(4):
            base = (at + step) * SLICE_ROWS
            terms[base : base + 80] = total[step * 80 : step * 80 + 80]
    for copy in copies:
        copy.wait()
    hidden = jnp.concatenate([sources[step + 8][...] for step in range(4)], axis=0)
    moves = []
    for at in range(0, 16, 4):
        total = mm_tn(hidden[:, at * 32 : at * 32 + 128], grads[...]).astype(BF16)
        for step in range(4):
            rows_here = total[step * 32 : step * 32 + 32]
            base = (at + step) * SLICE_ROWS
            terms[base + 80 : base + 112] = rows_here[:, :1024]
            rest = [rows_here[part * 8 : part * 8 + 8, 1024:] for part in range(4)]
            terms[base + 112 : base + 120] = jnp.concatenate(rest, axis=1)
        piece = slice(at * SLICE_ROWS, (at + 4) * SLICE_ROWS)
        moves.append(
            pltpu.make_async_copy(terms.at[piece], term_out.at[piece], out_sems.at[at // 4])
        )
        moves[-1].start()
    for move in moves:
        move.wait()


def weight_terms(rows, all_grads, places, chunks, feed_swaps):
    sources = list(rows)
    for part in (0, 1, 4):
        sources += [chunk[part] for chunk in chunks]
    sources += list(feed_swaps)
    count, width = 8 * rows[0].shape[0], rows[0].shape[1]
    smem, hbm = pl.BlockSpec(memory_space=pltpu.SMEM), pl.BlockSpec(memory_space=pltpu.HBM)
    return pl.pallas_call(
        weight_kernel,
        out_shape=[jax.ShapeDtypeStruct((16 * SLICE_ROWS, 1024), BF16)]
        + [jax.ShapeDtypeStruct(rows[0].shape, BF16)] * 4,
        in_specs=[pl.BlockSpec(memory_space=pltpu.VMEM)] * 24 + [hbm, smem],
        out_specs=[hbm] + [pl.BlockSpec(memory_space=pltpu.VMEM)] * 4,
        scratch_shapes=[
            pltpu.VMEM((count, width), BF16),
            pltpu.VMEM((16 * SLICE_ROWS, 1024), BF16),
            pltpu.SemaphoreType.DMA((8,)),
            pltpu.SemaphoreType.DMA((4,)),
        ],
        compiler_params=pltpu.CompilerParams(vmem_limit_bytes=24 * 1024 * 1024),
        cost_estimate=pl.CostEstimate(
            flops=2 * count * 1280 * 1536, bytes_accessed=2**20, transcendentals=0
        ),
    )(*sources, all_grads, places)


def term_kernel(normed_ref, q_ref, qs_ref, attended_ref, as_ref, b_ref, bs_ref, *outs):
    count = outs[0].shape[0]
    half = normed_ref.shape[1]
    queries = jnp.concatenate([q_ref[...], qs_ref[...]], axis=0)
    outs[4][...] = queries
    branch = jnp.concatenate([b_ref[...], bs_ref[...]], axis=0)
    attended = jnp.concatenate([attended_ref[:, :half], as_ref[...]], axis=0)
    query_term = mm_tn(normed_ref[...], queries).astype(BF16)
    out_term = mm_tn(attended, branch).astype(BF16)
    for step in range(4):
        at = slice(step * count, (step + 1) * count)
        outs[step][:, :QUERY_WIDTH] = query_term[at]
        outs[step][:, QUERY_WIDTH:] = out_term[at]


def pack_slice(units, down):
    rest = [down[part * 8 : part * 8 + 8, 1024:] for part in range(4)]
    return jnp.concatenate([units, down[:, :1024], jnp.concatenate(rest, axis=1)], axis=0)


def unpack_down(rows):
    rest = [rows[32:, part * 256 : part * 256 + 256] for part in range(4)]
    return jnp.concatenate([rows[:32], jnp.concatenate(rest, axis=0)], axis=1)


def group_places(pair_row, devices_ctx, block_size):
    slots = jnp.arange(devices_ctx * 2 * block_size, dtype=jnp.int32)
    owners = slots // (2 * block_size)
    inside = slots % (2 * block_size)
    columns = jnp.arange(devices_ctx, dtype=jnp.int32)
    paired = jnp.sum(jnp.where(owners[:, None] == columns[None, :], pair_row[None, :], 0), axis=1)
    blocks = jnp.where(inside < block_size, paired, 2 * devices_ctx - 1 - paired)
    return blocks * block_size + inside % block_size


def pack_units(weight):
    rows = weight.shape[0]
    runs = weight.reshape(rows, 8, 4, 2, 2, 28).transpose(1, 0, 2, 4, 3, 5)
    runs = jnp.pad(runs, ((0, 0),) * 5 + ((0, PAD_UNITS - 28),))
    return runs.reshape(8, rows, 16 * PAD_UNITS)


def unpack_units(packed):
    rows = packed.shape[1]
    runs = packed.reshape(8, rows, 4, 2, 2, PAD_UNITS)[..., :28]
    return runs.transpose(1, 0, 2, 4, 3, 5).reshape(rows, 8 * 16 * 28)


def local(
    tokens,
    norm_gain,
    w_query,
    w_key,
    w_value,
    w_out,
    mlp_gain,
    w_gate,
    w_up,
    w_down,
    block_pair,
    seq_len,
    seq_start,
    out_grad,
):
    shard_rows, model_width = tokens.shape
    block_size = shard_rows // 2
    half = model_width // 2
    devices_ctx = 8
    at_y, at_zh, at_x, at_zl, at_core = (lax.axis_index(name) for name in AXES)
    place = (at_x, at_y, at_zh * 2 + at_zl)
    position = at_y * 2 + at_zh
    pair_cols = 2 * KEY_WIDTH
    split = pair_cols + GAIN_COLS

    first_slot = seq_start[0]
    seq_length = seq_len[0]
    grad_rows = lax.all_gather(out_grad, ROW_AXES, axis=0, tiled=True)
    gains = jnp.stack([norm_gain, mlp_gain], axis=1)
    gains = jnp.pad(gains, ((0, 0), (0, GAIN_COLS - 2)))
    front = jnp.concatenate([w_key, w_value, gains, w_query, w_out], axis=1)
    front = spread(front, 0)
    units = jnp.concatenate([pack_units(w_gate), pack_units(w_up)], axis=2)
    *arrived, units, tokens, block_pair, out_grad = phase(
        *front, units, tokens, block_pair, out_grad
    )

    front = spread(join(arrived), 1)
    units = lax.all_to_all(units, ROW_AXES, 0, 0, tiled=True)
    down_rows = jnp.pad(w_down, ((0, PAD_UNITS - w_down.shape[0]), (0, 0)))
    down_rows = swap_half_core(after(down_rows, block_pair))
    places_all = group_places(block_pair[0], devices_ctx, block_size)
    places_here = lax.dynamic_slice_in_dim(places_all, position * shard_rows, shard_rows)
    valid_here = (places_here >= first_slot) & (places_here < first_slot + seq_length)
    row_weight = valid_here.astype(F32)[:, None]
    valid_all = (places_all >= first_slot) & (places_all < first_slot + seq_length)
    ring_valid = valid_all.astype(F32).reshape(4, 2, shard_rows)
    ring_valid = lax.dynamic_index_in_dim(ring_valid, at_zh, 1, keepdims=False)
    ring_valid = lax.dynamic_slice_in_dim(
        jnp.concatenate([ring_valid, ring_valid]), at_y, 4, axis=0
    )
    ring_valid = jnp.concatenate([ring_valid, swap_cores(ring_valid)])
    key_places = jnp.stack([jnp.where(valid_all, places_all, 1 << 20), places_all])
    key_places = jnp.concatenate(
        [key_places[:, at : at + 64] for side in (0, 64) for at in range(side, 1024, 128)], axis=1
    )
    key_places = jnp.pad(key_places, ((0, 6), (0, 0)))
    row_places = jnp.stack([jnp.where(valid_here, places_here, -1), places_here])
    row_places = jnp.concatenate([row_places[:, :64]] * 4 + [row_places[:, 64:]] * 4, axis=1)
    cosine, sine = rope_tables((places_here - first_slot).astype(F32))
    inputs = tokens.astype(F32)
    factor_one = norm_factor(inputs)
    *arrived, factor_one, order_seed = phase(*front, factor_one, at_core)

    key_part = join([block[:, :split] for block in arrived])
    units, down_rows = after((units, down_rows), key_part)
    slices = pack_slice(units.reshape(-1, units.shape[2]), down_rows)
    slices = lax.all_gather(after(slices, grad_rows), SLICE_AXES, axis=0, tiled=True)
    key_part = spread(key_part, 2)
    rest = join([block[:, split:] for block in arrived])
    orders = [row_order(place, core) for core in (0, 1)]
    mine = jnp.where(order_seed == 0, orders[0], orders[1])
    other = jnp.where(order_seed == 0, orders[1], orders[0])
    order = jnp.concatenate([mine, other])
    hot = one_hot(order)
    tokens_moved = mm(tokens, hot)
    *key_part, rest, hot, tokens_moved, order = phase(
        *key_part, rest, hot, tokens_moved, order
    )

    rest_part = spread(rest, 2)
    key_part = join(key_part)
    key_part, key_other = phase(key_part, swap_cores(key_part))

    pairs, normed, halves, gain_rows = run_kernel(
        pair_kernel,
        [
            ((devices_ctx, shard_rows, pair_cols), BF16),
            ((shard_rows, model_width), BF16),
            ((shard_rows, half), BF16),
            ((8, model_width), F32),
        ],
        (tokens_moved, factor_one, key_part, key_other, cosine, sine),
        2 * shard_rows * model_width * pair_cols,
        LARGE_BYTES,
    )
    gain_one = gain_rows[0:1]

    def project(rows, part, other_part):
        return mm(rows[:, :half], part) + mm(rows[:, half:], other_part)

    gathered = lax.all_to_all(pairs, ("y", "zh"), 0, 0, tiled=True)
    gathered = gathered.reshape(devices_ctx * shard_rows, pair_cols)
    halves = swap_cores(halves)
    hot_back = one_hot_back(order)
    gain_two = mm(gain_rows.astype(BF16), hot_back)[1:2]
    slice_places = after(jnp.asarray(slice_order()), order)
    slice_hot, slice_back = one_hot(slice_places), one_hot_back(slice_places)
    grad_places = jnp.stack(
        [
            ((at_y + step) % 4 * 2 + (at_core + side) % 2) * shard_rows
            for side in (0, 1)
            for step in range(4)
        ]
    ).astype(jnp.int32)
    (
        *rest_part,
        gathered,
        gain_two,
        halves,
        slice_hot,
        slice_back,
        hot_back,
        grad_places,
        ring_valid,
        row_weight,
    ) = phase(
        *rest_part,
        gathered,
        gain_two,
        halves,
        slice_hot,
        slice_back,
        hot_back,
        grad_places,
        ring_valid,
        row_weight,
    )

    query_own, query_other, normed_both, query_part, out_part = query_parts(
        normed, halves, rest_part
    )
    query_other = swap_cores(query_other)
    out_other = swap_cores(after(out_part, query_other))
    attended, queries, logs = run_kernel(
        attend_kernel,
        [((shard_rows, QUERY_WIDTH), BF16), ((shard_rows, QUERY_WIDTH), BF16), ((8, 512), F32)],
        (query_own, query_other, gathered, cosine, sine, key_places, row_places),
        shard_rows * 1024 * QUERY_WIDTH * 4,
        LARGE_BYTES,
    )
    attended_moved = mm(attended, hot).astype(BF16)
    branch = project(attended_moved, out_part, out_other)
    middle = inputs + branch
    factor_two = norm_factor(middle)
    normed_two = (middle * factor_two * gain_two).astype(BF16)
    normed_two = mm(normed_two, slice_hot).astype(BF16)
    normed_two, middle, factor_two, branch = phase(normed_two, middle, factor_two, branch)

    ahead, behind = along_y(normed_two, -1), along_y(normed_two, 1)
    cut_at = shard_rows // 2
    row_blocks = [normed_two, ahead, None, behind, swap_cores(normed_two), None, None, None]
    units_full, down_full = unpack_slices(slices)
    chunks = [None] * 4
    back_parts, ready, feed_swaps = [None] * 4, [None] * 4, [None] * 4
    for step in (0, 1, 3, 2):
        if step == 1:
            ahead, behind = after((ahead, behind), chunks[0][0])
            across = [along_y(ahead[:cut_at], -1), along_y(behind[cut_at:], 1)]
            row_blocks[1], row_blocks[3] = ahead, behind
        if step == 2:
            row_blocks[2] = jnp.concatenate(after(tuple(across), chunks[1][0]), axis=0)
        if step:
            row_blocks[step + 4] = swap_cores(row_blocks[step])
        block = after(row_blocks[step], ready[1], ready[3]) if step == 2 else row_blocks[step]
        chunks[step] = feed_chunk(
            step,
            block,
            row_blocks[step + 4],
            grad_rows,
            grad_places,
            ring_valid,
            units_full,
            down_full,
        )
        swapped = swap_cores(chunks[step][3])
        feed_swaps[step] = swap_cores(chunks[step][5])
        total = chunks[step][2].astype(F32) + swapped.astype(F32)
        ready[step] = total.astype(BF16) if step else swapped
        back_parts[step] = along_y(ready[step], step) if step else None
    terms, *feed_sums = weight_terms(
        row_blocks[:1] + [after(block, *ready) for block in row_blocks[1:]],
        grad_rows,
        grad_places,
        chunks,
        feed_swaps,
    )
    back_parts[0] = chunks[0][2]
    attended_swap = swap_cores(attended_moved[:, half:])
    *arrived, attended_swap, terms, own_swap = phase(
        *back_parts, *feed_sums, attended_swap, terms, ready[0]
    )
    back_parts, feed_sums = arrived[:4], arrived[4:]
    terms = lax.psum_scatter(terms, "x", scatter_dimension=0, tiled=True)

    units_here = 16 * PAD_UNITS
    feed_parts = [feed_sums[0]] + [along_y(feed_sums[step], step) for step in (1, 2, 3)]
    mid_grad, branch_grad, attended_grad = middle_call(
        (own_swap, *back_parts, out_grad, row_weight, middle, factor_two, gain_two),
        (slice_back, out_part, out_other, hot_back),
    )
    branch_swap = swap_cores(branch_grad)
    attended_grad = after(attended_grad, feed_parts[1])
    query_low, pair_grads = run_kernel(
        attend_back_kernel,
        [((shard_rows, QUERY_WIDTH), BF16), ((1024, pair_cols), BF16)],
        (
            queries,
            gathered,
            attended,
            attended_grad,
            logs,
            cosine,
            sine,
            key_places,
            row_places,
        ),
        shard_rows * 1024 * QUERY_WIDTH * 10,
        LARGE_BYTES,
    )
    *feed_parts, query_low, pair_grads, mid_grad, branch_grad, branch_swap = phase(
        *feed_parts, query_low, pair_grads, mid_grad, branch_grad, branch_swap
    )

    pair_grads = lax.all_to_all(
        pair_grads.reshape(devices_ctx, shard_rows, pair_cols), ("y", "zh"), 0, 0, tiled=True
    )
    query_swap = swap_cores(query_low)
    *rest_term, query_both = run_kernel(
        term_kernel,
        [((160, 2 * QUERY_WIDTH), BF16)] * 4 + [((2 * shard_rows, QUERY_WIDTH), BF16)],
        (
            normed_both,
            query_low,
            query_swap,
            attended_moved,
            attended_swap,
            branch_grad,
            branch_swap,
        ),
        4 * half * 2 * shard_rows * QUERY_WIDTH,
        LARGE_BYTES,
    )
    rest_blocks = scatter(rest_term, 2)
    activations, sums = run_kernel(
        finish_kernel,
        [((shard_rows, model_width), BF16), ((8, 128), F32)],
        (*feed_parts, middle, branch, row_weight),
        0,
        LARGE_BYTES,
    )
    sums_one = send(sums, lambda x, y, z, core: (x, y, z + 2, core))
    pair_grads, query_both, sums, sums_one, terms = phase(
        pair_grads, query_both, sums, sums_one, terms
    )
    terms = terms.reshape(4, SLICE_ROWS, terms.shape[1])
    unit_parts = lax.all_to_all(
        terms[:, :80].reshape(32, 10, terms.shape[2]), ("zh", "zl", "y", "core"), 0, 0, tiled=True
    )
    down_term = lax.psum_scatter(
        terms[:, 80:].reshape(4 * (SLICE_ROWS - 80), terms.shape[2]), ("zh", "zl"), scatter_dimension=0, tiled=True
    )

    (pair_low,) = run_kernel(
        pair_back_kernel,
        [((shard_rows, pair_cols), BF16)],
        (pair_grads, cosine, sine),
        0,
    )
    pair_both = jnp.concatenate([pair_low, swap_cores(pair_low)])
    query_back = mm_nt(query_both, query_part)
    sums = sums + sums_one
    sums_one = send(sums, lambda x, y, z, core: (x, y ^ 1, z, core))
    pair_both, sums, sums_one, query_back = phase(pair_both, sums, sums_one, query_back)

    normed_grad = query_back + mm_nt(pair_both, key_part[:, :pair_cols])
    pair_term = mm_tn(normed_both, pair_both)
    pair_cuts = cut(pair_term)
    pair_blocks = scatter(pair_cuts, 2)
    normed_grad_swap = swap_cores(after(normed_grad, pair_cuts[1])[shard_rows:].astype(BF16))
    normed_grad = jnp.concatenate(
        [normed_grad[:shard_rows], after(normed_grad_swap, pair_cuts[1]).astype(F32)], axis=1
    )
    input_part = norm_back(tokens_moved, factor_one, gain_one, normed_grad)
    input_grad = (mid_grad + mm(input_part.astype(BF16), hot_back)).astype(BF16)
    rest_total = add_up([after(rest_blocks[0], pair_cuts[1])] + rest_blocks[1:])
    sums = sums + sums_one
    sums_one = send(sums, lambda x, y, z, core: (x, y ^ 2, z, core))
    (
        *pair_blocks,
        rest_total,
        sums,
        sums_one,
        input_grad,
    ) = phase(
        *pair_blocks,
        rest_total,
        sums,
        sums_one,
        input_grad,
    )

    cuts = cut(jnp.concatenate([add_up(pair_blocks), rest_total], axis=1))
    blocks = scatter(cuts, 1)
    down_sum = swap_half_core(unpack_down(after(down_term, cuts[1])))
    unit_parts = after(unit_parts, cuts[1]).reshape(4, 8, 10, -1)
    unit_term = jnp.sum(unit_parts.astype(F32), axis=0)
    *blocks, unit_term, down_sum = phase(*blocks, unit_term, down_sum)

    cuts = cut(add_up(blocks))
    blocks = scatter(cuts, 0)
    unit_term = after(unit_term, cuts[1])
    grad_gate = unpack_units(unit_term[:, :, :units_here])
    grad_up = unpack_units(unit_term[:, :, units_here:])
    mlp_term = jnp.sum(w_gate.astype(F32) * grad_gate, axis=1)
    mlp_term = mlp_term + jnp.sum(w_up.astype(F32) * grad_up, axis=1)
    grad_mlp_gain = mlp_term / mlp_gain.astype(F32)
    down_sum = down_sum[: w_down.shape[0]].astype(F32)
    sums = sums + sums_one
    sums = sums[:3, :1].reshape(1, 3)
    seq_rms = jnp.sqrt(sums / (seq_length.astype(F32) * model_width))
    total = add_up(blocks)
    weights = jnp.concatenate([w_key, w_value, w_query], axis=1).astype(F32)
    grad_norm_gain = jnp.sum(weights * total[:, : pair_cols + QUERY_WIDTH], axis=1)
    grad_norm_gain = grad_norm_gain / norm_gain.astype(F32)
    return (
        activations,
        input_grad,
        grad_norm_gain,
        total[:, pair_cols : pair_cols + QUERY_WIDTH],
        total[:, :KEY_WIDTH],
        total[:, KEY_WIDTH:pair_cols],
        total[:, pair_cols + QUERY_WIDTH :],
        grad_mlp_gain,
        grad_gate,
        grad_up,
        down_sum,
        seq_rms,
    )


def solution(mesh):
    fine = Mesh(mesh.devices.reshape(SIZES), AXES)
    rows = P(AXES, None)
    flat = P(AXES)
    group = ("x", "zl", "core")
    in_specs = (
        (rows, flat, rows, rows, rows, rows, flat, rows, rows, rows)
        + (P(group, None), P(group), P(group))
        + (rows,)
    )
    out_specs = (rows, rows, flat, rows, rows, rows, rows, flat, rows, rows, rows, P(group, None))
    return jax.shard_map(
        local, mesh=fine, in_specs=in_specs, out_specs=out_specs, check_vma=False
    )
```

```python
import functools

import jax
import jax.numpy as jnp
import numpy as np
from jax import lax
from jax.experimental import pallas as pl
from jax.experimental.pallas import tpu as pltpu
from jax.sharding import Mesh, PartitionSpec as P

QUERY_HEADS = 20
KEY_VALUE_HEADS = 5
HEAD_WIDTH = 64
QUERY_WIDTH = QUERY_HEADS * HEAD_WIDTH
KEY_WIDTH = KEY_VALUE_HEADS * HEAD_WIDTH
GAIN_COLS = 128
KERNEL_BYTES = 20 * 1024 * 1024
LARGE_BYTES = 58 * 1024 * 1024
FEED_BYTES = 24 * 1024 * 1024
PAD_UNITS = 32

EPSILON = 1e-05
ROPE_BASE = 10000.0
MASKED_SCORE = -1e30

AXES = ("y", "zh", "x", "zl", "core")
SIZES = (4, 2, 4, 2, 2)
ROW_AXES = ("y", "core")
SLICE_AXES = ("x", "zh", "zl")
F32 = jnp.float32
BF16 = jnp.bfloat16


def device_number(x, y, z, core):
    return (((y * 2 + z // 2) * 4 + x) * 2 + z % 2) * 2 + core


def pairs_of(move):
    pairs = []
    for y in range(4):
        for z in range(4):
            for x in range(4):
                for core in range(2):
                    tx, ty, tz, tc = move(x, y, z, core)
                    pairs.append(
                        (device_number(x, y, z, core), device_number(tx % 4, ty % 4, tz % 4, tc))
                    )
    return pairs


def send(values, move):
    return lax.ppermute(values, AXES, pairs_of(move))


def swap_cores(values):
    return send(values, lambda x, y, z, core: (x, y, z, 1 - core))


def swap_half_core(values):
    return send(values, lambda x, y, z, core: (x, y, core * 2 + z % 2, z // 2))


def stage_move(stage, distance):
    def move(x, y, z, core):
        spot = [x, y, z]
        spot[(stage + core + 1) % 3] += distance
        return (spot[0], spot[1], spot[2], core)

    return move


def spread(values, stage):
    arrived = [send(values, stage_move(stage, -distance)) for distance in (1, 2, 3)]
    return [values] + arrived


def join(blocks):
    return lax.optimization_barrier(jnp.concatenate(blocks, axis=0))


def cut(total):
    low = total.astype(BF16)
    rows = low.shape[0] // 4
    return [low[step * rows : (step + 1) * rows] for step in range(4)]


def scatter(total, stage):
    parts = total if isinstance(total, list) else cut(total)
    arrived = [send(parts[step], stage_move(stage, step)) for step in (1, 2, 3)]
    return [parts[0]] + arrived


def add_up(blocks):
    total = blocks[0].astype(F32)
    for block in blocks[1:]:
        total = total + block.astype(F32)
    return total


def phase(*values):
    return lax.optimization_barrier(values)


def along_y(values, distance):
    return send(values, lambda x, y, z, core: (x, y + distance, z, core))


def gather_rows(own):
    blocks = [own] + [along_y(own, -distance) for distance in (1, 2, 3)]
    return blocks + [swap_cores(block) for block in blocks]


def add_cores(own, other):
    return [(a.astype(F32) + swap_cores(b).astype(F32)) for a, b in zip(own, other)]


def reduce_blocks(sums):
    total = sums[0]
    for distance in (1, 2, 3):
        total = total + along_y(sums[distance].astype(BF16), distance).astype(F32)
    return total


def after(values, *earlier):
    return lax.optimization_barrier((values,) + earlier)[0]


def row_order(place, core):
    third, second, first, inner = jnp.meshgrid(
        jnp.arange(4), jnp.arange(4), jnp.arange(4), jnp.arange(10), indexing="ij"
    )
    spot = list(place)
    for stage, step in enumerate((first, second, third)):
        axis = (stage + core + 1) % 3
        spot[axis] = spot[axis] + step
    sx, sy, sz = spot
    numbers = device_number(sx % 4, sy % 4, sz % 4, core) * 10 + inner
    return numbers.reshape(-1).astype(jnp.int32)


def slice_order():
    x, zh, zl, y, core, inner = np.meshgrid(
        *(np.arange(n) for n in (4, 2, 2, 4, 2, 10)), indexing="ij"
    )
    return (device_number(x, y, zh * 2 + zl, core) * 10 + inner).reshape(-1).astype(np.int32)


def one_hot_back(order):
    return (order[:, None] == jnp.arange(order.shape[0], dtype=jnp.int32)[None, :]).astype(BF16)


def one_hot(order):
    return (jnp.arange(order.shape[0], dtype=jnp.int32)[:, None] == order[None, :]).astype(BF16)


def exact_move(values, hot):
    high = values.astype(BF16)
    low = (values - high.astype(F32)).astype(BF16)
    return mm(high, hot) + mm(low, hot)


def mm(left, right):
    return jnp.dot(left, right, preferred_element_type=F32)


def mm_nt(left, right):
    return lax.dot_general(left, right, (((1,), (1,)), ((), ())), preferred_element_type=F32)


def mm_tn(left, right):
    return lax.dot_general(left, right, (((0,), (0,)), ((), ())), preferred_element_type=F32)


def norm_factor(values):
    return lax.rsqrt(jnp.mean(values * values, axis=-1, keepdims=True) + EPSILON)


def norm_back(values, factor, gain, grad):
    weighted = gain * grad
    inner = jnp.mean(weighted * values, axis=-1, keepdims=True)
    return factor * weighted - values * (factor * factor * factor) * inner


def rope_tables(angles_at):
    half_size = HEAD_WIDTH // 2
    powers = jnp.arange(half_size, dtype=F32) * (2.0 / HEAD_WIDTH)
    speeds = jnp.power(ROPE_BASE, -powers)
    angles = angles_at[:, None] * speeds[None, :]
    cosine, sine = jnp.cos(angles), jnp.sin(angles)
    return (jnp.concatenate([cosine] * 4, axis=1), jnp.concatenate([-sine, sine] * 2, axis=1))


def rotate_pairs(values, cosine, sine):
    width = values.shape[1]
    half_size = HEAD_WIDTH // 2
    lanes = lax.broadcasted_iota(jnp.int32, values.shape, 1) % HEAD_WIDTH
    ahead = pltpu.roll(values, width - half_size, 1)
    behind = pltpu.roll(values, half_size, 1)
    return values * cosine + jnp.where(lanes < half_size, ahead, behind) * sine


def wide_table(table, width):
    return jnp.concatenate([table] * (width // table.shape[1]), axis=1)


def low_high(rows):
    low = [rows[at : at + 64] for at in range(0, rows.shape[0], 128)]
    high = [rows[at + 64 : at + 128] for at in range(0, rows.shape[0], 128)]
    return jnp.concatenate(low, axis=0), jnp.concatenate(high, axis=0)


def stack_heads(rows, head):
    pieces = [
        rows[at : at + 64, (4 * head + step) * HEAD_WIDTH : (4 * head + step + 1) * HEAD_WIDTH]
        for at in (0, 64)
        for step in range(4)
    ]
    return jnp.concatenate(pieces, axis=0)


def unstack_heads(stack):
    halves = [
        jnp.concatenate([stack[at + 64 * step : at + 64 * step + 64] for step in range(4)], axis=1)
        for at in (0, 256)
    ]
    return jnp.concatenate(halves, axis=0)


def mask_bias(keys_ref, rows_ref):
    columns = keys_ref[...].T
    keys_low, keys_high = columns[:512], columns[512:]

    def bias(keys, lanes):
        seen = (keys[:, 0:1] <= rows_ref[0:1, lanes]) | (keys[:, 1:2] == rows_ref[1:2, lanes])
        return jnp.where(seen, 0.0, MASKED_SCORE).astype(F32)

    return bias(keys_low, slice(0, 512)), bias(keys_high, slice(256, 512))


def attend_kernel(q_ref, part_ref, kv_ref, cos_ref, sin_ref, keys_ref, rows_ref, out_ref, turned_ref, log_ref):
    cosine = wide_table(cos_ref[...], QUERY_WIDTH)
    sine = wide_table(sin_ref[...], QUERY_WIDTH)
    queries = q_ref[...] + part_ref[...].astype(F32)
    queries = (rotate_pairs(queries, cosine, sine) * HEAD_WIDTH**-0.5).astype(BF16)
    turned_ref[...] = queries
    kv_low, kv_high = low_high(kv_ref[...])
    bias_low, bias_high = mask_bias(keys_ref, rows_ref)
    for head in range(KEY_VALUE_HEADS):
        at = slice(head * HEAD_WIDTH, (head + 1) * HEAD_WIDTH)
        vat = slice(KEY_WIDTH + head * HEAD_WIDTH, KEY_WIDTH + (head + 1) * HEAD_WIDTH)
        stack = stack_heads(queries, head)
        score_low = mm_nt(kv_low[:, at], stack) + bias_low
        score_high = mm_nt(kv_high[:, at], stack[256:]) + bias_high
        top_low = jnp.max(score_low, axis=0, keepdims=True)
        top_high = jnp.max(score_high, axis=0, keepdims=True)
        top = jnp.concatenate(
            [top_low[:, :256], jnp.maximum(top_low[:, 256:], top_high)], axis=1
        )
        exp_low = jnp.exp(score_low - top)
        exp_high = jnp.exp(score_high - top[:, 256:])
        total = jnp.sum(exp_low, axis=0, keepdims=True)
        total_high = jnp.sum(exp_high, axis=0, keepdims=True)
        total = jnp.concatenate([total[:, :256], total[:, 256:] + total_high], axis=1)
        result = mm_tn(kv_low[:, vat], exp_low.astype(BF16))
        result_high = mm_tn(kv_high[:, vat], exp_high.astype(BF16))
        result = jnp.concatenate([result[:, :256], result[:, 256:] + result_high], axis=1)
        result = (result / total).T
        out_ref[:, head * 256 : (head + 1) * 256] = unstack_heads(result).astype(BF16)
        log_ref[head : head + 1, :] = top + jnp.log(total)


def attend_back_kernel(
    q_ref, kv_ref, out_ref, grad_ref, log_ref, cos_ref, sin_ref, keys_ref, rows_ref, dq_ref, dkv_ref
):
    kv_low, kv_high = low_high(kv_ref[...])
    bias_low, bias_high = mask_bias(keys_ref, rows_ref)
    queries = q_ref[...]
    outs = out_ref[...]
    grads = grad_ref[...]
    ones = jnp.ones((8, HEAD_WIDTH), F32)
    dq_parts, dk_low, dk_high, dv_low, dv_high = [], [], [], [], []
    for head in range(KEY_VALUE_HEADS):
        at = slice(head * HEAD_WIDTH, (head + 1) * HEAD_WIDTH)
        vat = slice(KEY_WIDTH + head * HEAD_WIDTH, KEY_WIDTH + (head + 1) * HEAD_WIDTH)
        stack = stack_heads(queries, head)
        grad = stack_heads(grads, head)
        product = grad.astype(F32) * stack_heads(outs, head).astype(F32)
        delta = lax.dot_general(
            ones,
            product,
            (((1,), (1,)), ((), ())),
            preferred_element_type=F32,
            precision=lax.Precision.HIGHEST,
        )[0:1]
        logs = log_ref[head : head + 1, :]
        key_low, key_high = kv_low[:, at], kv_high[:, at]
        probs_low = jnp.exp(mm_nt(key_low, stack) + bias_low - logs)
        probs_high = jnp.exp(mm_nt(key_high, stack[256:]) + bias_high - logs[:, 256:])
        back_low = mm_nt(kv_low[:, vat], grad)
        back_high = mm_nt(kv_high[:, vat], grad[256:])
        score_low = (probs_low * (back_low - delta)).astype(BF16)
        score_high = (probs_high * (back_high - delta[:, 256:])).astype(BF16)
        dv_low.append(mm(probs_low.astype(BF16), grad))
        dv_high.append(mm(probs_high.astype(BF16), grad[256:]))
        dk_low.append(mm(score_low, stack))
        dk_high.append(mm(score_high, stack[256:]))
        dq = mm_tn(key_low, score_low)
        dq_high = mm_tn(key_high, score_high)
        dq = jnp.concatenate([dq[:, :256], dq[:, 256:] + dq_high], axis=1)
        dq_parts.append(unstack_heads((dq * HEAD_WIDTH**-0.5).T))
    cosine = wide_table(cos_ref[...], QUERY_WIDTH)
    sine = wide_table(sin_ref[...], QUERY_WIDTH)
    dq_ref[...] = rotate_pairs(jnp.concatenate(dq_parts, axis=1), cosine, -sine).astype(BF16)
    low = jnp.concatenate(dk_low + dv_low, axis=1).astype(BF16)
    high = jnp.concatenate(dk_high + dv_high, axis=1).astype(BF16)
    for at in range(8):
        dkv_ref[128 * at : 128 * at + 64] = low[64 * at : 64 * at + 64]
        dkv_ref[128 * at + 64 : 128 * at + 128] = high[64 * at : 64 * at + 64]


def run_kernel(kernel, shapes, operands, flops, limit=KERNEL_BYTES):
    return pl.pallas_call(
        kernel,
        out_shape=[jax.ShapeDtypeStruct(shape, kind) for shape, kind in shapes],
        in_specs=[pl.BlockSpec(memory_space=pltpu.VMEM)] * len(operands),
        out_specs=[pl.BlockSpec(memory_space=pltpu.VMEM)] * len(shapes),
        compiler_params=pltpu.CompilerParams(vmem_limit_bytes=limit),
        cost_estimate=pl.CostEstimate(
            flops=flops,
            bytes_accessed=sum(v.size * v.dtype.itemsize for v in operands),
            transcendentals=0,
        ),
    )(*operands)


def pair_kernel(
    moved_ref,
    factor_ref,
    part_ref,
    other_ref,
    cos_ref,
    sin_ref,
    pairs_ref,
    normed_ref,
    halves_ref,
    gains_ref,
):
    half = part_ref.shape[0]
    pair_cols = 2 * KEY_WIDTH
    gains = [ref[:, pair_cols:].astype(F32).T[:8] for ref in (part_ref, other_ref)]
    gains = jnp.concatenate(gains, axis=1)
    gains_ref[...] = gains
    scaled = moved_ref[...] * factor_ref[...]
    normed = (scaled * gains[0:1]).astype(BF16)
    normed_ref[...] = normed
    halves_ref[...] = normed[:, half:]
    both = mm(normed[:, :half], part_ref[:, :pair_cols]) + mm(
        normed[:, half:], other_ref[:, :pair_cols]
    )
    wide = 3 * cos_ref.shape[1]
    turned = rotate_pairs(
        both[:, :wide], wide_table(cos_ref[...], wide), wide_table(sin_ref[...], wide)
    )
    pairs = jnp.concatenate([turned[:, :KEY_WIDTH], both[:, KEY_WIDTH:]], axis=1).astype(BF16)
    for at in range(8):
        pairs_ref[at] = pairs


def pair_back_kernel(parts_ref, cos_ref, sin_ref, low_ref):
    total = parts_ref[0].astype(F32)
    for at in range(1, 8):
        total = total + parts_ref[at].astype(F32)
    wide = 3 * cos_ref.shape[1]
    turned = rotate_pairs(
        total[:, :wide], wide_table(cos_ref[...], wide), -wide_table(sin_ref[...], wide)
    )
    low_ref[...] = jnp.concatenate(
        [turned[:, :KEY_WIDTH], total[:, KEY_WIDTH:]], axis=1
    ).astype(BF16)


def middle_kernel(
    own_swap,
    back_a,
    back_b,
    back_c,
    back_d,
    cot_ref,
    weight_ref,
    middle_ref,
    factor_ref,
    gain_ref,
    hot_slice_ref,
    part_ref,
    other_ref,
    hot_ref,
    mid_ref,
    branch_ref,
    grad_ref,
    hot_slice,
    parts,
    hot,
    sems,
):
    half = part_ref.shape[0]
    copies = [
        pltpu.make_async_copy(hot_slice_ref, hot_slice, sems.at[0]),
        pltpu.make_async_copy(part_ref, parts.at[0:half], sems.at[1]),
        pltpu.make_async_copy(other_ref, parts.at[half : 2 * half], sems.at[2]),
        pltpu.make_async_copy(hot_ref, hot, sems.at[3]),
    ]
    for copy in copies:
        copy.start()
    total = own_swap[...].astype(F32) + back_a[...].astype(F32) + back_b[...].astype(F32)
    total = total + back_c[...].astype(F32)
    total = (total + back_d[...].astype(F32)).astype(BF16)
    copies[0].wait()
    grad = mm(total, hot_slice[...])
    middle, factor = middle_ref[...], factor_ref[...]
    mid = cot_ref[...].astype(F32) * weight_ref[...] + norm_back(middle, factor, gain_ref[...], grad)
    mid_ref[...] = mid
    branch = mid.astype(BF16)
    branch_ref[...] = branch
    copies[1].wait()
    copies[2].wait()
    moved = mm_nt(branch, parts[...]).astype(BF16)
    copies[3].wait()
    grad_ref[...] = mm(moved, hot[...]).astype(BF16)


def middle_call(small, large):
    vmem, hbm = pl.BlockSpec(memory_space=pltpu.VMEM), pl.BlockSpec(memory_space=pltpu.HBM)
    rows, width = small[0].shape
    square = pltpu.VMEM((width, width), BF16)
    return pl.pallas_call(
        middle_kernel,
        out_shape=[jax.ShapeDtypeStruct((rows, width), kind) for kind in (F32, BF16, BF16)],
        in_specs=[vmem] * len(small) + [hbm] * len(large),
        out_specs=[vmem] * 3,
        scratch_shapes=[square, square, square, pltpu.SemaphoreType.DMA((4,))],
        compiler_params=pltpu.CompilerParams(vmem_limit_bytes=LARGE_BYTES),
        cost_estimate=pl.CostEstimate(
            flops=6 * rows * width * width, bytes_accessed=16 * 2**20, transcendentals=0
        ),
    )(*small, *large)


def finish_kernel(
    feed_a, feed_b, feed_c, feed_d, middle_ref, branch_ref, weight_ref, out_ref, sums_ref
):
    feed = feed_a[...].astype(F32) + feed_b[...].astype(F32) + feed_c[...].astype(F32)
    feed = feed + feed_d[...].astype(F32)
    final = middle_ref[...] + feed
    out_ref[...] = final.astype(BF16)
    sums_ref[...] = jnp.zeros(sums_ref.shape, F32)
    for row, values in enumerate((branch_ref[...], feed, final)):
        part = jnp.sum(weight_ref[...] * values * values, axis=0, keepdims=True)
        part = jnp.sum(part, axis=1, keepdims=True)
        sums_ref[row : row + 1] = jnp.broadcast_to(part, (1, 128))


def query_kernel(
    normed_ref,
    halves_ref,
    a_ref,
    b_ref,
    c_ref,
    d_ref,
    own_ref,
    other_ref,
    both_ref,
    query_ref,
    out_ref,
    sems,
):
    width, count = query_ref.shape[1], a_ref.shape[0]
    copies = []
    for step, block in enumerate((a_ref, b_ref, c_ref, d_ref)):
        at = slice(step * count, (step + 1) * count)
        copies.append(
            pltpu.make_async_copy(block.at[:, 0:width], query_ref.at[at], sems.at[step])
        )
    for step, block in enumerate((a_ref, b_ref, c_ref, d_ref)):
        at = slice(step * count, (step + 1) * count)
        copies.append(
            pltpu.make_async_copy(
                block.at[:, width : 2 * width], out_ref.at[at], sems.at[4 + step]
            )
        )
    for copy in copies:
        copy.start()
    for copy in copies[:4]:
        copy.wait()
    half = own_ref.shape[0]
    both_ref[0:half] = normed_ref[:, : both_ref.shape[1]]
    both_ref[half : 2 * half] = halves_ref[...]
    both = mm(both_ref[...], query_ref[...])
    own_ref[...] = both[:half]
    other_ref[...] = both[half:].astype(BF16)
    for copy in copies[4:]:
        copy.wait()


def query_parts(normed, halves, blocks):
    vmem = pl.BlockSpec(memory_space=pltpu.VMEM)
    half, width = normed.shape[0], QUERY_WIDTH
    joined = jax.ShapeDtypeStruct((4 * blocks[0].shape[0], width), BF16)
    return pl.pallas_call(
        query_kernel,
        out_shape=[
            jax.ShapeDtypeStruct((half, width), F32),
            jax.ShapeDtypeStruct((half, width), BF16),
            jax.ShapeDtypeStruct((2 * half, halves.shape[1]), BF16),
            joined,
            joined,
        ],
        in_specs=[vmem] * 2 + [pl.BlockSpec(memory_space=pltpu.HBM)] * 4,
        out_specs=[vmem] * 5,
        scratch_shapes=[pltpu.SemaphoreType.DMA((8,))],
        compiler_params=pltpu.CompilerParams(vmem_limit_bytes=LARGE_BYTES),
        cost_estimate=pl.CostEstimate(
            flops=4 * halves.size * width, bytes_accessed=10 * 2**20, transcendentals=0
        ),
    )(normed, halves, *blocks)


def unpack_kernel(slices_ref, units_ref, down_ref):
    for block in range(16):
        base, at = block * 128, block * 32
        units_ref[block * 80 : block * 80 + 80] = slices_ref[base : base + 80]
        down_ref[at : at + 32, :1024] = slices_ref[base + 80 : base + 112]
        down_ref[at : at + 16, 1024:] = slices_ref[base + 112 : base + 128, :256]
        down_ref[at + 16 : at + 32, 1024:] = slices_ref[base + 112 : base + 128, 256:512]


def unpack_slices(slices):
    return run_kernel(
        unpack_kernel, [((1280, 1024), BF16), ((512, 1280), BF16)], (slices,), 0, FEED_BYTES
    )


def feed_kernel(
    xa_ref,
    xb_ref,
    all_grads_ref,
    places_ref,
    valid_ref,
    units_ref,
    down_ref,
    hidden_ref,
    unit_ref,
    back_a_ref,
    back_b_ref,
    out_a_ref,
    out_b_ref,
    rows_ref,
    grads_ref,
    sems,
    *,
    step,
):
    half = xa_ref.shape[0]
    low = slice(0, half)
    high = slice(half, 2 * half)
    spot_a = pl.ds(pl.multiple_of(places_ref[step], half), half)
    spot_b = pl.ds(pl.multiple_of(places_ref[step + 4], half), half)
    copies = [
        pltpu.make_async_copy(xa_ref, rows_ref.at[low], sems.at[0]),
        pltpu.make_async_copy(xb_ref, rows_ref.at[high], sems.at[1]),
    ]
    copies += [
        pltpu.make_async_copy(all_grads_ref.at[spot_a], grads_ref.at[low], sems.at[2]),
        pltpu.make_async_copy(all_grads_ref.at[spot_b], grads_ref.at[high], sems.at[3]),
    ]
    for copy in copies:
        copy.start()
    copies[0].wait()
    copies[1].wait()
    units = units_ref.shape[1] // 2
    both = mm(rows_ref[...], units_ref[...])
    gate, up = both[:, :units], both[:, units:]
    sigmoid = 1.0 / (1.0 + jnp.exp(-gate))
    silu = gate * sigmoid
    hidden = silu * up
    columns = valid_ref[...].T
    valid = jnp.concatenate(
        [columns[:, step : step + 1], columns[:, step + 4 : step + 5]], axis=0
    )
    hidden_ref[...] = (hidden * valid).astype(BF16)
    hidden = hidden.astype(BF16)
    for copy in copies[2:]:
        copy.wait()
    hidden_grad = mm_nt(grads_ref[...], down_ref[...]) * valid
    gate_low = (hidden_grad * up * sigmoid * (1.0 + gate * (1.0 - sigmoid))).astype(BF16)
    up_low = (hidden_grad * silu).astype(BF16)
    unit = jnp.concatenate([gate_low, up_low], axis=1)
    unit_ref[...] = unit
    back = mm_nt(unit, units_ref[...]).astype(BF16)
    back_a_ref[...] = back[:half]
    back_b_ref[...] = back[half:]
    outs = mm(hidden, down_ref[...]).astype(BF16)
    out_a_ref[...] = outs[:half]
    out_b_ref[...] = outs[half:]


def feed_chunk(step, rows_a, rows_b, all_grads, places, valid, units, down):
    count, width = rows_a.shape[0] * 2, rows_a.shape[1]
    vmem = pl.BlockSpec(memory_space=pltpu.VMEM)
    hbm = pl.BlockSpec(memory_space=pltpu.HBM)
    shapes = [(count, 512), (count, 1024)] + [rows_a.shape] * 4
    return pl.pallas_call(
        functools.partial(feed_kernel, step=step),
        out_shape=[jax.ShapeDtypeStruct(shape, BF16) for shape in shapes],
        in_specs=[hbm] * 3 + [pl.BlockSpec(memory_space=pltpu.SMEM)] + [vmem] * 3,
        out_specs=[vmem] * 6,
        scratch_shapes=[
            pltpu.VMEM((count, width), BF16),
            pltpu.VMEM((count, width), BF16),
            pltpu.SemaphoreType.DMA((4,)),
        ],
        compiler_params=pltpu.CompilerParams(vmem_limit_bytes=FEED_BYTES),
        cost_estimate=pl.CostEstimate(
            flops=2 * count * width * 3 * 1024,
            bytes_accessed=2 * (units.size + down.size + 4 * rows_a.size),
            transcendentals=0,
        ),
    )(rows_a, rows_b, all_grads, places, valid, units, down)


def weight_kernel(*refs):
    sources, all_grads, places, term_out = refs[:24], refs[24], refs[25], refs[26]
    feed_outs = refs[27:31]
    grads, terms, in_sems, out_sems = refs[31:]
    copies = []
    for step in range(4):
        base = step * 256
        for place, start in ((step, base), (step + 4, base + 128)):
            spot = pl.ds(pl.multiple_of(places[place], 128), 128)
            copies.append(
                pltpu.make_async_copy(
                    all_grads.at[spot], grads.at[start : start + 128], in_sems.at[len(copies)]
                )
            )
    for copy in copies:
        copy.start()
    for step in range(4):
        total = sources[step + 16][...].astype(F32) + sources[step + 20][...].astype(F32)
        feed_outs[step][...] = total.astype(BF16)
    for at in range(0, 16, 4):
        lanes = slice(at * 80, at * 80 + 320)
        total = None
        for step in range(4):
            pair = jnp.concatenate([sources[step][:, lanes], sources[step + 4][:, lanes]], axis=0)
            term = mm_tn(pair, sources[step + 12][...])
            total = term if total is None else total + term
        total = total.astype(BF16)
        for step in range(4):
            base = (at + step) * 128
            terms[base : base + 80] = total[step * 80 : step * 80 + 80]
    for copy in copies:
        copy.wait()
    hidden = jnp.concatenate([sources[step + 8][...] for step in range(4)], axis=0)
    moves = []
    for at in range(0, 16, 4):
        total = mm_tn(hidden[:, at * 32 : at * 32 + 128], grads[...]).astype(BF16)
        for step in range(4):
            rows_here = total[step * 32 : step * 32 + 32]
            base = (at + step) * 128
            terms[base + 80 : base + 112] = rows_here[:, :1024]
            terms[base + 112 : base + 128, 0:256] = rows_here[:16, 1024:]
            terms[base + 112 : base + 128, 256:512] = rows_here[16:, 1024:]
            terms[base + 112 : base + 128, 512:] = jnp.zeros((16, 512), BF16)
        piece = slice(at * 128, at * 128 + 512)
        moves.append(
            pltpu.make_async_copy(terms.at[piece], term_out.at[piece], out_sems.at[at // 4])
        )
        moves[-1].start()
    for move in moves:
        move.wait()


def weight_terms(rows, all_grads, places, chunks, feed_swaps):
    sources = list(rows)
    for part in (0, 1, 4):
        sources += [chunk[part] for chunk in chunks]
    sources += list(feed_swaps)
    count, width = 8 * rows[0].shape[0], rows[0].shape[1]
    smem, hbm = pl.BlockSpec(memory_space=pltpu.SMEM), pl.BlockSpec(memory_space=pltpu.HBM)
    return pl.pallas_call(
        weight_kernel,
        out_shape=[jax.ShapeDtypeStruct((2048, 1024), BF16)]
        + [jax.ShapeDtypeStruct(rows[0].shape, BF16)] * 4,
        in_specs=[pl.BlockSpec(memory_space=pltpu.VMEM)] * 24 + [hbm, smem],
        out_specs=[hbm] + [pl.BlockSpec(memory_space=pltpu.VMEM)] * 4,
        scratch_shapes=[
            pltpu.VMEM((count, width), BF16),
            pltpu.VMEM((2048, 1024), BF16),
            pltpu.SemaphoreType.DMA((8,)),
            pltpu.SemaphoreType.DMA((4,)),
        ],
        compiler_params=pltpu.CompilerParams(vmem_limit_bytes=24 * 1024 * 1024),
        cost_estimate=pl.CostEstimate(
            flops=2 * count * 1280 * 1536, bytes_accessed=2**20, transcendentals=0
        ),
    )(*sources, all_grads, places)


def term_kernel(normed_ref, q_ref, qs_ref, attended_ref, as_ref, b_ref, bs_ref, *outs):
    count = outs[0].shape[0]
    half = normed_ref.shape[1]
    queries = jnp.concatenate([q_ref[...], qs_ref[...]], axis=0)
    outs[4][...] = queries
    branch = jnp.concatenate([b_ref[...], bs_ref[...]], axis=0)
    attended = jnp.concatenate([attended_ref[:, :half], as_ref[...]], axis=0)
    query_term = mm_tn(normed_ref[...], queries).astype(BF16)
    out_term = mm_tn(attended, branch).astype(BF16)
    for step in range(4):
        at = slice(step * count, (step + 1) * count)
        outs[step][:, :QUERY_WIDTH] = query_term[at]
        outs[step][:, QUERY_WIDTH:] = out_term[at]


def pack_slice(units, down):
    rest = jnp.concatenate([down[:16, 1024:], down[16:, 1024:]], axis=1)
    rest = jnp.pad(rest, ((0, 0), (0, 512)))
    return jnp.concatenate([units, down[:, :1024], rest], axis=0)


def unpack_down(rows):
    rest = jnp.concatenate([rows[32:, :256], rows[32:, 256:512]], axis=0)
    return jnp.concatenate([rows[:32], rest], axis=1)


def group_places(pair_row, devices_ctx, block_size):
    slots = jnp.arange(devices_ctx * 2 * block_size, dtype=jnp.int32)
    owners = slots // (2 * block_size)
    inside = slots % (2 * block_size)
    columns = jnp.arange(devices_ctx, dtype=jnp.int32)
    paired = jnp.sum(jnp.where(owners[:, None] == columns[None, :], pair_row[None, :], 0), axis=1)
    blocks = jnp.where(inside < block_size, paired, 2 * devices_ctx - 1 - paired)
    return blocks * block_size + inside % block_size


def pack_units(weight):
    rows = weight.shape[0]
    runs = weight.reshape(rows, 8, 4, 2, 2, 28).transpose(1, 0, 2, 4, 3, 5)
    runs = jnp.pad(runs, ((0, 0),) * 5 + ((0, PAD_UNITS - 28),))
    return runs.reshape(8, rows, 16 * PAD_UNITS)


def unpack_units(packed):
    rows = packed.shape[1]
    runs = packed.reshape(8, rows, 4, 2, 2, PAD_UNITS)[..., :28]
    return runs.transpose(1, 0, 2, 4, 3, 5).reshape(rows, 8 * 16 * 28)


def local(
    tokens,
    norm_gain,
    w_query,
    w_key,
    w_value,
    w_out,
    mlp_gain,
    w_gate,
    w_up,
    w_down,
    block_pair,
    seq_len,
    seq_start,
    out_grad,
):
    shard_rows, model_width = tokens.shape
    block_size = shard_rows // 2
    half = model_width // 2
    devices_ctx = 8
    at_y, at_zh, at_x, at_zl, at_core = (lax.axis_index(name) for name in AXES)
    place = (at_x, at_y, at_zh * 2 + at_zl)
    position = at_y * 2 + at_zh
    pair_cols = 2 * KEY_WIDTH
    split = pair_cols + GAIN_COLS

    first_slot = seq_start[0]
    seq_length = seq_len[0]
    grad_rows = lax.all_gather(out_grad, ROW_AXES, axis=0, tiled=True)
    gains = jnp.stack([norm_gain, mlp_gain], axis=1)
    gains = jnp.pad(gains, ((0, 0), (0, GAIN_COLS - 2)))
    front = jnp.concatenate([w_key, w_value, gains, w_query, w_out], axis=1)
    front = spread(front, 0)
    units = jnp.concatenate([pack_units(w_gate), pack_units(w_up)], axis=2)
    *arrived, units, tokens, block_pair, out_grad = phase(
        *front, units, tokens, block_pair, out_grad
    )

    front = spread(join(arrived), 1)
    units = lax.all_to_all(units, ROW_AXES, 0, 0, tiled=True)
    down_rows = jnp.pad(w_down, ((0, PAD_UNITS - w_down.shape[0]), (0, 0)))
    down_rows = swap_half_core(after(down_rows, block_pair))
    places_all = group_places(block_pair[0], devices_ctx, block_size)
    places_here = lax.dynamic_slice_in_dim(places_all, position * shard_rows, shard_rows)
    valid_here = (places_here >= first_slot) & (places_here < first_slot + seq_length)
    row_weight = valid_here.astype(F32)[:, None]
    valid_all = (places_all >= first_slot) & (places_all < first_slot + seq_length)
    ring_valid = valid_all.astype(F32).reshape(4, 2, shard_rows)
    ring_valid = lax.dynamic_index_in_dim(ring_valid, at_zh, 1, keepdims=False)
    ring_valid = lax.dynamic_slice_in_dim(
        jnp.concatenate([ring_valid, ring_valid]), at_y, 4, axis=0
    )
    ring_valid = jnp.concatenate([ring_valid, swap_cores(ring_valid)])
    key_places = jnp.stack([jnp.where(valid_all, places_all, 1 << 20), places_all])
    key_places = jnp.concatenate(
        [key_places[:, at : at + 64] for side in (0, 64) for at in range(side, 1024, 128)], axis=1
    )
    key_places = jnp.pad(key_places, ((0, 6), (0, 0)))
    row_places = jnp.stack([jnp.where(valid_here, places_here, -1), places_here])
    row_places = jnp.concatenate([row_places[:, :64]] * 4 + [row_places[:, 64:]] * 4, axis=1)
    cosine, sine = rope_tables((places_here - first_slot).astype(F32))
    inputs = tokens.astype(F32)
    factor_one = norm_factor(inputs)
    *arrived, factor_one, order_seed = phase(*front, factor_one, at_core)

    key_part = join([block[:, :split] for block in arrived])
    units, down_rows = after((units, down_rows), key_part)
    slices = pack_slice(units.reshape(-1, units.shape[2]), down_rows)
    slices = lax.all_gather(after(slices, grad_rows), SLICE_AXES, axis=0, tiled=True)
    key_part = spread(key_part, 2)
    rest = join([block[:, split:] for block in arrived])
    orders = [row_order(place, core) for core in (0, 1)]
    mine = jnp.where(order_seed == 0, orders[0], orders[1])
    other = jnp.where(order_seed == 0, orders[1], orders[0])
    order = jnp.concatenate([mine, other])
    hot = one_hot(order)
    tokens_moved = mm(tokens, hot)
    *key_part, rest, hot, tokens_moved, order = phase(
        *key_part, rest, hot, tokens_moved, order
    )

    rest_part = spread(rest, 2)
    key_part = join(key_part)
    key_part, key_other = phase(key_part, swap_cores(key_part))

    pairs, normed, halves, gain_rows = run_kernel(
        pair_kernel,
        [
            ((devices_ctx, shard_rows, pair_cols), BF16),
            ((shard_rows, model_width), BF16),
            ((shard_rows, half), BF16),
            ((8, model_width), F32),
        ],
        (tokens_moved, factor_one, key_part, key_other, cosine, sine),
        2 * shard_rows * model_width * pair_cols,
        LARGE_BYTES,
    )
    gain_one = gain_rows[0:1]

    def project(rows, part, other_part):
        return mm(rows[:, :half], part) + mm(rows[:, half:], other_part)

    gathered = lax.all_to_all(pairs, ("y", "zh"), 0, 0, tiled=True)
    gathered = gathered.reshape(devices_ctx * shard_rows, pair_cols)
    halves = swap_cores(halves)
    hot_back = one_hot_back(order)
    gain_two = mm(gain_rows.astype(BF16), hot_back)[1:2]
    slice_places = after(jnp.asarray(slice_order()), order)
    slice_hot, slice_back = one_hot(slice_places), one_hot_back(slice_places)
    grad_places = jnp.stack(
        [
            ((at_y + step) % 4 * 2 + (at_core + side) % 2) * shard_rows
            for side in (0, 1)
            for step in range(4)
        ]
    ).astype(jnp.int32)
    (
        *rest_part,
        gathered,
        gain_two,
        halves,
        slice_hot,
        slice_back,
        hot_back,
        grad_places,
        ring_valid,
        row_weight,
    ) = phase(
        *rest_part,
        gathered,
        gain_two,
        halves,
        slice_hot,
        slice_back,
        hot_back,
        grad_places,
        ring_valid,
        row_weight,
    )

    query_own, query_other, normed_both, query_part, out_part = query_parts(
        normed, halves, rest_part
    )
    query_other = swap_cores(query_other)
    out_other = swap_cores(after(out_part, query_other))
    attended, queries, logs = run_kernel(
        attend_kernel,
        [((shard_rows, QUERY_WIDTH), BF16), ((shard_rows, QUERY_WIDTH), BF16), ((8, 512), F32)],
        (query_own, query_other, gathered, cosine, sine, key_places, row_places),
        shard_rows * 1024 * QUERY_WIDTH * 4,
        LARGE_BYTES,
    )
    attended_moved = mm(attended, hot).astype(BF16)
    branch = project(attended_moved, out_part, out_other)
    middle = inputs + branch
    factor_two = norm_factor(middle)
    normed_two = (middle * factor_two * gain_two).astype(BF16)
    normed_two = mm(normed_two, slice_hot).astype(BF16)
    normed_two, middle, factor_two, branch = phase(normed_two, middle, factor_two, branch)

    ahead, behind = along_y(normed_two, -1), along_y(normed_two, 1)
    cut_at = shard_rows // 2
    row_blocks = [normed_two, ahead, None, behind, swap_cores(normed_two), None, None, None]
    units_full, down_full = unpack_slices(slices)
    chunks = [None] * 4
    back_parts, ready, feed_swaps = [None] * 4, [None] * 4, [None] * 4
    for step in (0, 1, 3, 2):
        if step == 1:
            ahead, behind = after((ahead, behind), chunks[0][0])
            across = [along_y(ahead[:cut_at], -1), along_y(behind[cut_at:], 1)]
            row_blocks[1], row_blocks[3] = ahead, behind
        if step == 2:
            row_blocks[2] = jnp.concatenate(after(tuple(across), chunks[1][0]), axis=0)
        if step:
            row_blocks[step + 4] = swap_cores(row_blocks[step])
        block = after(row_blocks[step], ready[1], ready[3]) if step == 2 else row_blocks[step]
        chunks[step] = feed_chunk(
            step,
            block,
            row_blocks[step + 4],
            grad_rows,
            grad_places,
            ring_valid,
            units_full,
            down_full,
        )
        swapped = swap_cores(chunks[step][3])
        feed_swaps[step] = swap_cores(chunks[step][5])
        total = chunks[step][2].astype(F32) + swapped.astype(F32)
        ready[step] = total.astype(BF16) if step else swapped
        back_parts[step] = along_y(ready[step], step) if step else None
    terms, *feed_sums = weight_terms(
        row_blocks[:1] + [after(block, *ready) for block in row_blocks[1:]],
        grad_rows,
        grad_places,
        chunks,
        feed_swaps,
    )
    back_parts[0] = chunks[0][2]
    attended_swap = swap_cores(attended_moved[:, half:])
    *arrived, attended_swap, terms, own_swap = phase(
        *back_parts, *feed_sums, attended_swap, terms, ready[0]
    )
    back_parts, feed_sums = arrived[:4], arrived[4:]
    terms = lax.psum_scatter(terms, "x", scatter_dimension=0, tiled=True)

    units_here = 16 * PAD_UNITS
    feed_parts = [feed_sums[0]] + [along_y(feed_sums[step], step) for step in (1, 2, 3)]
    mid_grad, branch_grad, attended_grad = middle_call(
        (own_swap, *back_parts, out_grad, row_weight, middle, factor_two, gain_two),
        (slice_back, out_part, out_other, hot_back),
    )
    branch_swap = swap_cores(branch_grad)
    attended_grad = after(attended_grad, feed_parts[1])
    query_low, pair_grads = run_kernel(
        attend_back_kernel,
        [((shard_rows, QUERY_WIDTH), BF16), ((1024, pair_cols), BF16)],
        (
            queries,
            gathered,
            attended,
            attended_grad,
            logs,
            cosine,
            sine,
            key_places,
            row_places,
        ),
        shard_rows * 1024 * QUERY_WIDTH * 10,
        LARGE_BYTES,
    )
    *feed_parts, query_low, pair_grads, mid_grad, branch_grad, branch_swap = phase(
        *feed_parts, query_low, pair_grads, mid_grad, branch_grad, branch_swap
    )

    pair_grads = lax.all_to_all(
        pair_grads.reshape(devices_ctx, shard_rows, pair_cols), ("y", "zh"), 0, 0, tiled=True
    )
    query_swap = swap_cores(query_low)
    *rest_term, query_both = run_kernel(
        term_kernel,
        [((160, 2 * QUERY_WIDTH), BF16)] * 4 + [((2 * shard_rows, QUERY_WIDTH), BF16)],
        (
            normed_both,
            query_low,
            query_swap,
            attended_moved,
            attended_swap,
            branch_grad,
            branch_swap,
        ),
        4 * half * 2 * shard_rows * QUERY_WIDTH,
        LARGE_BYTES,
    )
    rest_blocks = scatter(rest_term, 2)
    activations, sums = run_kernel(
        finish_kernel,
        [((shard_rows, model_width), BF16), ((8, 128), F32)],
        (*feed_parts, middle, branch, row_weight),
        0,
        LARGE_BYTES,
    )
    sums_one = send(sums, lambda x, y, z, core: (x, y, z + 2, core))
    pair_grads, query_both, sums, sums_one, terms = phase(
        pair_grads, query_both, sums, sums_one, terms
    )
    terms = terms.reshape(4, 128, terms.shape[1])
    unit_parts = lax.all_to_all(
        terms[:, :80].reshape(32, 10, terms.shape[2]), ("zh", "zl", "y", "core"), 0, 0, tiled=True
    )
    down_term = lax.psum_scatter(
        terms[:, 80:].reshape(192, terms.shape[2]), ("zh", "zl"), scatter_dimension=0, tiled=True
    )

    (pair_low,) = run_kernel(
        pair_back_kernel,
        [((shard_rows, pair_cols), BF16)],
        (pair_grads, cosine, sine),
        0,
    )
    pair_both = jnp.concatenate([pair_low, swap_cores(pair_low)])
    query_back = mm_nt(query_both, query_part)
    sums = sums + sums_one
    sums_one = send(sums, lambda x, y, z, core: (x, y ^ 1, z, core))
    pair_both, query_back = phase(pair_both, query_back)

    normed_grad = query_back + mm_nt(pair_both, key_part[:, :pair_cols])
    pair_term = mm_tn(normed_both, pair_both)
    pair_cuts = cut(pair_term)
    pair_blocks = scatter(pair_cuts, 2)
    normed_grad_swap = swap_cores(after(normed_grad, pair_cuts[1])[shard_rows:].astype(BF16))
    normed_grad = jnp.concatenate(
        [normed_grad[:shard_rows], after(normed_grad_swap, pair_cuts[1]).astype(F32)], axis=1
    )
    input_part = norm_back(tokens_moved, factor_one, gain_one, normed_grad)
    input_grad = (mid_grad + mm(input_part.astype(BF16), hot_back)).astype(BF16)
    rest_total = add_up([after(rest_blocks[0], pair_cuts[1])] + rest_blocks[1:])
    (
        *pair_blocks,
        rest_total,
        sums,
        sums_one,
        input_grad,
    ) = phase(
        *pair_blocks,
        rest_total,
        sums,
        sums_one,
        input_grad,
    )

    cuts = cut(jnp.concatenate([add_up(pair_blocks), rest_total], axis=1))
    blocks = scatter(cuts, 1)
    down_sum = swap_half_core(unpack_down(after(down_term, cuts[1])))
    unit_parts = after(unit_parts, cuts[1]).reshape(4, 8, 10, -1)
    unit_term = jnp.sum(unit_parts.astype(F32), axis=0)
    sums = sums + sums_one
    sums_one = send(sums, lambda x, y, z, core: (x, y ^ 2, z, core))
    *blocks, unit_term, down_sum, sums, sums_one = phase(
        *blocks, unit_term, down_sum, sums, sums_one
    )

    cuts = cut(add_up(blocks))
    blocks = scatter(cuts, 0)
    unit_term = after(unit_term, cuts[1])
    grad_gate = unpack_units(unit_term[:, :, :units_here])
    grad_up = unpack_units(unit_term[:, :, units_here:])
    mlp_term = jnp.sum(w_gate.astype(F32) * grad_gate, axis=1)
    mlp_term = mlp_term + jnp.sum(w_up.astype(F32) * grad_up, axis=1)
    grad_mlp_gain = mlp_term / mlp_gain.astype(F32)
    down_sum = down_sum[: w_down.shape[0]].astype(F32)
    sums = sums + sums_one
    sums = sums[:3, :1].reshape(1, 3)
    seq_rms = jnp.sqrt(sums / (seq_length.astype(F32) * model_width))
    total = add_up(blocks)
    weights = jnp.concatenate([w_key, w_value, w_query], axis=1).astype(F32)
    grad_norm_gain = jnp.sum(weights * total[:, : pair_cols + QUERY_WIDTH], axis=1)
    grad_norm_gain = grad_norm_gain / norm_gain.astype(F32)
    return (
        activations,
        input_grad,
        grad_norm_gain,
        total[:, pair_cols : pair_cols + QUERY_WIDTH],
        total[:, :KEY_WIDTH],
        total[:, KEY_WIDTH:pair_cols],
        total[:, pair_cols + QUERY_WIDTH :],
        grad_mlp_gain,
        grad_gate,
        grad_up,
        down_sum,
        seq_rms,
    )


def solution(mesh):
    fine = Mesh(mesh.devices.reshape(SIZES), AXES)
    rows = P(AXES, None)
    flat = P(AXES)
    group = ("x", "zl", "core")
    in_specs = (
        (rows, flat, rows, rows, rows, rows, flat, rows, rows, rows)
        + (P(group, None), P(group), P(group))
        + (rows,)
    )
    out_specs = (rows, rows, flat, rows, rows, rows, rows, flat, rows, rows, rows, P(group, None))
    return jax.shard_map(
        local, mesh=fine, in_specs=in_specs, out_specs=out_specs, check_vma=False
    )
```
